32 devices in a mesh: shard: 4 (over y, x), context: 2 (over core), tensor: 4 (over z).
Axes of the slice: x: 2, y: 2, z: 4, core: 2. Of those that a mesh axis runs over, the one named last changes fastest.
Arguments:
- inputs: bfloat16 [4096, 1024], P(('shard', 'context')), may hold values from -6 to 6
- teacher: bfloat16 [4096, 1024], P(('shard', 'context')), may hold values from -6 to 6
- segment_ids: int32 [4, 1024], P('shard', 'context'), may hold values from 0 to 11, never falling along the last dimension, each value on 1 to 256 neighbouring positions
- valid_mask: int32 [4, 1024], P('shard', 'context'), may hold values from 0 to 1, as said below
- norm_gain: float32 [1024], replicated, may hold values from 0.5 to 1.5
- norm_bias: float32 [1024], replicated, may hold values from -4 to 4
- gate_weight: bfloat16 [1024, 3072], P('shard', 'tensor'), may hold values from -0.1875 to 0.1875
- gate_bias: float32 [3072], P('tensor'), may hold values from -4 to 4
- reduce_weight: bfloat16 [1024, 512], P('shard', 'tensor'), may hold values from -0.1875 to 0.1875
- reduce_bias: float32 [512], P('tensor'), may hold values from -4 to 4
- damping: float32 [512, 512], P('tensor'), may hold values from 0.00024414062 to 0.03
- frequency: float32 [512, 512], P('tensor'), may hold values from 0.05 to 3
- timestep: float32 [512], P('tensor'), may hold values from 0.5 to 2
- mix_real: float32 [512, 512], P('tensor'), may hold values from -0.03125 to 0.03125
- mix_imaginary: float32 [512, 512], P('tensor'), may hold values from -0.03125 to 0.03125
- expand_weight: bfloat16 [512, 3072], P('shard', 'tensor'), may hold values from -0.25 to 0.25
- expand_bias: float32 [3072], P('tensor'), may hold values from -4 to 4
- output_weight: bfloat16 [3072, 1024], P('tensor', 'shard'), may hold values from -0.109375 to 0.109375
- output_bias: float32 [1024], replicated, may hold values from -4 to 4
Outputs:
- output: bfloat16 [4096, 1024], P(('shard', 'context'))
- loss: float32 [], replicated
- inputs_grad: bfloat16 [4096, 1024], P(('shard', 'context'))
- norm_gain_grad: float32 [1024], replicated
- norm_bias_grad: float32 [1024], replicated
- gate_weight_grad: float32 [1024, 3072], P('shard', 'tensor')
- gate_bias_grad: float32 [3072], P('tensor')
- reduce_weight_grad: float32 [1024, 512], P('shard', 'tensor')
- reduce_bias_grad: float32 [512], P('tensor')
- damping_grad: float32 [512, 512], P('tensor')
- frequency_grad: float32 [512, 512], P('tensor')
- timestep_grad: float32 [512], P('tensor')
- mix_real_grad: float32 [512, 512], P('tensor')
- mix_imaginary_grad: float32 [512, 512], P('tensor')
- expand_weight_grad: float32 [512, 3072], P('shard', 'tensor')
- expand_bias_grad: float32 [3072], P('tensor')
- output_weight_grad: float32 [3072, 1024], P('tensor', 'shard')
- output_bias_grad: float32 [1024], replicated
The draws below stay inside these ranges and needn't reach their ends.
Inputs may be any that keep to these rules, and one draw needn't show every extreme that they name: `segment_ids`: ids never fall along a sequence; a document is one run of equal ids. `valid_mask`: the first token of every sequence is valid.
All inputs are finite; a program needn't handle non-finite values.
Results may differ from the reference program's by a relative error of at most 0.015.
Values may be sent and summed in bfloat16 or wider, within the bound.
No kernel may reach another device: no remote copies, remote signals or barrier semaphores. Data moves between devices by JAX's collectives and lax.ppermute only.
A program may use at most 320 MiB of HBM per device.

```python
import math
import jax
import jax.numpy as jnp
import numpy as np
from jax import lax

D = 1024
F = 3072
H = 512
N = 512
BLOCK = 64
SEQ_LEN = 1024
SEQUENCES = 4
TOKENS = 4096
N_TENSOR = 4


def draw_valid_mask(key, part):
    dice_rolls = jax.random.randint(key, (SEQUENCES, SEQ_LEN), 0, 1000)
    places = jnp.arange(SEQUENCES * SEQ_LEN, dtype=jnp.int32).reshape(SEQUENCES, SEQ_LEN)
    limits = 300 + 600 * places // (SEQUENCES * SEQ_LEN)
    chosen = (dice_rolls < limits).astype(jnp.int32)
    return chosen.at[:, 0].set(1)


def levels(key, dims, shards, low, high):
    def one(axis_at, shards_of):
        steps = jax.random.uniform(jax.random.fold_in(jax.random.fold_in(key, 6), axis_at), (shards_of,), jnp.float32, low / len(shards), high / len(shards))
        return jnp.repeat(jnp.exp(steps), dims[axis_at] // shards_of).reshape((-1,) + (1,) * (len(dims) - axis_at - 1))

    factor_of = one(*shards[0])
    for cut in shards[1:]:
        factor_of = factor_of * one(*cut)
    return factor_of


def profile(amount, total, limit, slope):
    loads = [(1 << 20) // math.isqrt(standing ** slope) + 1 for standing in range(2, amount + 1)]
    rest, holding = total - limit - (amount - 1), [1] * (amount - 1)
    while rest > 0:
        free = [i for i in range(amount - 1) if holding[i] < limit]
        mass, remaining = sum([loads[i] for i in free]), rest
        for i in free:
            addition = min(limit - holding[i], max(1, remaining * loads[i] // mass), rest)
            holding[i] = holding[i] + addition
            rest = rest - addition
    return np.array([limit] + holding)


def ragged_sizes(stream_key, number_of, total, most, slope):
    if number_of == 2:
        one = jax.random.randint(stream_key, (), max(1, total - most), min(most, total - 1) + 1)
        return jnp.stack([one, total - one])
    tallies = jnp.asarray(profile(number_of, total, most, slope), jnp.int32)
    twos = (number_of - 1) // 2
    giver, taker = tallies[1:1 + 2 * twos:2], tallies[2:2 + 2 * twos:2]
    margin = jnp.minimum(giver - 1, most - taker)
    passed = jax.random.randint(jax.random.fold_in(stream_key, 1), (twos,), 0, 1 << 20) % (margin + 1)
    tallies = tallies.at[1:1 + 2 * twos:2].set(giver - passed).at[2:2 + 2 * twos:2].set(taker + passed)
    return tallies[jax.random.permutation(jax.random.fold_in(stream_key, 2), number_of)]


def bell_draw(rng, dims, scale, reach, shards=(), kind=jnp.bfloat16):
    level = levels(rng, dims, shards, -0.22, 0.18) if shards else 1.0
    array = jax.random.normal(rng, dims, jnp.float32) * scale * level
    return jnp.minimum(jnp.maximum(array, -reach), reach).astype(kind)


def setup_inputs(seed: int = 0) -> dict:
    splits = jax.random.split(jax.random.key(seed), 20)
    inputs = bell_draw(splits[0], (TOKENS, D), 1.0, 6.0, ((0, 8),))
    teacher = bell_draw(splits[1], (TOKENS, D), 1.0, 6.0, ((0, 8),))
    segment_ids = jax.vmap(lambda own: jnp.searchsorted(jnp.cumsum(ragged_sizes(own, 12, SEQ_LEN, SEQ_LEN // 4, 2)), jnp.arange(SEQ_LEN), side="right"))(jax.random.split(splits[2], SEQUENCES)).reshape((SEQUENCES, SEQ_LEN)).astype(jnp.int32)
    valid_mask = draw_valid_mask(jax.random.fold_in(splits[19], 71), 0)
    norm_gain = jnp.clip(1.0 + 0.1 * jax.random.normal(splits[4], (D,), jnp.float32), 0.5, 1.5)
    norm_bias = bell_draw(splits[5], (D,), 0.3, 4.0, (), jnp.float32)
    gate_weight = bell_draw(splits[6], (D, F), D ** -0.5, 0.1875, ((0, 4), (1, 4)))
    gate_bias = bell_draw(splits[7], (F,), 0.3, 4.0, ((0, 4),), jnp.float32)
    reduce_weight = bell_draw(splits[8], (D, H), D ** -0.5, 0.1875, ((0, 4), (1, 4)))
    reduce_bias = bell_draw(splits[9], (H,), 0.3, 4.0, ((0, 4),), jnp.float32)
    damping = jnp.clip(jnp.exp(math.log(0.03) - 4.8112082 * jax.random.uniform(splits[10], (H, N), jnp.float32) ** levels(splits[10], (H, N), ((0, 4),), -0.2, 0.2)), 0.00024414062, 0.03)
    frequency = jnp.clip(jnp.exp(math.log(3.0) - 4.0943445 * jax.random.uniform(splits[11], (H, N), jnp.float32) ** levels(splits[11], (H, N), ((0, 4),), -0.2, 0.2)), 0.05, 3.0)
    timestep = jnp.clip(jnp.exp(math.log(2.0) - 1.3862944 * jax.random.uniform(splits[12], (H,), jnp.float32) ** levels(splits[12], (H,), ((0, 4),), -0.2, 0.2)), 0.5, 2.0)
    mix_real = bell_draw(splits[13], (H, N), (64 * N) ** -0.5, 0.03125, ((0, 4),), jnp.float32)
    mix_imaginary = bell_draw(splits[14], (H, N), (64 * N) ** -0.5, 0.03125, ((0, 4),), jnp.float32)
    expand_weight = bell_draw(splits[15], (H, F), H ** -0.5, 0.25, ((0, 4), (1, 4)))
    expand_bias = bell_draw(splits[16], (F,), 0.3, 4.0, ((0, 4),), jnp.float32)
    output_weight = bell_draw(splits[17], (F, D), F ** -0.5, 0.109375, ((0, 4), (1, 4)))
    output_bias = bell_draw(splits[18], (D,), 0.3, 4.0, (), jnp.float32)
    return {"inputs": inputs, "teacher": teacher, "segment_ids": segment_ids, "valid_mask": valid_mask, "norm_gain": norm_gain, "norm_bias": norm_bias, "gate_weight": gate_weight, "gate_bias": gate_bias, "reduce_weight": reduce_weight, "reduce_bias": reduce_bias, "damping": damping, "frequency": frequency, "timestep": timestep, "mix_real": mix_real, "mix_imaginary": mix_imaginary, "expand_weight": expand_weight, "expand_bias": expand_bias, "output_weight": output_weight, "output_bias": output_bias}


PRECISE = lax.Precision.HIGHEST
EPSILON = 1e-05

@jax.custom_vjp
def low(v):
    return lax.optimization_barrier(v.astype(jnp.bfloat16)).astype(jnp.float32)

@jax.custom_vjp
def low_back(v):
    return v

def low_keep(v):
    return (low(v), None)

def low_pass(kept, grad):
    return (grad,)

def back_keep(v):
    return (v, None)

def back_low(kept, grad):
    return (low(grad),)
low.defvjp(low_keep, low_pass)
low_back.defvjp(back_keep, back_low)

def coefficients(damping, frequency, timestep, mix_real, mix_imaginary):
    rate_real = -timestep[:, None] * damping
    rate_imaginary = timestep[:, None] * frequency
    magnitude = jnp.exp(rate_real)
    minus_real = magnitude * jnp.cos(rate_imaginary) - 1.0
    minus_imaginary = magnitude * jnp.sin(rate_imaginary)
    divisor = damping * damping + frequency * frequency
    ratio_real = (minus_imaginary * frequency - minus_real * damping) / divisor
    ratio_imaginary = -(minus_real * frequency + minus_imaginary * damping) / divisor
    readout_real = mix_real * ratio_real - mix_imaginary * ratio_imaginary
    readout_imaginary = mix_real * ratio_imaginary + mix_imaginary * ratio_real
    return (rate_real, rate_imaginary, readout_real, readout_imaginary)

def powers(rate_real, rate_imaginary, exponents):
    magnitude = jnp.exp(rate_real[..., None] * exponents)
    angles = rate_imaginary[..., None] * exponents
    return (magnitude * jnp.cos(angles), magnitude * jnp.sin(angles))

def powers_first(rate_real, rate_imaginary, exponents):
    magnitude = jnp.exp(exponents[:, None, None] * rate_real[None])
    angles = exponents[:, None, None] * rate_imaginary[None]
    return (magnitude * jnp.cos(angles), magnitude * jnp.sin(angles))

def intra_part(segments, signal, rate_real, rate_imaginary, readout_real, readout_imaginary):
    length, channels = signal.shape
    blocks = length // BLOCK
    number_type = signal.dtype
    offsets = jnp.arange(BLOCK + 1).astype(number_type)
    power_real, power_imaginary = powers(rate_real, rate_imaginary, offsets)
    kernel = jnp.einsum('hn,hnl->hl', readout_real, power_real[..., :BLOCK], precision=PRECISE) - jnp.einsum('hn,hnl->hl', readout_imaginary, power_imaginary[..., :BLOCK], precision=PRECISE)
    places = jnp.arange(BLOCK)
    lag_matrix = places[:, None] - places[None, :]
    one_hot = (lag_matrix[:, :, None] == places[None, None, :]).astype(number_type)
    toeplitz = jnp.einsum('hl,tsl->hts', kernel, one_hot, precision=PRECISE)
    signal_blocks = signal.reshape(blocks, BLOCK, channels)
    segment_blocks = segments.reshape(blocks, BLOCK)
    same_segment = (segment_blocks[:, :, None] == segment_blocks[:, None, :]).astype(number_type)
    weighted = toeplitz[None] * same_segment[:, None]
    within = jnp.einsum('khts,ksh->kth', weighted, signal_blocks, precision=PRECISE)
    block_last = segment_blocks[:, -1]
    kept_rows = signal_blocks * (segment_blocks == block_last[:, None]).astype(number_type)[:, :, None]
    reverse_real = power_real[..., :BLOCK][..., ::-1]
    reverse_imaginary = power_imaginary[..., :BLOCK][..., ::-1]
    added_real = jnp.einsum('hns,ksh->khn', reverse_real, kept_rows, precision=PRECISE)
    added_imaginary = jnp.einsum('hns,ksh->khn', reverse_imaginary, kept_rows, precision=PRECISE)
    jump_real = power_real[..., BLOCK]
    jump_imaginary = power_imaginary[..., BLOCK]
    block_links = jnp.concatenate([jnp.zeros((1,), number_type), (block_last[1:] == block_last[:-1]).astype(number_type)])

    def advance(carried, pieces):
        state_real, state_imaginary = carried
        linked, add_real, add_imaginary = pieces
        new_real = linked * (jump_real * state_real - jump_imaginary * state_imaginary) + add_real
        new_imaginary = linked * (jump_real * state_imaginary + jump_imaginary * state_real) + add_imaginary
        return ((new_real, new_imaginary), (new_real, new_imaginary))
    zeros_state = jnp.zeros_like(jump_real)
    unused, states = lax.scan(advance, (zeros_state, zeros_state), (block_links, added_real, added_imaginary))
    return (within.reshape(length, channels), states[0], states[1])

def state_part(segments, previous, ends_real, ends_imaginary, incoming_real, incoming_imaginary, rate_real, rate_imaginary, readout_real, readout_imaginary):
    length = segments.shape[0]
    blocks = length // BLOCK
    number_type = ends_real.dtype
    segment_blocks = segments.reshape(blocks, BLOCK)
    block_last = segment_blocks[:, -1]
    ahead_steps = jnp.arange(1, BLOCK + 1).astype(number_type)
    ahead_real, ahead_imaginary = powers(rate_real, rate_imaginary, ahead_steps)
    read_real = readout_real[..., None] * ahead_real - readout_imaginary[..., None] * ahead_imaginary
    read_imaginary = readout_real[..., None] * ahead_imaginary + readout_imaginary[..., None] * ahead_real
    span_steps = BLOCK * jnp.arange(1, blocks + 1).astype(number_type)
    span_real, span_imaginary = powers_first(rate_real, rate_imaginary, span_steps)
    carry_mask = (block_last == previous).astype(number_type)[:, None, None]
    full_real = ends_real + carry_mask * (span_real * incoming_real - span_imaginary * incoming_imaginary)
    full_imaginary = ends_imaginary + carry_mask * (span_real * incoming_imaginary + span_imaginary * incoming_real)
    start_real = jnp.concatenate([incoming_real[None], full_real[:-1]], 0)
    start_imaginary = jnp.concatenate([incoming_imaginary[None], full_imaginary[:-1]], 0)
    start_segment = jnp.concatenate([jnp.reshape(previous, (1,)).astype(number_type), block_last[:-1]])
    alive_mask = (segment_blocks == start_segment[:, None]).astype(number_type)
    reached = jnp.einsum('hnt,khn->kth', read_real, start_real, precision=PRECISE) - jnp.einsum('hnt,khn->kth', read_imaginary, start_imaginary, precision=PRECISE)
    return (reached * alive_mask[:, :, None]).reshape(length, -1)

def state_space(signal, segments, damping, frequency, timestep, mix_real, mix_imaginary):
    length, channels = signal.shape
    group_size = channels // N_TENSOR

    def one_group(pieces):
        part_signal, part_damping, part_frequency, part_timestep, part_real, part_imaginary = pieces
        rate_terms = coefficients(part_damping, part_frequency, part_timestep, part_real, part_imaginary)
        within, ends_real, ends_imaginary = intra_part(segments, part_signal, *rate_terms)
        empty_state = jnp.zeros_like(ends_real[0])
        reached = state_part(segments, jnp.asarray(-1.0, ends_real.dtype), ends_real, ends_imaginary, empty_state, empty_state, *rate_terms)
        return within + reached
    grouped = (signal.reshape(length, N_TENSOR, group_size).transpose(1, 0, 2), damping.reshape(N_TENSOR, group_size, -1), frequency.reshape(N_TENSOR, group_size, -1), timestep.reshape(N_TENSOR, group_size), mix_real.reshape(N_TENSOR, group_size, -1), mix_imaginary.reshape(N_TENSOR, group_size, -1))
    outcome = lax.map(jax.checkpoint(one_group), grouped)
    return outcome.transpose(1, 0, 2).reshape(length, channels)

def normalize(values, norm_gain, norm_bias):
    center = lax.optimization_barrier(jnp.mean(values, axis=-1, keepdims=True))
    shifted = values - center
    spread = lax.optimization_barrier(jnp.mean(shifted * shifted, axis=-1, keepdims=True))
    return shifted * lax.rsqrt(spread + EPSILON) * norm_gain + norm_bias

def layer_forward(tokens_in, segments, norm_gain, norm_bias, gate_weight, gate_bias, reduce_weight, reduce_bias, damping, frequency, timestep, mix_real, mix_imaginary, expand_weight, expand_bias, output_weight, output_bias):
    normed = low(normalize(tokens_in, norm_gain, norm_bias))
    gate_linear = low_back(jnp.dot(normed, gate_weight, precision=PRECISE, preferred_element_type=jnp.float32))
    gate_act = jax.nn.gelu(gate_linear + gate_bias, approximate=True)
    reduce_linear = low_back(jnp.dot(normed, reduce_weight, precision=PRECISE, preferred_element_type=jnp.float32))
    reduced = jax.nn.gelu(reduce_linear + reduce_bias, approximate=True)
    mixed_rows = low(state_space(reduced, segments, damping, frequency, timestep, mix_real, mix_imaginary))
    expand_linear = low_back(jnp.dot(mixed_rows, expand_weight, precision=PRECISE, preferred_element_type=jnp.float32))
    gated_rows = low((expand_linear + expand_bias) * gate_act)
    output_linear = low_back(jnp.dot(gated_rows, output_weight, precision=PRECISE, preferred_element_type=jnp.float32))
    return tokens_in + output_linear + output_bias

def reference(inputs, teacher, segment_ids, valid_mask, norm_gain, norm_bias, gate_weight, gate_bias, reduce_weight, reduce_bias, damping, frequency, timestep, mix_real, mix_imaginary, expand_weight, expand_bias, output_weight, output_bias):
    number_type = jnp.float32
    parameters = (norm_gain, norm_bias, gate_weight.astype(number_type), gate_bias, reduce_weight.astype(number_type), reduce_bias, damping, frequency, timestep, mix_real, mix_imaginary, expand_weight.astype(number_type), expand_bias, output_weight.astype(number_type), output_bias)
    counted = jnp.sum(valid_mask).astype(number_type)
    scaling = TOKENS / counted
    sequences = inputs.astype(number_type).reshape(SEQUENCES, SEQ_LEN, D)
    targets = teacher.astype(number_type).reshape(SEQUENCES, SEQ_LEN, D)
    documents = segment_ids.astype(number_type)
    mask_rows = valid_mask.astype(number_type)

    def one_sequence(carried, pieces):
        grad_total, error_total = carried
        sequence, target, document_ids, mask_row = pieces

        def objective(tokens_in, *weights):
            outcome = layer_forward(tokens_in, document_ids, *weights)
            difference = outcome - target
            errors = lax.optimization_barrier(jnp.sum(difference * difference, axis=-1))
            masked_error = jnp.sum(mask_row * errors)
            return (0.5 * scaling * masked_error, (outcome, masked_error))
        objective_value, pullback, extras = jax.vjp(objective, sequence, *parameters, has_aux=True)
        gradients = pullback(jnp.ones_like(objective_value))
        new_total = jax.tree.map(lambda summed, addend: summed + addend, grad_total, tuple(gradients[1:]))
        return ((new_total, error_total + extras[1]), (extras[0], gradients[0]))
    initial = (jax.tree.map(jnp.zeros_like, parameters), jnp.zeros((), number_type))
    finals, stacked = lax.scan(one_sequence, initial, (sequences, targets, documents, mask_rows))
    grad_total, error_total = finals
    outputs, input_grads = stacked
    loss_value = error_total / (counted * D)
    return (outputs.reshape(TOKENS, D).astype(jnp.bfloat16), loss_value, input_grads.reshape(TOKENS, D).astype(jnp.bfloat16), grad_total[0], grad_total[1], grad_total[2], grad_total[3], grad_total[4], grad_total[5], grad_total[6], grad_total[7], grad_total[8], grad_total[9], grad_total[10], grad_total[11], grad_total[12], grad_total[13], grad_total[14])
```

```python
from functools import partial

import jax
import jax.numpy as jnp
from jax import lax
from jax.experimental import pallas as pl
from jax.experimental.pallas import tpu as pltpu
from jax.sharding import PartitionSpec as P

BLOCK = 64
REACH = 256
EPSILON = 1e-05
F32 = jnp.float32
BF16 = jnp.bfloat16
VMEM_LIMIT = 50 * 1024 * 1024


def xor_pairs(size, mask):
    return [(i, i ^ mask) for i in range(size)]


def shift_pairs(size, step):
    return [(i, (i + step) % size) for i in range(size)]


def swap_context(x):
    return lax.ppermute(x, "context", [(0, 1), (1, 0)])


def sum_over(x, axis):
    size = lax.axis_size(axis)
    if size == 4:
        first = lax.ppermute(x, axis, xor_pairs(4, 1))
        second = lax.ppermute(x, axis, xor_pairs(4, 2))
        third = lax.ppermute(x, axis, xor_pairs(4, 3))
        return (x + first) + (second + third)
    step = 1
    while step < size:
        x = x + lax.ppermute(x, axis, xor_pairs(size, step))
        step *= 2
    return x


def gather_weight(w, axis):
    if lax.axis_size("shard") != 4 or lax.axis_size("context") != 2:
        return lax.all_gather(w, "shard", axis=axis, tiled=True)
    core = lax.axis_index("context")
    me = lax.axis_index("shard")
    rows, cols = w.shape
    half = rows // 2
    mine = lax.dynamic_slice_in_dim(w, core * half, half, 0)
    near = [lax.ppermute(mine, "shard", xor_pairs(4, k)) for k in (1, 2, 3)]
    far = [swap_context(a) for a in near]
    full = jnp.zeros((4, rows, cols), w.dtype)
    full = lax.dynamic_update_slice(full, w[None], (me, 0, 0))
    for k in (1, 2, 3):
        full = lax.dynamic_update_slice(full, near[k - 1][None], (me ^ k, core * half, 0))
        full = lax.dynamic_update_slice(full, far[k - 1][None], (me ^ k, (1 - core) * half, 0))
    if axis == 0:
        return full.reshape(4 * rows, cols)
    return full.transpose(1, 0, 2).reshape(rows, 4 * cols)


def scatter_grad(grad, axis):
    if lax.axis_size("shard") != 4 or lax.axis_size("context") != 2:
        paired = lax.psum(grad.astype(BF16), "context").astype(F32)
        return lax.psum_scatter(paired, "shard", scatter_dimension=axis, tiled=True)
    core = lax.axis_index("context")
    me = lax.axis_index("shard")
    if axis == 0:
        pieces = grad.reshape(4, 2, grad.shape[0] // 8, grad.shape[1])
    else:
        pieces = grad.reshape(2, grad.shape[0] // 2, 4, grad.shape[1] // 4).transpose(2, 0, 1, 3)
    keep = lax.dynamic_index_in_dim(pieces, core, 1, False)
    give = lax.dynamic_index_in_dim(pieces, 1 - core, 1, False).astype(BF16)
    paired = keep + swap_context(give).astype(F32)
    total = lax.dynamic_index_in_dim(paired, me, 0, False)
    sent = paired.astype(BF16)
    for k in (1, 2, 3):
        piece = lax.dynamic_index_in_dim(sent, me ^ k, 0, False)
        total = total + lax.ppermute(piece, "shard", xor_pairs(4, k)).astype(F32)
    other = swap_context(total)
    both = jnp.where(core == 0, jnp.stack([total, other]), jnp.stack([other, total]))
    return both.reshape(2 * total.shape[0], total.shape[1])


def scatter_rows(x):
    size = lax.axis_size("tensor")
    me = lax.axis_index("tensor")
    pieces = x.reshape(size, x.shape[0] // size, x.shape[1])
    total = lax.dynamic_index_in_dim(pieces, me, 0, False).astype(F32)
    for k in range(1, size):
        piece = lax.dynamic_index_in_dim(pieces, (me + k) % size, 0, False)
        total = total + lax.ppermute(piece, "tensor", shift_pairs(size, k)).astype(F32)
    return total


def gather_rows(x):
    size = lax.axis_size("tensor")
    me = lax.axis_index("tensor")
    full = jnp.zeros((size,) + x.shape, x.dtype)
    full = lax.dynamic_update_slice(full, x[None], (me, 0, 0))
    for k in range(1, size):
        part = lax.ppermute(x, "tensor", shift_pairs(size, k))
        full = lax.dynamic_update_slice(full, part[None], ((me - k) % size, 0, 0))
    return full


def cmul(ar, ai, br, bi):
    return ar * br - ai * bi, ar * bi + ai * br


def modes(damping, frequency, timestep):
    magnitude = jnp.exp(-timestep * damping)
    angle = timestep * frequency
    return magnitude * jnp.cos(angle), magnitude * jnp.sin(angle)


def ratios(damping, frequency, ar, ai):
    minus = ar - 1.0
    inverse = 1.0 / (damping * damping + frequency * frequency)
    return (ai * frequency - minus * damping) * inverse, -(
        minus * frequency + ai * damping
    ) * inverse


def low_powers(ar, ai, count):
    found = [None, (ar, ai)]
    for j in range(2, count):
        found.append(cmul(*found[j // 2], *found[j - j // 2]))
    return found


def taps_kernel(d_ref, f_ref, t_ref, mr_ref, mi_ref, k_ref, rev_ref, ar_s, ai_s, wr_s, wi_s, acc):
    damping, frequency, timestep = d_ref[...], f_ref[...], t_ref[...]
    ar, ai = modes(damping, frequency, timestep)
    qr, qi = ratios(damping, frequency, ar, ai)
    mr, mi = mr_ref[...], mi_ref[...]
    ar_s[...] = ar
    ai_s[...] = ai
    wr_s[...] = mr * qr - mi * qi
    wi_s[...] = mr * qi + mi * qr
    acc[...] = jnp.zeros_like(acc)

    def pair(p, carry):
        rows = pl.ds(pl.multiple_of(16 * p, 16), 16)
        a = (ar_s[rows, :], ai_s[rows, :])
        base = low_powers(*a, 8)
        eight = cmul(*base[4], *base[4])

        def outer(o, w):
            wr, wi = w
            at = pl.multiple_of(64 * o, 64)
            for j in range(8):
                term = wr if j == 0 else wr * base[j][0] - wi * base[j][1]
                acc[pl.ds(at + 8 * j, 8), :] += term[:8] + term[8:]
            return cmul(wr, wi, *eight)

        lax.fori_loop(0, REACH // 8, outer, (wr_s[rows, :], wi_s[rows, :]))
        return carry

    lax.fori_loop(0, ar_s.shape[0] // 16, pair, 0)
    k_ref[...] = jnp.sum(acc[...].reshape(REACH, 8, acc.shape[1]), axis=1)
    for l in range(REACH):
        rev_ref[REACH - 1 - l : REACH - l, :] = k_ref[l : l + 1, :]


def make_taps(damping, frequency, timestep, mix_real, mix_imaginary):
    count, channels = damping.shape
    return pl.pallas_call(
        taps_kernel,
        out_shape=[jax.ShapeDtypeStruct((REACH, channels), F32)] * 2,
        scratch_shapes=[pltpu.VMEM((count, channels), F32)] * 4
        + [pltpu.VMEM((REACH * 8, channels), F32)],
        compiler_params=pltpu.CompilerParams(vmem_limit_bytes=VMEM_LIMIT),
        cost_estimate=pl.CostEstimate(flops=80_000_000, bytes_accessed=2_000_000, transcendentals=200_000),
        name="taps",
    )(damping, frequency, timestep, mix_real, mix_imaginary)


def shifted_copies(source_ref, pad, copies, lead):
    length = copies.shape[1]
    pad[...] = jnp.zeros_like(pad)
    pad[64 : 64 + REACH, :] = source_ref[...]
    for r in range(8):
        start = 64 + lead - r
        copies[r, :, :] = pad[start : start + length, :]


def linked_blocks(seg, first, last, step, bound):
    def more(count):
        at = last + step * count
        edge = 64 * at + (63 if step < 0 else 0)
        mine = 64 * first + (0 if step < 0 else 63)
        return jnp.logical_and(count < bound, seg[jnp.clip(edge, 0, seg.shape[0] - 1)] == seg[mine])

    return lax.while_loop(more, lambda c: c + 1, 0)


def tile(at):
    return pl.ds(pl.multiple_of(8 * at, 8), 8)


def forward_kernel(seg, k_ref, u_ref, s_ref, y_ref, pad, copies, kept):
    channels = u_ref.shape[1]
    blocks = u_ref.shape[0] // 64
    ahead = REACH // 64
    shifted_copies(k_ref, pad, copies, 0)
    for b in range(blocks):
        rows = slice(64 * b, 64 * b + 64)
        kept[rows, :] = jnp.where(s_ref[rows, :] == seg[64 * b + 63], u_ref[rows, :], 0.0)

    def block(i, carry):
        mine = i + ahead
        zero = jnp.zeros((8, channels), F32)
        reach = linked_blocks(seg, mine, mine - 1, -1, ahead)

        def far(d, sums):
            sums = list(sums)
            at = pl.multiple_of(64 * (mine - 1 - d), 64)
            for r in range(8):
                taps = [copies[r, tile(8 * (d + 1) + m), :] for m in range(-7, 8)]
                for q in range(8):
                    u = kept[pl.ds(at + 8 * q + r, 1), :]
                    for t in range(8):
                        sums[t] += taps[t - q + 7] * u
            return tuple(sums)

        sums = lax.fori_loop(0, reach, far, (zero,) * 8)
        base = pl.multiple_of(64 * mine, 64)
        ids = [s_ref[pl.ds(base + 8 * t, 8), :] for t in range(8)]
        sums = [jnp.where(ids[t] == seg[64 * mine], sums[t], 0.0) for t in range(8)]
        for r in range(8):
            taps = [copies[r, 8 * m : 8 * m + 8, :] for m in range(8)]
            for q in range(8):
                u = u_ref[pl.ds(base + 8 * q + r, 1), :]
                own = s_ref[pl.ds(base + 8 * q + r, 1), :]
                for t in range(q, 8):
                    sums[t] += jnp.where(ids[t] == own, taps[t - q], 0.0) * u
        for t in range(0, 8, 2):
            both = jnp.concatenate([sums[t], sums[t + 1]], 0)
            y_ref[pl.ds(pl.multiple_of(64 * i + 8 * t, 16), 16), :] = both.astype(y_ref.dtype)
        return carry

    lax.fori_loop(0, blocks - ahead, block, 0)


SMEM_SPEC = pl.BlockSpec(memory_space=pltpu.SMEM)
VMEM_SPEC = pl.BlockSpec(memory_space=pltpu.VMEM)


def forward_mix(seg, taps, u, ids):
    channels = u.shape[1]
    return pl.pallas_call(
        forward_kernel,
        out_shape=jax.ShapeDtypeStruct((u.shape[0] - REACH, channels), BF16),
        in_specs=[SMEM_SPEC] + [VMEM_SPEC] * 3,
        scratch_shapes=[
            pltpu.VMEM((64 + REACH + 128, channels), F32),
            pltpu.VMEM((8, 64 + REACH, channels), F32),
            pltpu.VMEM(u.shape, F32),
        ],
        compiler_params=pltpu.CompilerParams(vmem_limit_bytes=VMEM_LIMIT),
        cost_estimate=pl.CostEstimate(flops=20_000_000, bytes_accessed=1_000_000, transcendentals=0),
        name="forward_mix",
    )(seg, taps, u, ids)


def backward_kernel(seg, rev_ref, g_ref, s_ref, slope_ref, low_ref, sum_ref, pad, copies, alive):
    channels = g_ref.shape[1]
    blocks = g_ref.shape[0] // 64
    ahead = REACH // 64
    shifted_copies(rev_ref, pad, copies, -57)
    for b in range(blocks):
        rows = slice(64 * b, 64 * b + 64)
        alive[rows, :] = jnp.where(s_ref[rows, :] == seg[64 * b], g_ref[rows, :], 0.0)

    def block(j, total):
        zero = jnp.zeros((8, channels), F32)
        reach = linked_blocks(seg, j, j + 1, 1, ahead)

        def far(d, sums):
            sums = list(sums)
            at = pl.multiple_of(64 * (j + 1 + d), 64)
            for r in range(8):
                taps = [copies[r, tile(39 - (8 * (d + 1) + m)), :] for m in range(-7, 8)]
                for q in range(8):
                    g = alive[pl.ds(at + 8 * q + r, 1), :]
                    for t in range(8):
                        sums[t] += taps[q - t + 7] * g
            return tuple(sums)

        sums = lax.fori_loop(0, reach, far, (zero,) * 8)
        base = pl.multiple_of(64 * j, 64)
        ids = [s_ref[pl.ds(base + 8 * t, 8), :] for t in range(8)]
        last = seg[64 * j + 63]
        sums = [jnp.where(ids[t] == last, sums[t], 0.0) for t in range(8)]
        for r in range(8):
            taps = [copies[r, 8 * (39 - m) : 8 * (39 - m) + 8, :] for m in range(8)]
            for q in range(8):
                g = g_ref[pl.ds(base + 8 * q + r, 1), :]
                own = s_ref[pl.ds(base + 8 * q + r, 1), :]
                for t in range(q + 1):
                    sums[t] += jnp.where(ids[t] == own, taps[q - t], 0.0) * g
        for t in range(0, 8, 2):
            rows = pl.ds(pl.multiple_of(64 * j + 8 * t, 16), 16)
            both = jnp.concatenate([sums[t], sums[t + 1]], 0) * slope_ref[rows, :]
            low_ref[rows, :] = both.astype(low_ref.dtype)
            total = total + both
        return total

    total = lax.fori_loop(0, blocks - ahead, block, jnp.zeros((16, channels), F32))
    sum_ref[...] = jnp.sum(total, axis=0, keepdims=True)


def backward_mix(seg, reversed_taps, g, ids, slope):
    channels = g.shape[1]
    return pl.pallas_call(
        backward_kernel,
        out_shape=[
            jax.ShapeDtypeStruct(slope.shape, BF16),
            jax.ShapeDtypeStruct((1, channels), F32),
        ],
        in_specs=[SMEM_SPEC] + [VMEM_SPEC] * 4,
        scratch_shapes=[
            pltpu.VMEM((64 + REACH + 128, channels), F32),
            pltpu.VMEM((8, 64 + REACH, channels), F32),
            pltpu.VMEM(g.shape, F32),
        ],
        compiler_params=pltpu.CompilerParams(vmem_limit_bytes=VMEM_LIMIT),
        cost_estimate=pl.CostEstimate(flops=20_000_000, bytes_accessed=1_000_000, transcendentals=0),
        name="backward_mix",
    )(seg, reversed_taps, g, ids, slope)


def taps_back_kernel(seg, u_ref, s_ref, g_ref, out_ref, kept, sums, pad):
    channels = u_ref.shape[1]
    blocks = u_ref.shape[0] // 64
    ahead = REACH // 64
    sums[...] = jnp.zeros_like(sums)
    for b in range(blocks):
        rows = slice(64 * b, 64 * b + 64)
        kept[rows, :] = jnp.where(s_ref[rows, :] == seg[64 * b + 63], u_ref[rows, :], 0.0)

    def block(i, carry):
        mine = i + ahead
        reach = linked_blocks(seg, mine, mine - 1, -1, ahead)
        base = pl.multiple_of(64 * mine, 64)
        back = pl.multiple_of(64 * i, 64)
        ids = [s_ref[pl.ds(base + 8 * t, 8), :] for t in range(8)]
        whole = [g_ref[pl.ds(back + 8 * t, 8), :] for t in range(8)]
        alive = [jnp.where(ids[t] == seg[64 * mine], whole[t], 0.0) for t in range(8)]

        def far(d, carried):
            at = pl.multiple_of(64 * (mine - 1 - d), 64)
            for r in range(8):
                found = [None] * 15
                for q in range(8):
                    u = kept[pl.ds(at + 8 * q + r, 1), :]
                    for t in range(8):
                        term = carried[t] * u
                        m = t - q + 7
                        found[m] = term if found[m] is None else found[m] + term
                for m in range(-7, 8):
                    sums[r, tile(8 * (d + 1) + m), :] += found[m + 7]
            return carried

        lax.fori_loop(0, reach, far, tuple(alive))
        for r in range(8):
            found = [None] * 8
            for q in range(8):
                u = u_ref[pl.ds(base + 8 * q + r, 1), :]
                own = s_ref[pl.ds(base + 8 * q + r, 1), :]
                for t in range(q, 8):
                    term = jnp.where(ids[t] == own, whole[t], 0.0) * u
                    m = t - q
                    found[m] = term if found[m] is None else found[m] + term
            for m in range(8):
                sums[r, 8 * m : 8 * m + 8, :] += found[m]
        return carry

    lax.fori_loop(0, blocks - ahead, block, 0)
    total = sums[0, 0:REACH, :]
    for r in range(1, 8):
        total = total + sums[r, r : r + REACH, :]
    out_ref[...] = total


def taps_back(seg, u, ids, g):
    channels = u.shape[1]
    return pl.pallas_call(
        taps_back_kernel,
        out_shape=jax.ShapeDtypeStruct((REACH, channels), F32),
        in_specs=[SMEM_SPEC] + [VMEM_SPEC] * 3,
        scratch_shapes=[
            pltpu.VMEM(u.shape, F32),
            pltpu.VMEM((8, 64 + REACH, channels), F32),
            pltpu.VMEM((8, channels), F32),
        ],
        compiler_params=pltpu.CompilerParams(vmem_limit_bytes=VMEM_LIMIT),
        cost_estimate=pl.CostEstimate(flops=20_000_000, bytes_accessed=1_000_000, transcendentals=0),
        name="taps_back",
    )(seg, u, ids, g)


def modes_back_kernel(
    c_ref, d_ref, f_ref, t_ref, mr_ref, mi_ref, dd_ref, df_ref, dt_ref, dmr_ref, dmi_ref,
    ar_s, ai_s, gr_s, gi_s, hr_s, hi_s, wide, wide_l,
):
    channels = c_ref.shape[1]
    damping, frequency, timestep = d_ref[...], f_ref[...], t_ref[...]
    ar, ai = modes(damping, frequency, timestep)
    ar_s[...] = ar
    ai_s[...] = ai
    for l in range(REACH):
        row = jnp.broadcast_to(c_ref[l : l + 1, :], (8, channels))
        wide[8 * l : 8 * l + 8, :] = row
        wide_l[8 * l : 8 * l + 8, :] = row * float(l)

    def one(p, carry):
        rows = pl.ds(pl.multiple_of(8 * p, 8), 8)
        a = (ar_s[rows, :], ai_s[rows, :])
        base = low_powers(*a, 16)
        jump = cmul(*base[8], *base[8])
        zero = jnp.zeros((8, channels), F32)

        def outer(o, state):
            pr, pi, gr, gi, hr, hi = state
            at = pl.multiple_of(128 * o, 128)
            sr = wide[pl.ds(at, 8), :]
            tr = wide_l[pl.ds(at, 8), :]
            si = zero
            ti = zero
            for j in range(1, 16):
                c = wide[pl.ds(at + 8 * j, 8), :]
                e = wide_l[pl.ds(at + 8 * j, 8), :]
                br, bi = base[j]
                sr += c * br
                si += c * bi
                tr += e * br
                ti += e * bi
            gr += pr * sr - pi * si
            gi += pr * si + pi * sr
            hr += pr * tr - pi * ti
            hi += pr * ti + pi * tr
            pr, pi = cmul(pr, pi, *jump)
            return pr, pi, gr, gi, hr, hi

        one_ = jnp.ones((8, channels), F32)
        _, _, gr, gi, hr, hi = lax.fori_loop(
            0, REACH // 16, outer, (one_, zero, zero, zero, zero, zero)
        )
        gr_s[rows, :] = gr
        gi_s[rows, :] = gi
        hr_s[rows, :] = hr
        hi_s[rows, :] = hi
        return carry

    lax.fori_loop(0, ar_s.shape[0] // 8, one, 0)
    gr, gi, hr, hi = gr_s[...], gi_s[...], hr_s[...], hi_s[...]
    mr, mi = mr_ref[...], mi_ref[...]
    qr, qi = ratios(damping, frequency, ar, ai)
    wr, wi = cmul(mr, mi, qr, qi)
    mixr, mixi = cmul(qr, qi, gr, gi)
    dmr_ref[...] = mixr
    dmi_ref[...] = -mixi
    inverse = 1.0 / (damping * damping + frequency * frequency)
    nr, ni = -damping * inverse, -frequency * inverse
    vr, vi = cmul(*cmul(mr, mi, gr, gi), nr, ni)
    xr, xi = cmul(vr, vi, ar, ai)
    zr, zi = cmul(wr, wi, hr, hi)
    xr, xi = xr + zr, xi + zi
    yr, yi = cmul(vr, vi, qr, qi)
    dd_ref[...] = yr - timestep * xr
    df_ref[...] = yi - timestep * xi
    dt_ref[...] = jnp.sum(-damping * xr - frequency * xi, axis=0, keepdims=True)


def modes_back(c, damping, frequency, timestep, mix_real, mix_imaginary):
    count, channels = damping.shape
    whole = jax.ShapeDtypeStruct((count, channels), F32)
    return pl.pallas_call(
        modes_back_kernel,
        out_shape=[whole, whole, jax.ShapeDtypeStruct((1, channels), F32), whole, whole],
        scratch_shapes=[pltpu.VMEM((count, channels), F32)] * 6
        + [pltpu.VMEM((REACH * 8, channels), F32)] * 2,
        compiler_params=pltpu.CompilerParams(vmem_limit_bytes=VMEM_LIMIT),
        cost_estimate=pl.CostEstimate(flops=160_000_000, bytes_accessed=2_000_000, transcendentals=200_000),
        name="modes_back",
    )(c, damping, frequency, timestep, mix_real, mix_imaginary)


GELU_SCALE = 0.7978845608028654


def gelu_pair(a):
    square = a * a
    bent = jnp.tanh(GELU_SCALE * (a + 0.044715 * (a * square)))
    half = 0.5 * (1.0 + bent)
    slope = half + 0.5 * a * (1.0 - bent * bent) * (GELU_SCALE + 3 * 0.044715 * GELU_SCALE * square)
    return a * half, slope


def dot(a, b):
    return jnp.dot(a, b, preferred_element_type=F32)


def dot_t(a, b):
    return lax.dot_general(a, b, (((1,), (1,)), ((), ())), preferred_element_type=F32)


def t_dot(a, b):
    return lax.dot_general(a, b, (((0,), (0,)), ((), ())), preferred_element_type=F32)


def per_device(
    inputs,
    teacher,
    segment_ids,
    valid_mask,
    norm_gain,
    norm_bias,
    gate_weight,
    gate_bias,
    reduce_weight,
    reduce_bias,
    damping,
    frequency,
    timestep,
    mix_real,
    mix_imaginary,
    expand_weight,
    expand_bias,
    output_weight,
    output_bias,
):
    tokens, width = inputs.shape
    channels = reduce_bias.shape[0]
    tensor_size = lax.axis_size("tensor")
    tensor_at = lax.axis_index("tensor")
    contexts = lax.axis_size("context")
    context_at = lax.axis_index("context")

    mask_row = valid_mask[0].astype(F32)
    counted = jnp.sum(mask_row)
    counted = jnp.broadcast_to(counted, (1, 128))
    counted = sum_over(sum_over(counted, "context"), "shard")[0, 0]

    reduce_full = gather_weight(reduce_weight, 0)
    gate_full = gather_weight(gate_weight, 0)
    expand_full = gather_weight(expand_weight, 0)
    output_full = gather_weight(output_weight, 1)

    rows_in = inputs.astype(F32)
    center = jnp.mean(rows_in, axis=-1, keepdims=True)
    shifted = rows_in - center
    spread = jnp.mean(shifted * shifted, axis=-1, keepdims=True)
    inverse = lax.rsqrt(spread + EPSILON)
    unit = shifted * inverse
    normed = (unit * norm_gain + norm_bias).astype(BF16)

    mode_args = (damping.T, frequency.T, timestep[None, :], mix_real.T, mix_imaginary.T)
    taps, reversed_taps = make_taps(*mode_args)

    segments = segment_ids[0]
    before = [(i, i + 1) for i in range(contexts - 1)]
    after = [(i + 1, i) for i in range(contexts - 1)]
    seg_before = jnp.where(
        context_at > 0, lax.ppermute(segments[tokens - REACH :], "context", before), -1
    )
    seg_after = jnp.where(
        context_at < contexts - 1, lax.ppermute(segments[:REACH], "context", after), -1
    )
    seg_early = jnp.concatenate([seg_before, segments])
    seg_late = jnp.concatenate([segments, seg_after])
    ids_early = jnp.broadcast_to(seg_early[:, None], (tokens + REACH, channels))
    ids_late = jnp.broadcast_to(seg_late[:, None], (tokens + REACH, channels))

    reduced, reduce_slope = gelu_pair(dot(normed, reduce_full) + reduce_bias)
    halo = lax.ppermute(reduced[tokens - REACH :], "context", before)
    u = jnp.concatenate([halo, reduced], 0)
    mixed_rows = forward_mix(seg_early, taps, u, ids_early)

    gate_act, gate_slope = gelu_pair(dot(normed, gate_full) + gate_bias)
    mixed_parts = gather_rows(mixed_rows)
    mixed_full = mixed_parts.transpose(1, 0, 2).reshape(tokens, tensor_size * channels)
    expanded = dot(mixed_full, expand_full) + expand_bias
    gated_rows = (expanded * gate_act).astype(BF16)
    branch_own = scatter_rows(dot(gated_rows, output_full).astype(BF16)).astype(BF16)
    branch = gather_rows(branch_own).reshape(tokens, width).astype(F32)

    result = rows_in + branch + output_bias
    difference = result - teacher.astype(F32)
    errors = jnp.sum(mask_row * jnp.sum(difference * difference, axis=-1))
    tokens_all = tokens * lax.axis_size("shard") * contexts
    result_back = (tokens_all / counted) * mask_row[:, None] * difference
    branch_back = result_back.astype(BF16)
    gated_back = dot_t(branch_back, output_full)
    expanded_back = gated_back * gate_act
    activation_back = gated_back * expanded
    expand_low = expanded_back.astype(BF16)
    mixed_back_part = dot_t(expand_low, expand_full).astype(BF16)
    mixed_back = scatter_rows(
        mixed_back_part.reshape(tokens, tensor_size, channels)
        .transpose(1, 0, 2)
        .reshape(tensor_size * tokens, channels)
    )
    gate_pre_back = gate_slope * activation_back
    gate_low = gate_pre_back.astype(BF16)

    halo_back = lax.ppermute(mixed_back[:REACH], "context", after)
    g_late = jnp.concatenate([mixed_back, halo_back], 0)
    reduce_low, reduce_bias_part = backward_mix(
        seg_late, reversed_taps, g_late, ids_late, reduce_slope
    )
    normed_part = dot_t(gate_low, gate_full) + dot_t(reduce_low, reduce_full)
    normed_own = scatter_rows(normed_part.astype(BF16))

    taps_grad = taps_back(seg_early, u, ids_early, mixed_back)
    taps_grad = sum_over(sum_over(taps_grad, "context"), "shard")
    mode_grads = modes_back(taps_grad, *mode_args)

    own_rows = tokens // tensor_size

    def mine(x):
        return lax.dynamic_slice_in_dim(x, tensor_at * own_rows, own_rows, 0)

    scaled = normed_own * norm_gain
    unit_own = mine(unit)
    rows_back = mine(inverse) * (
        scaled
        - jnp.mean(scaled, axis=-1, keepdims=True)
        - unit_own * jnp.mean(scaled * unit_own, axis=-1, keepdims=True)
    )
    inputs_grad_own = (mine(result_back) + rows_back).astype(BF16)
    inputs_grad = gather_rows(inputs_grad_own).reshape(tokens, width)

    gain_grad = jnp.sum(normed_own * unit_own, axis=0)
    bias_grad = jnp.sum(normed_own, axis=0)
    norm_pack = jnp.concatenate([gain_grad, bias_grad]).reshape(-1, 128)
    norm_pack = sum_over(sum_over(sum_over(norm_pack, "context"), "shard"), "tensor").reshape(-1)

    sizes = (gate_bias.shape[0], expand_bias.shape[0], width, channels, 128)
    pack = jnp.concatenate(
        [
            jnp.sum(gate_pre_back, axis=0),
            jnp.sum(expanded_back, axis=0),
            jnp.sum(result_back, axis=0),
            reduce_bias_part[0],
            jnp.broadcast_to(errors, (128,)),
        ]
    )
    pack = sum_over(sum_over(pack[None, :], "context"), "shard")[0]
    offsets = [sum(sizes[:k]) for k in range(6)]
    gate_bias_grad, expand_bias_grad, output_bias_grad, reduce_bias_grad, error_total = (
        pack[offsets[k] : offsets[k + 1]] for k in range(5)
    )
    loss_value = error_total[0] / (counted * width)

    output_grad = scatter_grad(t_dot(gated_rows, branch_back), 1)
    expand_grad = scatter_grad(t_dot(mixed_full, expand_low), 0)
    gate_grad = scatter_grad(t_dot(normed, gate_low), 0)
    reduce_grad = scatter_grad(t_dot(normed, reduce_low), 0)

    return (
        result.astype(BF16),
        loss_value,
        inputs_grad,
        norm_pack[:width],
        norm_pack[width:],
        gate_grad,
        gate_bias_grad,
        reduce_grad,
        reduce_bias_grad,
        mode_grads[0].T,
        mode_grads[1].T,
        mode_grads[2][0],
        mode_grads[3].T,
        mode_grads[4].T,
        expand_grad,
        expand_bias_grad,
        output_grad,
        output_bias_grad,
    )


def solution(mesh):
    tokens = P(("shard", "context"), None)
    ids = P("shard", "context")
    split = P("shard", "tensor")
    rows = P("tensor", None)
    units = P("tensor")
    return jax.shard_map(
        per_device,
        mesh=mesh,
        in_specs=(
            tokens, tokens, ids, ids, P(), P(), split, units, split, units,
            rows, rows, units, rows, rows, split, units, P("tensor", "shard"), P(),
        ),
        out_specs=(
            tokens, P(), tokens, P(), P(), split, units, split, units,
            rows, rows, units, rows, rows, split, units, P("tensor", "shard"), P(),
        ),
        check_vma=False,
    )
```

```python
import math
from functools import partial

import jax
import jax.numpy as jnp
from jax import lax
from jax.experimental import pallas as pl
from jax.experimental.pallas import tpu as pltpu
from jax.sharding import PartitionSpec as P

REACH = 256
EPSILON = 1e-05
EARLY, PAIR, LATE, TAPS_BACK, MODES_BACK, TAPS = 0.2,0.2,1,6,13,9
GELU_SCALE = 0.7978845608028654
F32 = jnp.float32
BF16 = jnp.bfloat16
SMEM_SPEC = pl.BlockSpec(memory_space=pltpu.SMEM)
VMEM_SPEC = pl.BlockSpec(memory_space=pltpu.VMEM)


def call(body, name, outs, args, scalars=1, scratch=(), micros=2, ties=()):
    held = [(a.shape, a.dtype) for a in args[scalars:]] + list(outs)
    held += [entry for entry in scratch if isinstance(entry, tuple)]
    room = 0
    for shape, kind in held:
        shape = (8,) * (2 - len(shape)) + tuple(shape)
        room += math.prod(shape[:-2] + (max(shape[-2], 8), max(shape[-1], 128))) * jnp.dtype(kind).itemsize
    count = len(args)

    def kernel(*refs):
        body(*refs[:count], *refs[count + len(ties) :])

    return pl.pallas_call(
        kernel,
        out_shape=[jax.ShapeDtypeStruct(shape, kind) for shape, kind in outs],
        in_specs=[SMEM_SPEC] * scalars
        + [VMEM_SPEC] * (len(args) - scalars)
        + [pl.BlockSpec(memory_space=pl.ANY)] * len(ties),
        out_specs=[VMEM_SPEC] * len(outs),
        scratch_shapes=[
            pltpu.VMEM(*entry) if isinstance(entry, tuple) else entry for entry in scratch
        ],
        compiler_params=pltpu.CompilerParams(vmem_limit_bytes=room + room // 16 + (3 << 20)),
        cost_estimate=pl.CostEstimate(
            flops=int(micros * 0.3e9), bytes_accessed=int(micros * 1e5), transcendentals=0
        ),
        name=name,
    )(*args, *ties)


def dot(a, b):
    return jnp.dot(a, b, preferred_element_type=F32)


def dot_t(a, b):
    return lax.dot_general(a, b, (((1,), (1,)), ((), ())), preferred_element_type=F32)


def t_dot(a, b):
    return lax.dot_general(a, b, (((0,), (0,)), ((), ())), preferred_element_type=F32)


def at(start, size, unit=None):
    return pl.ds(pl.multiple_of(start, unit or size), size)


def gelu_pair(a):
    square = a * a
    bent = jnp.tanh(GELU_SCALE * (a + 0.044715 * (a * square)))
    half = 0.5 * (1.0 + bent)
    slope = half + 0.5 * a * (1.0 - bent * bent) * (GELU_SCALE + 3 * 0.044715 * GELU_SCALE * square)
    return a * half, slope


def xor_pairs(size, mask):
    return [(i, i ^ mask) for i in range(size)]


def shift_pairs(size, step):
    return [(i, (i + step) % size) for i in range(size)]


def swap_context(x):
    return lax.ppermute(x, "context", [(0, 1), (1, 0)])


def sum_over(x, axis):
    size = lax.axis_size(axis)
    if size == 4:
        first = lax.ppermute(x, axis, xor_pairs(4, 1))
        second = lax.ppermute(x, axis, xor_pairs(4, 2))
        third = lax.ppermute(x, axis, xor_pairs(4, 3))
        return (x + first) + (second + third)
    step = 1
    while step < size:
        x = x + lax.ppermute(x, axis, xor_pairs(size, step))
        step *= 2
    return x


def copy_kernel(x_ref, out_ref):
    out_ref[...] = x_ref[...]


def add_kernel(x_ref, y_ref, out_ref):
    out_ref[...] = (x_ref[...].astype(F32) + y_ref[...].astype(F32)).astype(out_ref.dtype)


def toward(place, k, size):
    return place[2] ^ k if size == 4 else lax.rem(place[2] + k, size)


def origin(place, k, size):
    return place[2] ^ k if size == 4 else lax.rem(place[2] + size - k, size)


def spread_tensor(x):
    size = lax.axis_size("tensor")
    if size == 4:
        near = lax.ppermute(x, "tensor", xor_pairs(4, 1))
        far = lax.ppermute(x, "tensor", xor_pairs(4, 2))
        (again,) = call(copy_kernel, "again", [(x.shape, x.dtype)], (far,), scalars=0, micros=0.5, ties=(near,))
        return [near, far, lax.ppermute(again, "tensor", xor_pairs(4, 1))]
    return [lax.ppermute(x, "tensor", shift_pairs(size, k)) for k in range(1, size)]


def deliver_tensor(pieces):
    size = lax.axis_size("tensor")
    if size == 4:
        passed = lax.ppermute(pieces[2], "tensor", xor_pairs(4, 1))
        near = lax.ppermute(pieces[0], "tensor", xor_pairs(4, 1))
        (joined,) = call(
            add_kernel, "joined", [(passed.shape, BF16)], (pieces[1], passed), scalars=0, micros=0.5, ties=(near,)
        )
        return [near, lax.ppermute(joined, "tensor", xor_pairs(4, 2))]
    return [lax.ppermute(x, "tensor", shift_pairs(size, k + 1)) for k, x in enumerate(pieces)]


def cmul(ar, ai, br, bi):
    return ar * br - ai * bi, ar * bi + ai * br


def modes(damping, frequency, timestep):
    magnitude = jnp.exp(-timestep * damping)
    angle = timestep * frequency
    return magnitude * jnp.cos(angle), magnitude * jnp.sin(angle)


def ratios(damping, frequency, ar, ai):
    minus = ar - 1.0
    inverse = 1.0 / (damping * damping + frequency * frequency)
    return (ai * frequency - minus * damping) * inverse, -(
        minus * frequency + ai * damping
    ) * inverse


def low_powers(ar, ai, count):
    found = [None, (ar, ai)]
    for j in range(2, count):
        found.append(cmul(*found[j // 2], *found[j - j // 2]))
    return found


def taps_kernel(place, d_ref, f_ref, t_ref, mr_ref, mi_ref, k_ref, ar_s, ai_s, wr_s, wi_s, acc, lags):
    damping, frequency, timestep = d_ref[...].T, f_ref[...].T, t_ref[...][None, :]
    ar, ai = modes(damping, frequency, timestep)
    qr, qi = ratios(damping, frequency, ar, ai)
    mr, mi = mr_ref[...].T, mi_ref[...].T
    wr, wi = mr * qr - mi * qi, mr * qi + mi * qr
    ar_s[...] = ar
    ai_s[...] = ai
    if lags < REACH:
        power = (ar, ai)
        for _ in range(lags.bit_length() - 1):
            power = cmul(*power, *power)
        later = place[1] > 0
        vr, vi = cmul(wr, wi, *power)
        wr, wi = jnp.where(later, vr, wr), jnp.where(later, vi, wi)
    wr_s[...] = wr
    wi_s[...] = wi
    acc[...] = jnp.zeros_like(acc)

    def pair(p, carry):
        rows = at(16 * p, 16)
        a = (ar_s[rows, :], ai_s[rows, :])
        base = low_powers(*a, 8)
        eight = cmul(*base[4], *base[4])

        def outer(o, w):
            wr, wi = w
            start = pl.multiple_of(64 * o, 64)
            for j in range(8):
                term = wr if j == 0 else wr * base[j][0] - wi * base[j][1]
                acc[pl.ds(start + 8 * j, 8), :] += term[:8] + term[8:]
            return cmul(wr, wi, *eight)

        lax.fori_loop(0, lags // 8, outer, (wr_s[rows, :], wi_s[rows, :]), unroll=2)
        return carry

    lax.fori_loop(0, ar_s.shape[0] // 16, pair, 0)
    k_ref[...] = jnp.sum(acc[...].reshape(lags, 8, acc.shape[1]), axis=1)


def make_taps(place, damping, frequency, timestep, mix_real, mix_imaginary, lags):
    channels, count = damping.shape
    return call(
        partial(taps_kernel, lags=lags),
        "taps",
        [((lags, channels), F32)],
        (place, damping, frequency, timestep, mix_real, mix_imaginary),
        scratch=[((count, channels), F32)] * 4 + [((lags * 8, channels), F32)],
        micros=TAPS,
    )[0]


def shifted_copies(pad, copies, lead):
    length = copies.shape[1]
    for r in range(8):
        start = 64 + lead - r
        copies[r, :, :] = pad[start : start + length, :]


def linked_blocks(edges, first, step, bound):
    blocks = edges.shape[0] // 2
    mine = edges[first] if step < 0 else edges[blocks + first]

    def more(count):
        there = jnp.clip(first + step * (count + 1), 0, blocks - 1)
        edge = edges[blocks + there] if step < 0 else edges[there]
        return jnp.logical_and(count < bound, edge == mine)

    return lax.while_loop(more, lambda c: c + 1, 0)


def tile(index):
    return at(8 * index, 8)


def fill_ids(place, own, other, own_row, other_row, edges, ids, early):
    length, channels = ids.shape
    tokens = own_row.shape[1]
    valid = place[1] > 0 if early else place[1] == 0
    near = slice(tokens - REACH, tokens) if early else slice(0, REACH)
    halo = jnp.where(valid, other_row[:, near].astype(F32), -1.0)
    mine = own_row[...].astype(F32)
    at_halo, at_own = (0, REACH) if early else (tokens, 0)
    ids[at_halo : at_halo + REACH, :] = jnp.broadcast_to(halo, (channels, REACH)).T
    ids[at_own : at_own + tokens, :] = jnp.broadcast_to(mine, (channels, tokens)).T
    blocks = length // 64
    for b in range(blocks):
        for edge, offset in ((0, 0), (blocks, 63)):
            position = 64 * b + offset
            if at_own <= position < at_own + tokens:
                edges[edge + b] = own[0, position - at_own]
            else:
                value = other[0, position - at_halo + near.start]
                edges[edge + b] = jnp.where(valid, value, -1)


def fill_taps(place, pad, mine_ref, other_ref, flip):
    mine, other = mine_ref[...], other_ref[...]
    first = jnp.where(place[1] == 0, mine, other)
    second = jnp.where(place[1] == 0, other, mine)
    half = mine.shape[0]
    pad[...] = jnp.zeros_like(pad)
    if not flip:
        pad[64 : 64 + half, :] = first
        pad[64 + half : 64 + 2 * half, :] = second
        return
    end = 64 + 2 * half
    for l in range(half):
        pad[end - 1 - l : end - l, :] = first[l : l + 1]
        pad[end - half - 1 - l : end - half - l, :] = second[l : l + 1]


def fill_rows(whole, pieces):
    start = 0
    for piece in pieces:
        whole[start : start + piece.shape[0], :] = piece[...]
        start += piece.shape[0]


def forward_kernel(
    place, own, other, own_row, other_row, k0_ref, k1_ref, halo_ref, lo_ref, hi_ref, y_ref,
    edges, pad, copies, kept, u_s, s_ref,
):
    channels = lo_ref.shape[1]
    blocks = u_s.shape[0] // 64
    ahead = REACH // 64
    fill_ids(place, own, other, own_row, other_row, edges, s_ref, True)
    fill_taps(place, pad, k0_ref, k1_ref, False)
    shifted_copies(pad, copies, 0)
    fill_rows(u_s, (halo_ref, lo_ref, hi_ref))
    for b in range(blocks):
        rows = slice(64 * b, 64 * b + 64)
        edge = edges[blocks + b].astype(F32)
        kept[rows, :] = jnp.where(s_ref[rows, :] == edge, u_s[rows, :], 0.0)

    def block(i, carry):
        mine = i + ahead
        zero = jnp.zeros((8, channels), F32)
        reach = linked_blocks(edges, mine, -1, ahead)

        def far(d, sums):
            sums = list(sums)
            start = pl.multiple_of(64 * (mine - 1 - d), 64)
            for r in range(8):
                taps = [copies[r, tile(8 * (d + 1) + m), :] for m in range(-7, 8)]
                for q in range(8):
                    u = kept[pl.ds(start + 8 * q + r, 1), :]
                    for t in range(8):
                        sums[t] += taps[t - q + 7] * u
            return tuple(sums)

        sums = lax.fori_loop(0, reach, far, (zero,) * 8)
        base = pl.multiple_of(64 * mine, 64)
        ids = [s_ref[pl.ds(base + 8 * t, 8), :] for t in range(8)]
        first = edges[mine].astype(F32)
        sums = [jnp.where(ids[t] == first, sums[t], 0.0) for t in range(8)]
        for r in range(8):
            taps = [copies[r, 8 * m : 8 * m + 8, :] for m in range(8)]
            for q in range(8):
                u = u_s[pl.ds(base + 8 * q + r, 1), :]
                own = s_ref[pl.ds(base + 8 * q + r, 1), :]
                for t in range(q, 8):
                    sums[t] += jnp.where(ids[t] == own, taps[t - q], 0.0) * u
        for t in range(0, 8, 2):
            both = jnp.concatenate([sums[t], sums[t + 1]], 0)
            y_ref[at(64 * i + 8 * t, 16), :] = both.astype(y_ref.dtype)
        return carry

    lax.fori_loop(0, blocks - ahead, block, 0)


def forward_mix(place, ids, taps, halo, low, high):
    channels = low.shape[1]
    length = halo.shape[0] + low.shape[0] + high.shape[0]
    return call(
        forward_kernel,
        "forward_mix",
        [((length - REACH, channels), BF16)],
        (place, *ids, *ids, *taps, halo, low, high),
        scalars=3,
        scratch=[
            pltpu.SMEM((2 * length // 64,), jnp.int32),
            ((64 + REACH + 128, channels), F32),
            ((8, 64 + REACH, channels), F32),
            ((length, channels), F32),
            ((length, channels), F32),
            ((length, channels), F32),
        ],
        micros=5,
    )[0]


def backward_kernel(
    place, own, other, own_row, other_row, k0_ref, k1_ref, lo_ref, hi_ref, halo_ref, slope_ref,
    part_ref, w_ref, low_ref, sum_ref, own_ref, *rest,
):
    *sends, edges, pad, copies, alive, g_s, s_ref = rest
    channels = lo_ref.shape[1]
    blocks = g_s.shape[0] // 64
    ahead = REACH // 64
    fill_ids(place, own, other, own_row, other_row, edges, s_ref, False)
    fill_taps(place, pad, k0_ref, k1_ref, True)
    shifted_copies(pad, copies, -57)
    fill_rows(g_s, (lo_ref, hi_ref, halo_ref))
    for b in range(blocks):
        rows = slice(64 * b, 64 * b + 64)
        edge = edges[b].astype(F32)
        alive[rows, :] = jnp.where(s_ref[rows, :] == edge, g_s[rows, :], 0.0)

    def block(j, total):
        zero = jnp.zeros((8, channels), F32)
        reach = linked_blocks(edges, j, 1, ahead)

        def far(d, sums):
            sums = list(sums)
            start = pl.multiple_of(64 * (j + 1 + d), 64)
            for r in range(8):
                taps = [copies[r, tile(39 - (8 * (d + 1) + m)), :] for m in range(-7, 8)]
                for q in range(8):
                    g = alive[pl.ds(start + 8 * q + r, 1), :]
                    for t in range(8):
                        sums[t] += taps[q - t + 7] * g
            return tuple(sums)

        sums = lax.fori_loop(0, reach, far, (zero,) * 8)
        base = pl.multiple_of(64 * j, 64)
        ids = [s_ref[pl.ds(base + 8 * t, 8), :] for t in range(8)]
        last = edges[blocks + j].astype(F32)
        sums = [jnp.where(ids[t] == last, sums[t], 0.0) for t in range(8)]
        for r in range(8):
            taps = [copies[r, 8 * (39 - m) : 8 * (39 - m) + 8, :] for m in range(8)]
            for q in range(8):
                g = g_s[pl.ds(base + 8 * q + r, 1), :]
                own = s_ref[pl.ds(base + 8 * q + r, 1), :]
                for t in range(q + 1):
                    sums[t] += jnp.where(ids[t] == own, taps[q - t], 0.0) * g
        for t in range(0, 8, 2):
            rows = at(64 * j + 8 * t, 16)
            both = jnp.concatenate([sums[t], sums[t + 1]], 0) * slope_ref[rows, :]
            low_ref[rows, :] = both.astype(low_ref.dtype)
            total = total + both
        return total

    total = lax.fori_loop(0, blocks - ahead, block, jnp.zeros((16, channels), F32))
    sum_ref[...] = jnp.sum(total, axis=0, keepdims=True)
    size = len(sends) + 1
    height = own_ref.shape[0]
    for k in range(size):
        rows = at(height * toward(place, k, size), height)
        piece = part_ref[rows, :] + dot_t(low_ref[rows, :], w_ref[...])
        if k == 0:
            own_ref[...] = piece
        else:
            sends[k - 1][...] = piece.astype(BF16)


def backward_mix(place, ids, taps, low, high, halo, slope, part, weight, size):
    channels = low.shape[1]
    length = halo.shape[0] + low.shape[0] + high.shape[0]
    piece = (part.shape[0] // size, part.shape[1])
    return call(
        backward_kernel,
        "backward_mix",
        [(slope.shape, BF16), ((1, channels), F32), (piece, F32)] + [(piece, BF16)] * (size - 1),
        (place, *ids, *ids, *taps, low, high, halo, slope, part, weight),
        scalars=3,
        scratch=[
            pltpu.SMEM((2 * length // 64,), jnp.int32),
            ((64 + REACH + 128, channels), F32),
            ((8, 64 + REACH, channels), F32),
            ((length, channels), F32),
            ((length, channels), F32),
            ((length, channels), F32),
        ],
        micros=6,
    )


def put_row(out_ref, start, row):
    width = out_ref.shape[1]
    for i in range(row.shape[1] // width):
        out_ref[start + i : start + i + 1, :] = row[:, width * i : width * (i + 1)]
    return start + row.shape[1] // width


def taps_back_kernel(
    place, own_id, other_id, own_row, other_row, halo_ref, ulo_ref, uhi_ref, lo_ref, hi_ref,
    out_ref, edges, kept, u_s, g_s, s_ref, sums,
):
    channels = ulo_ref.shape[1]
    blocks = u_s.shape[0] // 64
    ahead = REACH // 64
    fill_ids(place, own_id, other_id, own_row, other_row, edges, s_ref, True)
    fill_rows(u_s, (halo_ref, ulo_ref, uhi_ref))
    fill_rows(g_s, (lo_ref, hi_ref))
    sums[...] = jnp.zeros_like(sums)
    for b in range(blocks):
        rows = slice(64 * b, 64 * b + 64)
        edge = edges[blocks + b].astype(F32)
        kept[rows, :] = jnp.where(s_ref[rows, :] == edge, u_s[rows, :], 0.0)

    def block(i, carry):
        mine = i + ahead
        reach = linked_blocks(edges, mine, -1, ahead)
        base = pl.multiple_of(64 * mine, 64)
        back = pl.multiple_of(64 * i, 64)
        ids = [s_ref[pl.ds(base + 8 * t, 8), :] for t in range(8)]
        whole = [g_s[pl.ds(back + 8 * t, 8), :] for t in range(8)]
        first = edges[mine].astype(F32)
        alive = [jnp.where(ids[t] == first, whole[t], 0.0) for t in range(8)]

        def far(d, carried):
            start = pl.multiple_of(64 * (mine - 1 - d), 64)
            for r in range(8):
                found = [None] * 15
                for q in range(8):
                    u = kept[pl.ds(start + 8 * q + r, 1), :]
                    for t in range(8):
                        term = carried[t] * u
                        m = t - q + 7
                        found[m] = term if found[m] is None else found[m] + term
                for m in range(-7, 8):
                    sums[r, tile(8 * (d + 1) + m), :] += found[m + 7]
            return carried

        lax.fori_loop(0, reach, far, tuple(alive))
        for r in range(8):
            found = [None] * 8
            for q in range(8):
                u = u_s[pl.ds(base + 8 * q + r, 1), :]
                own = s_ref[pl.ds(base + 8 * q + r, 1), :]
                for t in range(q, 8):
                    term = jnp.where(ids[t] == own, whole[t], 0.0) * u
                    m = t - q
                    found[m] = term if found[m] is None else found[m] + term
            for m in range(8):
                sums[r, 8 * m : 8 * m + 8, :] += found[m]
        return carry

    lax.fori_loop(0, blocks - ahead, block, 0)
    total = sums[0, 0:REACH, :]
    for r in range(1, 8):
        total = total + sums[r, r : r + REACH, :]
    out_ref[...] = total


def gain_kernel(place, x_ref, own_ref, *rest, vectors):
    out_ref = rest[-1]
    sends = rest[: -1 - vectors]
    start = 0
    for ref in rest[-1 - vectors : -1]:
        start = put_row(out_ref, start, ref[...])
    size = len(sends) + 1
    height = own_ref.shape[0]
    gain = jnp.zeros((8, x_ref.shape[1]), F32)
    bias = gain
    step = min(64, height)
    for k in range(size):
        source = own_ref if k == 0 else sends[k - 1]

        def rows_step(i, state, source=source, k=k):
            gain, bias = state
            unit, _ = unit_rows(x_ref[at(height * toward(place, k, size) + step * i, step), :])
            part = source[at(step * i, step), :].astype(F32)
            scaled = part * unit
            for j in range(0, step, 8):
                gain = gain + scaled[j : j + 8]
                bias = bias + part[j : j + 8]
            return gain, bias

        gain, bias = lax.fori_loop(0, height // step, rows_step, (gain, bias))
    start = put_row(out_ref, start, jnp.sum(gain, axis=0, keepdims=True))
    put_row(out_ref, start, jnp.sum(bias, axis=0, keepdims=True))


def gain_sums(place, channels, rows, own, sends, vectors, ties):
    count = (sum(v.shape[1] for v in vectors) + 2 * rows.shape[1]) // channels
    return call(
        partial(gain_kernel, vectors=len(vectors)),
        "gain",
        [((count, channels), F32)],
        (place, rows, own, *sends, *vectors),
        micros=0.2,
        ties=ties,
    )[0]


def taps_back(place, ids, halo, u_low, u_high, low, high, ties):
    channels = low.shape[1]
    length = halo.shape[0] + low.shape[0] + high.shape[0]
    return call(
        taps_back_kernel,
        "taps_back",
        [((REACH, channels), F32)],
        (place, *ids, *ids, halo, u_low, u_high, low, high),
        scalars=3,
        ties=ties,
        scratch=[
            pltpu.SMEM((2 * length // 64,), jnp.int32),
            ((length, channels), F32),
            ((length, channels), F32),
            ((length - REACH, channels), F32),
            ((length, channels), F32),
            ((8, 64 + REACH, channels), F32),
        ],
        micros=TAPS_BACK,
    )[0]


def modes_back_kernel(
    place, c_ref, d_ref, f_ref, t_ref, mr_ref, mi_ref, out_ref,
    ar_s, ai_s, gr_s, gi_s, hr_s, hi_s, wide, wide_l,
):
    channels = c_ref.shape[1]
    count = ar_s.shape[0]
    half = at(count * place[1], count)
    damping, frequency, timestep = d_ref[:, half].T, f_ref[:, half].T, t_ref[...][None, :]
    ar, ai = modes(damping, frequency, timestep)
    ar_s[...] = ar
    ai_s[...] = ai
    for l in range(REACH):
        row = jnp.broadcast_to(c_ref[l : l + 1, :], (8, channels))
        wide[8 * l : 8 * l + 8, :] = row
        wide_l[8 * l : 8 * l + 8, :] = row * float(l)

    def one(p, carry):
        rows = at(8 * p, 8)
        a = (ar_s[rows, :], ai_s[rows, :])
        base = low_powers(*a, 16)
        jump = cmul(*base[8], *base[8])
        zero = jnp.zeros((8, channels), F32)

        def outer(o, state):
            pr, pi, gr, gi, hr, hi = state
            start = pl.multiple_of(128 * o, 128)
            sr = wide[pl.ds(start, 8), :]
            tr = wide_l[pl.ds(start, 8), :]
            si = zero
            ti = zero
            for j in range(1, 16):
                c = wide[pl.ds(start + 8 * j, 8), :]
                e = wide_l[pl.ds(start + 8 * j, 8), :]
                br, bi = base[j]
                sr += c * br
                si += c * bi
                tr += e * br
                ti += e * bi
            gr += pr * sr - pi * si
            gi += pr * si + pi * sr
            hr += pr * tr - pi * ti
            hi += pr * ti + pi * tr
            pr, pi = cmul(pr, pi, *jump)
            return pr, pi, gr, gi, hr, hi

        one_ = jnp.ones((8, channels), F32)
        _, _, gr, gi, hr, hi = lax.fori_loop(
            0, REACH // 16, outer, (one_, zero, zero, zero, zero, zero), unroll=2
        )
        gr_s[rows, :] = gr
        gi_s[rows, :] = gi
        hr_s[rows, :] = hr
        hi_s[rows, :] = hi
        return carry

    lax.fori_loop(0, ar_s.shape[0] // 8, one, 0)
    gr, gi, hr, hi = gr_s[...], gi_s[...], hr_s[...], hi_s[...]
    mr, mi = mr_ref[:, half].T, mi_ref[:, half].T
    qr, qi = ratios(damping, frequency, ar, ai)
    wr, wi = cmul(mr, mi, qr, qi)
    mixr, mixi = cmul(qr, qi, gr, gi)
    inverse = 1.0 / (damping * damping + frequency * frequency)
    nr, ni = -damping * inverse, -frequency * inverse
    vr, vi = cmul(*cmul(mr, mi, gr, gi), nr, ni)
    xr, xi = cmul(vr, vi, ar, ai)
    zr, zi = cmul(wr, wi, hr, hi)
    xr, xi = xr + zr, xi + zi
    yr, yi = cmul(vr, vi, qr, qi)
    grads = (yr - timestep * xr, yi - timestep * xi, mixr, -mixi)
    for i, grad in enumerate(grads):
        out_ref[channels * i : channels * (i + 1), :] = grad.T
    out_ref[4 * channels :, 0:channels] = jnp.broadcast_to(
        jnp.sum(-damping * xr - frequency * xi, axis=0, keepdims=True), (8, channels)
    )


def modes_back(place, c, damping, frequency, timestep, mix_real, mix_imaginary):
    channels, count = damping.shape
    count = count // 2
    return call(
        modes_back_kernel,
        "modes_back",
        [((4 * channels + 8, count), F32)],
        (place, c, damping, frequency, timestep, mix_real, mix_imaginary),
        scratch=[((count, channels), F32)] * 6 + [((REACH * 8, channels), F32)] * 2,
        micros=MODES_BACK,
    )[0]


def unit_rows(x):
    x = x.astype(F32)
    shifted = x - jnp.mean(x, axis=-1, keepdims=True)
    inverse = lax.rsqrt(jnp.mean(shifted * shifted, axis=-1, keepdims=True) + EPSILON)
    return shifted * inverse, inverse


def norm_kernel(x_ref, gain_ref, bias_ref, out_ref):
    def step(i, carry):
        rows = at(128 * i, 128)
        unit, _ = unit_rows(x_ref[rows, :])
        out_ref[rows, :] = (unit * gain_ref[...][None, :] + bias_ref[...][None, :]).astype(BF16)
        return carry

    lax.fori_loop(0, x_ref.shape[0] // 128, step, 0)


def reduce_kernel(place, x_ref, b_ref, *rest, count):
    pieces = rest[:count]
    lo_ref, hi_ref, slope_ref, full_ref = rest[count:]
    depth = pieces[0].shape[0]
    for k in range(count):
        full_ref[at(depth * (place[0] ^ k if count > 1 else 0), depth), :] = pieces[k][...]
    half = lo_ref.shape[0]
    for part, out in enumerate((lo_ref, hi_ref)):
        rows = slice(half * part, half * part + half)
        act, slope = gelu_pair(dot(x_ref[rows, :], full_ref[...]) + b_ref[...][None, :])
        out[...] = act
        slope_ref[rows, :] = slope


def gate_kernel(x_ref, w_ref, b_ref, act_ref, slope_ref):
    def step(i, carry):
        rows = at(128 * i, 128)
        act, slope = gelu_pair(dot(x_ref[rows, :], w_ref[...]) + b_ref[...][None, :])
        act_ref[rows, :] = act.astype(BF16)
        slope_ref[rows, :] = slope.astype(BF16)
        return carry

    lax.fori_loop(0, x_ref.shape[0] // 128, step, 0)


def pack_kernel(place, gate_ref, expand_ref, output_ref, mine_ref, rest_ref):
    rows = gate_ref.shape[0]
    some = expand_ref.shape[0] // 2

    def store(first_ref, second_ref):
        first_ref[0:rows, :] = gate_ref[...]
        first_ref[rows:, :] = expand_ref[0:some, :]
        second_ref[0:rows, :] = output_ref[...].T
        second_ref[rows:, :] = expand_ref[some:, :]

    @pl.when(place[1] == 0)
    def _():
        store(mine_ref, rest_ref)

    @pl.when(place[1] != 0)
    def _():
        store(rest_ref, mine_ref)


def stack_kernel(*refs):
    for k, ref in enumerate(refs[:-1]):
        refs[-1][k] = ref[...]


def unpack_kernel(place, mine_ref, rest_ref, near_ref, far_ref, gate_ref, expand_ref, output_ref):
    mines = [mine_ref] + [near_ref.at[k] for k in range(3)]
    rests = [rest_ref] + [far_ref.at[k] for k in range(3)]
    rows = gate_ref.shape[0] // 4
    some = expand_ref.shape[0] // 8

    def store(firsts, seconds):
        for k in range(4):
            s = place[0] ^ k
            gate_ref[at(rows * s, rows), :] = firsts[k][0:rows, :]
            output_ref[at(rows * s, rows), :] = seconds[k][0:rows, :]
            expand_ref[at(2 * some * s, some), :] = firsts[k][rows:, :]
            expand_ref[at(2 * some * s + some, some), :] = seconds[k][rows:, :]

    @pl.when(place[1] == 0)
    def _():
        store(mines, rests)

    @pl.when(place[1] != 0)
    def _():
        store(rests, mines)


def expand_kernel(place, act_ref, slope_ref, we_ref, b_ref, wo_ref, *rest, size):
    pieces, rest = rest[:size], rest[size:]
    gated_ref, coef_ref, own_ref, *sends = rest
    height = own_ref.shape[0]
    channels = pieces[0].shape[1]
    for k in range(size):
        rows = at(height * toward(place, k, size), height)
        expanded = b_ref[...][None, :]
        for j in range(size):
            source = origin(place, j, size)
            expanded = expanded + dot(pieces[j][rows, :], we_ref[at(channels * source, channels), :])
        coef_ref[rows, :] = (slope_ref[rows, :].astype(F32) * expanded).astype(BF16)
        gated = (expanded * act_ref[rows, :].astype(F32)).astype(BF16)
        gated_ref[rows, :] = gated
        piece = dot_t(gated, wo_ref[...])
        if k == 0:
            own_ref[...] = piece
        else:
            sends[k - 1][...] = piece.astype(BF16)


def loss_kernel(
    place, x_ref, t_ref, mask_ref, b_ref, act_ref, coef_ref, wo_ref, we_ref, *rest, size
):
    pieces, rest = rest[:size], rest[size:]
    out_ref, back_ref, keep_ref, low_ref, gate_ref, ob_ref, eb_ref, gb_ref, err_ref, own_ref, *rest = rest
    sends, mask_s = rest[:-1], rest[-1]
    height = pieces[0].shape[0]
    channels = own_ref.shape[1]
    mask_s[...] = jnp.broadcast_to(mask_ref[...].astype(F32), (mask_s.shape[1], mask_s.shape[0])).T
    outb = jnp.zeros_like(ob_ref)
    expb = jnp.zeros_like(eb_ref)
    gatb = jnp.zeros_like(gb_ref)
    errors = jnp.zeros((1, 1), F32)
    for j in range(size):
        rows = at(height * origin(place, j, size), height)
        result = x_ref[rows, :].astype(F32) + pieces[j][...].astype(F32) + b_ref[...][None, :]
        out_ref[rows, :] = result.astype(BF16)
        back = (result - t_ref[rows, :].astype(F32)) * mask_s[rows, 0:1]
        low = back.astype(BF16)
        back_ref[rows, :] = low
        if j == 0:
            keep_ref[...] = back
        outb = outb + jnp.sum(back, axis=0, keepdims=True)
        errors = errors + jnp.sum(jnp.sum(back * back, axis=0, keepdims=True), axis=1, keepdims=True)
        gated_back = dot(low, wo_ref[...])
        expanded_back = gated_back * act_ref[rows, :].astype(F32)
        expb = expb + jnp.sum(expanded_back, axis=0, keepdims=True)
        expand_low = expanded_back.astype(BF16)
        low_ref[rows, :] = expand_low
        gate_back = gated_back * coef_ref[rows, :].astype(F32)
        gatb = gatb + jnp.sum(gate_back, axis=0, keepdims=True)
        gate_ref[rows, :] = gate_back.astype(BF16)
        for k in range(size):
            target = toward(place, k, size)
            part = dot_t(expand_low, we_ref[at(channels * target, channels), :])
            if k == 0:
                own_ref[rows, :] = part
            else:
                sends[k - 1][rows, :] = part.astype(BF16)
    ob_ref[...] = outb
    eb_ref[...] = expb
    gb_ref[...] = gatb
    count = jnp.sum(mask_ref[...].astype(F32), axis=1, keepdims=True)
    half = err_ref.shape[1] // 2
    err_ref[...] = jnp.concatenate(
        [jnp.broadcast_to(errors, (1, half)), jnp.broadcast_to(count, (1, half))], 1
    )


def sum_kernel(own_ref, *rest):
    *pieces, lo_ref, hi_ref = rest
    total = own_ref[...]
    for piece in pieces:
        total = total + piece[...].astype(F32)
    half = lo_ref.shape[0]
    lo_ref[...] = total[:half]
    hi_ref[...] = total[half:]


def scale_of(total_ref, scale):
    row, tokens_all = scale
    return tokens_all / total_ref[row : row + 1, 0:1]


EXTRA = 16


def rows_kernel(place, x_ref, gain_ref, keep_ref, total_ref, own_ref, *rest, scale):
    *pieces, out_ref = rest
    height, features = own_ref.shape
    step = 32
    factor = scale_of(total_ref, scale)
    gain = gain_ref[...][None, :]

    def one(i, carry):
        rows = at(step * i, step)
        total = own_ref[rows, :]
        for piece in pieces:
            total = total + piece[rows, :].astype(F32)
        unit, inverse = unit_rows(x_ref[at(height * place[2] + step * i, step), :])
        scaled = total * gain
        back = inverse * (
            scaled
            - jnp.mean(scaled, axis=-1, keepdims=True)
            - unit * jnp.mean(scaled * unit, axis=-1, keepdims=True)
        )
        out_ref[rows, :] = (factor * (keep_ref[rows, :] + back)).astype(BF16)
        return carry

    lax.fori_loop(0, height // step, one, 0, unroll=2)
    width = total_ref.shape[1]
    count = features // width
    start = total_ref.shape[0] - 2 * count
    both = []
    for v in range(2):
        first = start + count * v
        both.append(
            jnp.concatenate(
                [total_ref[first + i : first + i + 1, :] for i in range(count)], axis=1
            )
        )
    both.append(jnp.zeros((EXTRA - 2, features), F32))
    out_ref[height:, :] = (factor * jnp.concatenate(both, 0)).astype(BF16)


def join_kernel(place, *rest):
    *pieces, out_ref, norm_ref, parts = rest
    size = len(pieces)
    height = pieces[0].shape[0] - EXTRA
    for k in range(size):
        source = origin(place, k, size)
        out_ref[at(height * source, height), :] = pieces[k][0:height, :]
        parts[source] = pieces[k][height:, :].astype(F32)
    total = parts[0]
    for k in range(1, size):
        total = total + parts[k]
    norm_ref[...] = total


def finish_kernel(place, sum_ref, mine_ref, other_ref, *outs, starts, scale):
    dd_ref, df_ref, dmr_ref, dmi_ref, dt_ref, loss_ref, *vectors = outs
    channels, count = dd_ref.shape
    count = count // 2
    counted = sum_ref[scale[0] : scale[0] + 1, 0:1]
    loss_ref[...] = sum_ref[scale[0] - 1 : scale[0], 0:1] / (counted * scale[2])
    scale = scale_of(sum_ref, scale[:2])
    for i, out in enumerate((dd_ref, df_ref, dmr_ref, dmi_ref)):
        rows = slice(channels * i, channels * (i + 1))
        out[:, at(count * place[1], count)] = mine_ref[rows, :] * scale
        out[:, at(count * (1 - place[1]), count)] = other_ref[rows, :] * scale
    row = slice(4 * channels, 4 * channels + 1)
    dt_ref[...] = (mine_ref[row, 0:channels] + other_ref[row, 0:channels]) * scale
    width = sum_ref.shape[1]
    for out, start in zip(vectors, starts):
        for i in range(out.shape[1] // width):
            out[:, width * i : width * (i + 1)] = sum_ref[start + i : start + i + 1, :] * scale


def early_kernel(place, gated_ref, back_ref, low_ref, *rest, size):
    pieces, (keep_ref, give_ref, mixed_s) = rest[:size], rest[size:]
    core = place[1]
    channels = pieces[0].shape[1]
    for j in range(size):
        source = origin(place, j, size)
        mixed_s[:, at(channels * source, channels)] = pieces[j][...]
    half = back_ref.shape[1] // 8
    some = mixed_s.shape[1] // 8
    for s in range(4):
        k = s
        keep_ref[k, 0:half, :] = t_dot(back_ref[:, at((2 * s + core) * half, half)], gated_ref[...])
        give_ref[k, 0:half, :] = t_dot(
            back_ref[:, at((2 * s + 1 - core) * half, half)], gated_ref[...]
        ).astype(BF16)
        both = t_dot(mixed_s[:, at(2 * some * s, 2 * some)], low_ref[...])
        keep_ref[k, half:, :] = jnp.where(core == 0, both[:some], both[some:])
        give_ref[k, half:, :] = jnp.where(core == 0, both[some:], both[:some]).astype(BF16)


def late_kernel(place, x_ref, gate_ref, reduce_ref, keep_ref, give_ref):
    core = place[1]
    half = x_ref.shape[1] // 8
    units = gate_ref.shape[1]
    for s in range(4):
        k = s
        mine = x_ref[:, at((2 * s + core) * half, half)]
        keep_ref[k, :, 0:units] = t_dot(mine, gate_ref[...])
        keep_ref[k, :, units:] = t_dot(mine, reduce_ref[...])
        other = x_ref[:, at((2 * s + 1 - core) * half, half)]
        give_ref[k, :, 0:units] = t_dot(other, gate_ref[...]).astype(BF16)
        give_ref[k, :, units:] = t_dot(other, reduce_ref[...]).astype(BF16)


def pair_kernel(place, keep_ref, got_ref, own_ref, *sends):
    s = place[0]
    own_ref[...] = keep_ref[s] + got_ref[s].astype(F32)
    for k in (1, 2, 3):
        sends[k - 1][...] = (keep_ref[s ^ k] + got_ref[s ^ k].astype(F32)).astype(BF16)


def early_out_kernel(place, own_ref, other_ref, total_ref, output_ref, expand_ref, *, scale):
    scale = scale_of(total_ref, scale)
    mine, other = own_ref[...].astype(F32) * scale, other_ref[...].astype(F32) * scale
    first = jnp.where(place[1] == 0, mine, other)
    second = jnp.where(place[1] == 0, other, mine)
    half = output_ref.shape[1] // 2
    some = expand_ref.shape[0] // 2
    output_ref[...] = jnp.concatenate([first[:half], second[:half]], 0).T
    expand_ref[0:some, :] = first[half:]
    expand_ref[some:, :] = second[half:]


def late_out_kernel(place, own_ref, other_ref, total_ref, gate_ref, reduce_ref, *, scale):
    scale = scale_of(total_ref, scale)
    mine, other = own_ref[...].astype(F32) * scale, other_ref[...].astype(F32) * scale
    first = jnp.where(place[1] == 0, mine, other)
    second = jnp.where(place[1] == 0, other, mine)
    half = gate_ref.shape[0] // 2
    units = gate_ref.shape[1]
    gate_ref[0:half, :] = first[:, :units]
    gate_ref[half:, :] = second[:, :units]
    reduce_ref[0:half, :] = first[:, units:]
    reduce_ref[half:, :] = second[:, units:]


def pair_grads(place, keep, give):
    shape = keep.shape[1:]
    return call(
        pair_kernel,
        "pair",
        [(shape, F32)] + [(shape, BF16)] * 3,
        (place, keep, swap_context(give)),
        micros=PAIR,
    )


def send_grads(pieces):
    own, *sends = pieces
    for k in (1, 2, 3):
        own = own + lax.ppermute(sends[k - 1], "shard", xor_pairs(4, k)).astype(F32)
    return own, swap_context(own)


def plain_grad(grad, scale, axis):
    paired = lax.psum(grad.astype(BF16), "context").astype(F32)
    return scale * lax.psum_scatter(paired, "shard", scatter_dimension=axis, tiled=True)


def per_device(
    inputs,
    teacher,
    segment_ids,
    valid_mask,
    norm_gain,
    norm_bias,
    gate_weight,
    gate_bias,
    reduce_weight,
    reduce_bias,
    damping,
    frequency,
    timestep,
    mix_real,
    mix_imaginary,
    expand_weight,
    expand_bias,
    output_weight,
    output_bias,
):
    tokens, width = inputs.shape
    channels = reduce_bias.shape[0]
    units = gate_bias.shape[0]
    size = lax.axis_size("tensor")
    shards = lax.axis_size("shard")
    contexts = lax.axis_size("context")
    core = lax.axis_index("context")
    shard = lax.axis_index("shard")
    tensor = lax.axis_index("tensor")
    fast = shards == 4 and contexts == 2 and size == 4
    height = tokens // size
    place = jnp.stack([shard, core, tensor]).astype(jnp.int32)

    ids = (segment_ids, swap_context(segment_ids))
    if fast:
        found = [lax.ppermute(reduce_weight, "shard", xor_pairs(4, k)) for k in (1, 2, 3)]
        reduce_pieces = [reduce_weight] + found
        some = expand_weight.shape[0] // 2
        shape = (gate_weight.shape[0] + some, units)
        mine, rest = call(
            pack_kernel, "pack", [(shape, BF16)] * 2, (place, gate_weight, expand_weight, output_weight)
        )
        nears = [lax.ppermute(mine, "shard", xor_pairs(4, k)) for k in (1, 2, 3)]
    else:
        reduce_pieces = [lax.all_gather(reduce_weight, "shard", axis=0, tiled=True)]
        gate_full = lax.all_gather(gate_weight, "shard", axis=0, tiled=True)
        expand_full = lax.all_gather(expand_weight, "shard", axis=0, tiled=True)
        output_full = lax.all_gather(output_weight.T, "shard", axis=0, tiled=True)

    (normed,) = call(
        norm_kernel,
        "norm",
        [(inputs.shape, BF16)],
        (inputs, norm_gain, norm_bias),
        scalars=0,
    )
    mode_args = (damping, frequency, timestep, mix_real, mix_imaginary)
    taps_mine = make_taps(place, *mode_args, REACH // 2)
    taps = (taps_mine, swap_context(taps_mine))
    half_rows = (tokens // 2, channels)
    u_low, u_high, reduce_slope, reduce_full = call(
        partial(reduce_kernel, count=len(reduce_pieces)),
        "reduce",
        [(half_rows, F32), (half_rows, F32), ((tokens, channels), F32), ((width, channels), BF16)],
        (place, normed, reduce_bias, *reduce_pieces),
    )
    before = [(i, i + 1) for i in range(contexts - 1)]
    after = [(i + 1, i) for i in range(contexts - 1)]
    halo = lax.ppermute(u_high[tokens // 2 - REACH :], "context", before)
    mixed_own = forward_mix(place, ids, taps, halo, u_low, u_high)
    mixed = [mixed_own] + spread_tensor(mixed_own)
    if fast:
        shape = (3,) + mine.shape
        (near,) = call(stack_kernel, "stack", [(shape, BF16)], nears, scalars=0, ties=(mixed_own,))
        gate_full, expand_full, output_full = call(
            unpack_kernel,
            "unpack",
            [
                ((4 * gate_weight.shape[0], units), BF16),
                ((4 * expand_weight.shape[0], units), BF16),
                ((width, units), BF16),
            ],
            (place, mine, rest, near, swap_context(near)),
            micros=1,
        )
    gate_act, gate_slope = call(
        gate_kernel,
        "gate",
        [((tokens, units), BF16)] * 2,
        (normed, gate_full, gate_bias),
        scalars=0,
        micros=4,
    )
    piece = (height, width)
    gated, coef, branch_part, *branch_sends = call(
        partial(expand_kernel, size=size),
        "expand",
        [((tokens, units), BF16), ((tokens, units), BF16), (piece, F32)] + [(piece, BF16)] * (size - 1),
        (place, gate_act, gate_slope, expand_full, expand_bias, output_full, *mixed),
        micros=4,
    )
    for got in deliver_tensor(branch_sends):
        branch_part = branch_part + got.astype(F32)
    branch_own = branch_part.astype(BF16)
    branch = [branch_own] + spread_tensor(branch_own)

    output, branch_back, keep_back, expand_low, gate_low, *rest = call(
        partial(loss_kernel, size=size),
        "loss",
        [
            (inputs.shape, BF16),
            (inputs.shape, BF16),
            (piece, F32),
            ((tokens, units), BF16),
            ((tokens, units), BF16),
            ((1, width), F32),
            ((1, units), F32),
            ((1, units), F32),
            ((1, 2 * channels), F32),
            ((tokens, channels), F32),
        ]
        + [((tokens, channels), BF16)] * (size - 1),
        (
            place,
            inputs,
            teacher,
            valid_mask,
            output_bias,
            gate_act,
            coef,
            output_full,
            expand_full,
            *branch,
        ),
        scratch=[((tokens, 128), F32)],
        micros=8,
    )
    output_sum, expand_sum, gate_sum, error_row, back_part, *back_sends = rest
    back_got = deliver_tensor(back_sends)
    ties = ()
    if fast:
        shape = (4, (gate_weight.shape[0] + expand_weight.shape[0]) // 2, units)
        early = call(
            partial(early_kernel, size=size),
            "early",
            [(shape, F32), (shape, BF16)],
            (place, gated, branch_back, expand_low, *mixed),
            scratch=[((tokens, size * channels), BF16)],
            micros=EARLY,
            ties=(),
        )
        early = pair_grads(place, *early)
        ties = ()
    g_low, g_high = call(
        sum_kernel,
        "sum",
        [(half_rows, F32)] * 2,
        (back_part, *back_got),
        scalars=0,
        ties=ties,
    )
    halo_back = lax.ppermute(g_low[:REACH], "context", after)
    gate_part = dot_t(gate_low, gate_full)
    reduce_low, reduce_sum, normed_part, *normed_sends = backward_mix(
        place, ids, taps, g_low, g_high, halo_back, reduce_slope, gate_part, reduce_full, size
    )
    normed_got = deliver_tensor(normed_sends)

    vectors = (gate_sum, expand_sum, output_sum, reduce_sum, error_row)
    pack = gain_sums(place, channels, inputs, normed_part, normed_sends, vectors, ())
    norm_at = pack.shape[0] - 2 * width // channels
    total = sum_over(sum_over(pack, "context"), "shard")
    error_at = norm_at - 2
    taps_grad = taps_back(place, ids, halo, u_low, u_high, g_low, g_high, ())
    taps_grad = sum_over(sum_over(taps_grad, "context"), "shard")
    tokens_all = float(tokens * shards * contexts)

    scale = (error_at + 1, tokens_all)

    (rows_own,) = call(
        partial(rows_kernel, scale=scale),
        "rows",
        [((height + EXTRA, width), BF16)],
        (place, inputs, norm_gain, keep_back, total, normed_part, *normed_got),
        micros=3,
    )
    inputs_grad, norm_grads = call(
        join_kernel,
        "join",
        [(inputs.shape, BF16), ((EXTRA, width), F32)],
        (place, rows_own, *spread_tensor(rows_own)),
        scratch=[((size, EXTRA, width), F32)],
    )
    mode_mine = modes_back(place, taps_grad, *mode_args)
    mode_other = swap_context(mode_mine)

    if fast:
        output_grad, expand_grad = call(
            partial(early_out_kernel, scale=scale),
            "early_out",
            [(output_weight.shape, F32), (expand_weight.shape, F32)],
            (place, *send_grads(early), total),
        )
        shape = (4, gate_weight.shape[0] // 2, units + channels)
        late = call(
            late_kernel,
            "late",
            [(shape, F32), (shape, BF16)],
            (place, normed, gate_low, reduce_low),
            micros=LATE,
            ties=(),
        )
        gate_grad, reduce_grad = call(
            partial(late_out_kernel, scale=scale),
            "late_out",
            [(gate_weight.shape, F32), (reduce_weight.shape, F32)],
            (place, *send_grads(pair_grads(place, *late)), total),
        )
    else:
        factor = tokens_all / total[error_at + 1, 0]
        mixed_full = lax.all_gather(mixed_own, "tensor", axis=1, tiled=True)
        output_grad = plain_grad(t_dot(gated, branch_back), factor, 1)
        expand_grad = plain_grad(t_dot(mixed_full, expand_low), factor, 0)
        gate_grad = plain_grad(t_dot(normed, gate_low), factor, 0)
        reduce_grad = plain_grad(t_dot(normed, reduce_low), factor, 0)

    counts = [v.shape[1] // channels for v in vectors]
    offsets = [sum(counts[:i]) for i in range(4)]
    whole = (damping.shape, F32)
    *mode_grads, timestep_grad, loss_value, gate_bias_grad, expand_bias_grad, output_bias_grad, reduce_bias_grad = call(
        partial(finish_kernel, starts=offsets, scale=scale + (float(width),)),
        "finish",
        [whole] * 4 + [((1, n), F32) for n in (channels, 1, units, units, width, channels)],
        (place, total, mode_mine, mode_other),
    )
    return (
        output,
        loss_value.reshape(()),
        inputs_grad,
        norm_grads[0],
        norm_grads[1],
        gate_grad,
        gate_bias_grad[0],
        reduce_grad,
        reduce_bias_grad[0],
        mode_grads[0],
        mode_grads[1],
        timestep_grad[0],
        mode_grads[2],
        mode_grads[3],
        expand_grad,
        expand_bias_grad[0],
        output_grad,
        output_bias_grad[0],
    )


def solution(mesh):
    tokens = P(("shard", "context"), None)
    ids = P("shard", "context")
    split = P("shard", "tensor")
    rows = P("tensor", None)
    units = P("tensor")
    return jax.shard_map(
        per_device,
        mesh=mesh,
        in_specs=(
            tokens, tokens, ids, ids, P(), P(), split, units, split, units,
            rows, rows, units, rows, rows, split, units, P("tensor", "shard"), P(),
        ),
        out_specs=(
            tokens, P(), tokens, P(), P(), split, units, split, units,
            rows, rows, units, rows, rows, split, units, P("tensor", "shard"), P(),
        ),
        check_vma=False,
    )
```

```python
import math
from functools import partial

import jax
import jax.numpy as jnp
from jax import lax
from jax.experimental import pallas as pl
from jax.experimental.pallas import tpu as pltpu
from jax.sharding import PartitionSpec as P

REACH = 256
EPSILON = 1e-05
EARLY, PAIR, LATE, TAPS_BACK, MODES_BACK, TAPS = 2, 1, 2, 4, 4, 9
GELU_SCALE = 0.7978845608028654
F32 = jnp.float32
BF16 = jnp.bfloat16
SMEM_SPEC = pl.BlockSpec(memory_space=pltpu.SMEM)
VMEM_SPEC = pl.BlockSpec(memory_space=pltpu.VMEM)


def call(body, name, outs, args, scalars=1, scratch=(), micros=2, ties=()):
    held = [(a.shape, a.dtype) for a in args[scalars:]] + list(outs)
    held += [entry for entry in scratch if isinstance(entry, tuple)]
    room = 0
    for shape, kind in held:
        shape = (8,) * (2 - len(shape)) + tuple(shape)
        room += math.prod(shape[:-2] + (max(shape[-2], 8), max(shape[-1], 128))) * jnp.dtype(kind).itemsize
    count = len(args)

    def kernel(*refs):
        body(*refs[:count], *refs[count + len(ties) :])

    return pl.pallas_call(
        kernel,
        out_shape=[jax.ShapeDtypeStruct(shape, kind) for shape, kind in outs],
        in_specs=[SMEM_SPEC] * scalars
        + [VMEM_SPEC] * (len(args) - scalars)
        + [pl.BlockSpec(memory_space=pl.ANY)] * len(ties),
        out_specs=[VMEM_SPEC] * len(outs),
        scratch_shapes=[
            pltpu.VMEM(*entry) if isinstance(entry, tuple) else entry for entry in scratch
        ],
        compiler_params=pltpu.CompilerParams(vmem_limit_bytes=room + room // 16 + (3 << 20)),
        cost_estimate=pl.CostEstimate(
            flops=int(micros * 0.2e9), bytes_accessed=int(micros * 1e5), transcendentals=0
        ),
        name=name,
    )(*args, *ties)


def dot(a, b):
    return jnp.dot(a, b, preferred_element_type=F32)


def dot_t(a, b):
    return lax.dot_general(a, b, (((1,), (1,)), ((), ())), preferred_element_type=F32)


def t_dot(a, b):
    return lax.dot_general(a, b, (((0,), (0,)), ((), ())), preferred_element_type=F32)


def at(start, size, unit=None):
    return pl.ds(pl.multiple_of(start, unit or size), size)


def gelu_pair(a):
    square = a * a
    bent = jnp.tanh(GELU_SCALE * (a + 0.044715 * (a * square)))
    half = 0.5 * (1.0 + bent)
    slope = half + 0.5 * a * (1.0 - bent * bent) * (GELU_SCALE + 3 * 0.044715 * GELU_SCALE * square)
    return a * half, slope


def xor_pairs(size, mask):
    return [(i, i ^ mask) for i in range(size)]


def shift_pairs(size, step):
    return [(i, (i + step) % size) for i in range(size)]


def swap_context(x):
    return lax.ppermute(x, "context", [(0, 1), (1, 0)])


def sum_over(x, axis):
    size = lax.axis_size(axis)
    if size == 4:
        first = lax.ppermute(x, axis, xor_pairs(4, 1))
        second = lax.ppermute(x, axis, xor_pairs(4, 2))
        third = lax.ppermute(x, axis, xor_pairs(4, 3))
        return (x + first) + (second + third)
    step = 1
    while step < size:
        x = x + lax.ppermute(x, axis, xor_pairs(size, step))
        step *= 2
    return x


def copy_kernel(x_ref, out_ref):
    out_ref[...] = x_ref[...]


def add_kernel(x_ref, y_ref, z_ref, sum_ref, copy_ref):
    sum_ref[...] = (x_ref[...].astype(F32) + y_ref[...].astype(F32)).astype(BF16)
    copy_ref[...] = z_ref[...]


def toward(place, k, size):
    return place[2] ^ k if size == 4 else lax.rem(place[2] + k, size)


def origin(place, k, size):
    return place[2] ^ k if size == 4 else lax.rem(place[2] + size - k, size)


def tensor_pairs(size, k):
    return xor_pairs(size, k) if size == 4 else shift_pairs(size, k)


def exchange_tensor(pieces):
    size = lax.axis_size("tensor")
    return [lax.ppermute(x, "tensor", tensor_pairs(size, k + 1)) for k, x in enumerate(pieces)]


def stage_kernel(x_ref, y_ref, z_ref, w_ref, sum_ref, copy_ref, next_ref):
    sum_ref[...] = (x_ref[...].astype(F32) + y_ref[...].astype(F32)).astype(BF16)
    copy_ref[...] = z_ref[...]
    next_ref[...] = w_ref[...]


def sum_tensor(owns, sends):
    size = lax.axis_size("tensor")
    if size != 4:
        found = []
        for own, pieces in zip(owns, sends):
            for got in exchange_tensor(pieces):
                own = own + got.astype(F32)
            own = own.astype(BF16)
            found.append([own] + exchange_tensor([own] * (size - 1)))
        return found
    near_pairs, far_pairs = xor_pairs(4, 1), xor_pairs(4, 2)

    def stage(pieces, passed, after):
        return call(
            stage_kernel,
            "stage",
            [(passed.shape, BF16)] * 3,
            (pieces[1], passed, pieces[0], after),
            scalars=0,
            micros=0.5,
        )

    first, second = sends
    passed = lax.ppermute(first[2], "tensor", near_pairs)
    joined, near, after = stage(first, passed, second[2])
    first_far = lax.ppermute(joined, "tensor", far_pairs)
    passed = lax.ppermute(after, "tensor", near_pairs)
    first_near = lax.ppermute(near, "tensor", near_pairs)
    joined, near, _ = stage(second, passed, second[0])
    second_far = lax.ppermute(joined, "tensor", far_pairs)
    second_near = lax.ppermute(near, "tensor", near_pairs)
    found = []
    for own, far, near in ((owns[0], first_far, first_near), (owns[1], second_far, second_near)):
        total = (own + (far.astype(F32) + near.astype(F32))).astype(BF16)
        away = lax.ppermute(total, "tensor", far_pairs)
        beside = lax.ppermute(total, "tensor", near_pairs)
        found.append([total, beside, away, lax.ppermute(away, "tensor", near_pairs)])
    return found


def spread_tensor(x, ties=()):
    size = lax.axis_size("tensor")
    if size == 4:
        near = lax.ppermute(x, "tensor", xor_pairs(4, 1))
        far = lax.ppermute(x, "tensor", xor_pairs(4, 2))
        (again,) = call(
            copy_kernel,
            "again",
            [(x.shape, x.dtype)],
            (far,),
            scalars=0,
            micros=0.5,
            ties=(near,) + ties,
        )
        return [near, far, lax.ppermute(again, "tensor", xor_pairs(4, 1))]
    return [lax.ppermute(x, "tensor", shift_pairs(size, k)) for k in range(1, size)]


def deliver_tensor(pieces):
    size = lax.axis_size("tensor")
    if size == 4:
        passed = lax.ppermute(pieces[2], "tensor", xor_pairs(4, 1))
        joined, near = call(
            add_kernel,
            "joined",
            [(passed.shape, BF16)] * 2,
            (pieces[1], passed, pieces[0]),
            scalars=0,
            micros=0.5,
        )
        found = [
            lax.ppermute(near, "tensor", xor_pairs(4, 1)),
            lax.ppermute(joined, "tensor", xor_pairs(4, 2)),
        ]
        return found, joined
    found = [lax.ppermute(x, "tensor", shift_pairs(size, k + 1)) for k, x in enumerate(pieces)]
    return found, found[0]


def cmul(ar, ai, br, bi):
    return ar * br - ai * bi, ar * bi + ai * br


def modes(damping, frequency, timestep):
    magnitude = jnp.exp(-timestep * damping)
    angle = timestep * frequency
    return magnitude * jnp.cos(angle), magnitude * jnp.sin(angle)


def ratios(damping, frequency, ar, ai):
    minus = ar - 1.0
    inverse = 1.0 / (damping * damping + frequency * frequency)
    return (ai * frequency - minus * damping) * inverse, -(
        minus * frequency + ai * damping
    ) * inverse


def low_powers(ar, ai, count):
    found = [None, (ar, ai)]
    for j in range(2, count):
        found.append(cmul(*found[j // 2], *found[j - j // 2]))
    return found


def taps_kernel(place, d_ref, f_ref, t_ref, mr_ref, mi_ref, k_ref, ar_s, ai_s, wr_s, wi_s, acc, lags):
    damping, frequency, timestep = d_ref[...].T, f_ref[...].T, t_ref[...][None, :]
    ar, ai = modes(damping, frequency, timestep)
    qr, qi = ratios(damping, frequency, ar, ai)
    mr, mi = mr_ref[...].T, mi_ref[...].T
    wr, wi = mr * qr - mi * qi, mr * qi + mi * qr
    ar_s[...] = ar
    ai_s[...] = ai
    if lags < REACH:
        power = (ar, ai)
        for _ in range(lags.bit_length() - 1):
            power = cmul(*power, *power)
        later = place[1] > 0
        vr, vi = cmul(wr, wi, *power)
        wr, wi = jnp.where(later, vr, wr), jnp.where(later, vi, wi)
    wr_s[...] = wr
    wi_s[...] = wi
    acc[...] = jnp.zeros_like(acc)

    def pair(p, carry):
        rows = at(16 * p, 16)
        a = (ar_s[rows, :], ai_s[rows, :])
        base = low_powers(*a, 8)
        eight = cmul(*base[4], *base[4])

        def outer(o, w):
            wr, wi = w
            start = pl.multiple_of(64 * o, 64)
            for j in range(8):
                term = wr if j == 0 else wr * base[j][0] - wi * base[j][1]
                acc[pl.ds(start + 8 * j, 8), :] += term[:8] + term[8:]
            return cmul(wr, wi, *eight)

        lax.fori_loop(0, lags // 8, outer, (wr_s[rows, :], wi_s[rows, :]), unroll=4)
        return carry

    lax.fori_loop(0, ar_s.shape[0] // 16, pair, 0)
    k_ref[...] = jnp.sum(acc[...].reshape(lags, 8, acc.shape[1]), axis=1)


def make_taps(place, damping, frequency, timestep, mix_real, mix_imaginary, lags):
    channels, count = damping.shape
    return call(
        partial(taps_kernel, lags=lags),
        "taps",
        [((lags, channels), F32)],
        (place, damping, frequency, timestep, mix_real, mix_imaginary),
        scratch=[((count, channels), F32)] * 4 + [((lags * 8, channels), F32)],
        micros=TAPS,
    )[0]


def shifted_copies(pad, copies, lead):
    length = copies.shape[1]
    for r in range(8):
        start = 64 + lead - r
        copies[r, :, :] = pad[start : start + length, :]


def linked_blocks(edges, first, step, bound):
    blocks = edges.shape[0] // 2
    mine = edges[first] if step < 0 else edges[blocks + first]

    def more(count):
        there = jnp.clip(first + step * (count + 1), 0, blocks - 1)
        edge = edges[blocks + there] if step < 0 else edges[there]
        return jnp.logical_and(count < bound, edge == mine)

    return lax.while_loop(more, lambda c: c + 1, 0)


def tile(index):
    return at(8 * index, 8)


def fill_ids(place, own, other, own_row, other_row, edges, ids, early):
    length, channels = ids.shape
    tokens = own_row.shape[1]
    valid = place[1] > 0 if early else place[1] == 0
    near = slice(tokens - REACH, tokens) if early else slice(0, REACH)
    halo = jnp.where(valid, other_row[:, near].astype(F32), -1.0)
    mine = own_row[...].astype(F32)
    at_halo, at_own = (0, REACH) if early else (tokens, 0)
    ids[at_halo : at_halo + REACH, :] = jnp.broadcast_to(halo, (channels, REACH)).T
    ids[at_own : at_own + tokens, :] = jnp.broadcast_to(mine, (channels, tokens)).T
    blocks = length // 64
    for b in range(blocks):
        for edge, offset in ((0, 0), (blocks, 63)):
            position = 64 * b + offset
            if at_own <= position < at_own + tokens:
                edges[edge + b] = own[0, position - at_own]
            else:
                value = other[0, position - at_halo + near.start]
                edges[edge + b] = jnp.where(valid, value, -1)


def fill_taps(place, pad, mine_ref, other_ref, flip):
    mine, other = mine_ref[...], other_ref[...]
    first = jnp.where(place[1] == 0, mine, other)
    second = jnp.where(place[1] == 0, other, mine)
    half = mine.shape[0]
    pad[...] = jnp.zeros_like(pad)
    if not flip:
        pad[64 : 64 + half, :] = first
        pad[64 + half : 64 + 2 * half, :] = second
        return
    end = 64 + 2 * half
    for l in range(half):
        pad[end - 1 - l : end - l, :] = first[l : l + 1]
        pad[end - half - 1 - l : end - half - l, :] = second[l : l + 1]


def fill_rows(whole, pieces):
    start = 0
    for piece in pieces:
        whole[start : start + piece.shape[0], :] = piece[...]
        start += piece.shape[0]


def forward_kernel(
    place, own, other, own_row, other_row, k0_ref, k1_ref, halo_ref, lo_ref, hi_ref, y_ref,
    edges, pad, copies, kept, u_s, s_ref,
):
    channels = lo_ref.shape[1]
    blocks = u_s.shape[0] // 64
    ahead = REACH // 64
    fill_ids(place, own, other, own_row, other_row, edges, s_ref, True)
    fill_taps(place, pad, k0_ref, k1_ref, False)
    shifted_copies(pad, copies, 0)
    fill_rows(u_s, (halo_ref, lo_ref, hi_ref))
    for b in range(blocks):
        rows = slice(64 * b, 64 * b + 64)
        edge = edges[blocks + b].astype(F32)
        kept[rows, :] = jnp.where(s_ref[rows, :] == edge, u_s[rows, :], 0.0)

    def block(i, carry):
        mine = i + ahead
        zero = jnp.zeros((8, channels), F32)
        reach = linked_blocks(edges, mine, -1, ahead)

        def far(d, sums):
            sums = list(sums)
            start = pl.multiple_of(64 * (mine - 1 - d), 64)
            for r in range(8):
                taps = [copies[r, tile(8 * (d + 1) + m), :] for m in range(-7, 8)]
                for q in range(8):
                    u = kept[pl.ds(start + 8 * q + r, 1), :]
                    for t in range(8):
                        sums[t] += taps[t - q + 7] * u
            return tuple(sums)

        sums = lax.fori_loop(0, reach, far, (zero,) * 8)
        base = pl.multiple_of(64 * mine, 64)
        ids = [s_ref[pl.ds(base + 8 * t, 8), :] for t in range(8)]
        first = edges[mine].astype(F32)
        sums = [jnp.where(ids[t] == first, sums[t], 0.0) for t in range(8)]
        for r in range(8):
            taps = [copies[r, 8 * m : 8 * m + 8, :] for m in range(8)]
            for q in range(8):
                u = u_s[pl.ds(base + 8 * q + r, 1), :]
                own = s_ref[pl.ds(base + 8 * q + r, 1), :]
                for t in range(q, 8):
                    sums[t] += jnp.where(ids[t] == own, taps[t - q], 0.0) * u
        for t in range(0, 8, 2):
            both = jnp.concatenate([sums[t], sums[t + 1]], 0)
            y_ref[at(64 * i + 8 * t, 16), :] = both.astype(y_ref.dtype)
        return carry

    lax.fori_loop(0, blocks - ahead, block, 0)


def forward_mix(place, ids, taps, halo, low, high):
    channels = low.shape[1]
    length = halo.shape[0] + low.shape[0] + high.shape[0]
    return call(
        forward_kernel,
        "forward_mix",
        [((length - REACH, channels), BF16)],
        (place, *ids, *ids, *taps, halo, low, high),
        scalars=3,
        scratch=[
            pltpu.SMEM((2 * length // 64,), jnp.int32),
            ((64 + REACH + 128, channels), F32),
            ((8, 64 + REACH, channels), F32),
            ((length, channels), F32),
            ((length, channels), F32),
            ((length, channels), F32),
        ],
        micros=5,
    )[0]


def backward_kernel(
    place, own, other, own_row, other_row, k0_ref, k1_ref, lo_ref, hi_ref, halo_ref, slope_ref,
    part_ref, w_ref, low_ref, sum_ref, own_ref, *rest,
):
    *sends, edges, pad, copies, alive, g_s, s_ref = rest
    channels = lo_ref.shape[1]
    blocks = g_s.shape[0] // 64
    ahead = REACH // 64
    fill_ids(place, own, other, own_row, other_row, edges, s_ref, False)
    fill_taps(place, pad, k0_ref, k1_ref, True)
    shifted_copies(pad, copies, -57)
    fill_rows(g_s, (lo_ref, hi_ref, halo_ref))
    for b in range(blocks):
        rows = slice(64 * b, 64 * b + 64)
        edge = edges[b].astype(F32)
        alive[rows, :] = jnp.where(s_ref[rows, :] == edge, g_s[rows, :], 0.0)

    def block(j, total):
        zero = jnp.zeros((8, channels), F32)
        reach = linked_blocks(edges, j, 1, ahead)

        def far(d, sums):
            sums = list(sums)
            start = pl.multiple_of(64 * (j + 1 + d), 64)
            for r in range(8):
                taps = [copies[r, tile(39 - (8 * (d + 1) + m)), :] for m in range(-7, 8)]
                for q in range(8):
                    g = alive[pl.ds(start + 8 * q + r, 1), :]
                    for t in range(8):
                        sums[t] += taps[q - t + 7] * g
            return tuple(sums)

        sums = lax.fori_loop(0, reach, far, (zero,) * 8)
        base = pl.multiple_of(64 * j, 64)
        ids = [s_ref[pl.ds(base + 8 * t, 8), :] for t in range(8)]
        last = edges[blocks + j].astype(F32)
        sums = [jnp.where(ids[t] == last, sums[t], 0.0) for t in range(8)]
        for r in range(8):
            taps = [copies[r, 8 * (39 - m) : 8 * (39 - m) + 8, :] for m in range(8)]
            for q in range(8):
                g = g_s[pl.ds(base + 8 * q + r, 1), :]
                own = s_ref[pl.ds(base + 8 * q + r, 1), :]
                for t in range(q + 1):
                    sums[t] += jnp.where(ids[t] == own, taps[q - t], 0.0) * g
        for t in range(0, 8, 2):
            rows = at(64 * j + 8 * t, 16)
            both = jnp.concatenate([sums[t], sums[t + 1]], 0) * slope_ref[rows, :]
            low_ref[rows, :] = both.astype(low_ref.dtype)
            total = total + both
        return total

    total = lax.fori_loop(0, blocks - ahead, block, jnp.zeros((16, channels), F32))
    sum_ref[...] = jnp.sum(total, axis=0, keepdims=True)
    size = len(sends) + 1
    height = own_ref.shape[0]
    for k in range(size):
        rows = at(height * toward(place, k, size), height)
        piece = part_ref[rows, :] + dot_t(low_ref[rows, :], w_ref[...])
        if k == 0:
            own_ref[...] = piece
        else:
            sends[k - 1][...] = piece.astype(BF16)


def backward_mix(place, ids, taps, low, high, halo, slope, part, weight, size):
    channels = low.shape[1]
    length = halo.shape[0] + low.shape[0] + high.shape[0]
    piece = (part.shape[0] // size, part.shape[1])
    return call(
        backward_kernel,
        "backward_mix",
        [(slope.shape, BF16), ((1, channels), F32), (piece, F32)] + [(piece, BF16)] * (size - 1),
        (place, *ids, *ids, *taps, low, high, halo, slope, part, weight),
        scalars=3,
        scratch=[
            pltpu.SMEM((2 * length // 64,), jnp.int32),
            ((64 + REACH + 128, channels), F32),
            ((8, 64 + REACH, channels), F32),
            ((length, channels), F32),
            ((length, channels), F32),
            ((length, channels), F32),
        ],
        micros=6,
    )


def put_row(out_ref, start, row):
    width = out_ref.shape[1]
    for i in range(row.shape[1] // width):
        out_ref[start + i : start + i + 1, :] = row[:, width * i : width * (i + 1)]
    return start + row.shape[1] // width


def taps_back_kernel(
    place, own_id, other_id, own_row, other_row, halo_ref, ulo_ref, uhi_ref, lo_ref, hi_ref,
    out_ref, edges, kept, u_s, g_s, s_ref, sums,
):
    channels = ulo_ref.shape[1]
    blocks = u_s.shape[0] // 64
    ahead = REACH // 64
    fill_ids(place, own_id, other_id, own_row, other_row, edges, s_ref, True)
    fill_rows(u_s, (halo_ref, ulo_ref, uhi_ref))
    fill_rows(g_s, (lo_ref, hi_ref))
    sums[...] = jnp.zeros_like(sums)
    for b in range(blocks):
        rows = slice(64 * b, 64 * b + 64)
        edge = edges[blocks + b].astype(F32)
        kept[rows, :] = jnp.where(s_ref[rows, :] == edge, u_s[rows, :], 0.0)

    def block(i, carry):
        mine = i + ahead
        reach = linked_blocks(edges, mine, -1, ahead)
        base = pl.multiple_of(64 * mine, 64)
        back = pl.multiple_of(64 * i, 64)
        ids = [s_ref[pl.ds(base + 8 * t, 8), :] for t in range(8)]
        whole = [g_s[pl.ds(back + 8 * t, 8), :] for t in range(8)]
        first = edges[mine].astype(F32)
        alive = [jnp.where(ids[t] == first, whole[t], 0.0) for t in range(8)]

        def far(d, carried):
            start = pl.multiple_of(64 * (mine - 1 - d), 64)
            for r in range(8):
                found = [None] * 15
                for q in range(8):
                    u = kept[pl.ds(start + 8 * q + r, 1), :]
                    for t in range(8):
                        term = carried[t] * u
                        m = t - q + 7
                        found[m] = term if found[m] is None else found[m] + term
                for m in range(-7, 8):
                    sums[r, tile(8 * (d + 1) + m), :] += found[m + 7]
            return carried

        lax.fori_loop(0, reach, far, tuple(alive))
        for r in range(8):
            found = [None] * 8
            for q in range(8):
                u = u_s[pl.ds(base + 8 * q + r, 1), :]
                own = s_ref[pl.ds(base + 8 * q + r, 1), :]
                for t in range(q, 8):
                    term = jnp.where(ids[t] == own, whole[t], 0.0) * u
                    m = t - q
                    found[m] = term if found[m] is None else found[m] + term
            for m in range(8):
                sums[r, 8 * m : 8 * m + 8, :] += found[m]
        return carry

    lax.fori_loop(0, blocks - ahead, block, 0)
    total = sums[0, 0:REACH, :]
    for r in range(1, 8):
        total = total + sums[r, r : r + REACH, :]
    out_ref[...] = total


def gain_kernel(place, taps_ref, x_ref, own_ref, *rest, vectors):
    out_ref = rest[-1]
    sends = rest[: -1 - vectors]
    start = taps_ref.shape[0]
    out_ref[0:start, :] = taps_ref[...]
    for ref in rest[-1 - vectors : -1]:
        start = put_row(out_ref, start, ref[...])
    size = len(sends) + 1
    height = own_ref.shape[0]
    gain = jnp.zeros((8, x_ref.shape[1]), F32)
    bias = gain
    step = min(64, height)
    for k in range(size):
        source = own_ref if k == 0 else sends[k - 1]

        def rows_step(i, state, source=source, k=k):
            gain, bias = state
            unit = x_ref[at(height * toward(place, k, size) + step * i, step), :].astype(F32)
            part = source[at(step * i, step), :].astype(F32)
            scaled = part * unit
            for j in range(0, step, 8):
                gain = gain + scaled[j : j + 8]
                bias = bias + part[j : j + 8]
            return gain, bias

        gain, bias = lax.fori_loop(0, height // step, rows_step, (gain, bias))
    start = put_row(out_ref, start, jnp.sum(gain, axis=0, keepdims=True))
    put_row(out_ref, start, jnp.sum(bias, axis=0, keepdims=True))


def gain_sums(place, taps, rows, own, sends, vectors):
    count, channels = taps.shape
    count += (sum(v.shape[1] for v in vectors) + 2 * rows.shape[1]) // channels
    return call(
        partial(gain_kernel, vectors=len(vectors)),
        "gain",
        [((count, channels), F32)],
        (place, taps, rows, own, *sends, *vectors),
        micros=2,
    )[0]


def taps_back(place, ids, halo, u_low, u_high, low, high, ties):
    channels = low.shape[1]
    length = halo.shape[0] + low.shape[0] + high.shape[0]
    return call(
        taps_back_kernel,
        "taps_back",
        [((REACH, channels), F32)],
        (place, *ids, *ids, halo, u_low, u_high, low, high),
        scalars=3,
        ties=ties,
        scratch=[
            pltpu.SMEM((2 * length // 64,), jnp.int32),
            ((length, channels), F32),
            ((length, channels), F32),
            ((length - REACH, channels), F32),
            ((length, channels), F32),
            ((8, 64 + REACH, channels), F32),
        ],
        micros=TAPS_BACK,
    )[0]


def modes_back_kernel(
    place, c_ref, d_ref, f_ref, t_ref, mr_ref, mi_ref, out_ref,
    ar_s, ai_s, gr_s, gi_s, hr_s, hi_s, wide, wide_l,
):
    channels = c_ref.shape[1]
    count = ar_s.shape[0]
    half = at(count * place[1], count)
    damping, frequency, timestep = d_ref[:, half].T, f_ref[:, half].T, t_ref[...][None, :]
    ar, ai = modes(damping, frequency, timestep)
    ar_s[...] = ar
    ai_s[...] = ai
    for l in range(REACH):
        row = jnp.broadcast_to(c_ref[l : l + 1, :], (8, channels))
        wide[8 * l : 8 * l + 8, :] = row
        wide_l[8 * l : 8 * l + 8, :] = row * float(l)

    def one(p, carry):
        rows = at(8 * p, 8)
        a = (ar_s[rows, :], ai_s[rows, :])
        base = low_powers(*a, 16)
        jump = cmul(*base[8], *base[8])
        zero = jnp.zeros((8, channels), F32)

        def outer(o, state):
            pr, pi, gr, gi, hr, hi = state
            start = pl.multiple_of(128 * o, 128)
            sr = wide[pl.ds(start, 8), :]
            tr = wide_l[pl.ds(start, 8), :]
            si = zero
            ti = zero
            for j in range(1, 16):
                c = wide[pl.ds(start + 8 * j, 8), :]
                e = wide_l[pl.ds(start + 8 * j, 8), :]
                br, bi = base[j]
                sr += c * br
                si += c * bi
                tr += e * br
                ti += e * bi
            gr += pr * sr - pi * si
            gi += pr * si + pi * sr
            hr += pr * tr - pi * ti
            hi += pr * ti + pi * tr
            pr, pi = cmul(pr, pi, *jump)
            return pr, pi, gr, gi, hr, hi

        one_ = jnp.ones((8, channels), F32)
        _, _, gr, gi, hr, hi = lax.fori_loop(
            0, REACH // 16, outer, (one_, zero, zero, zero, zero, zero), unroll=4
        )
        gr_s[rows, :] = gr
        gi_s[rows, :] = gi
        hr_s[rows, :] = hr
        hi_s[rows, :] = hi
        return carry

    lax.fori_loop(0, ar_s.shape[0] // 8, one, 0)
    gr, gi, hr, hi = gr_s[...], gi_s[...], hr_s[...], hi_s[...]
    mr, mi = mr_ref[:, half].T, mi_ref[:, half].T
    qr, qi = ratios(damping, frequency, ar, ai)
    wr, wi = cmul(mr, mi, qr, qi)
    mixr, mixi = cmul(qr, qi, gr, gi)
    inverse = 1.0 / (damping * damping + frequency * frequency)
    nr, ni = -damping * inverse, -frequency * inverse
    vr, vi = cmul(*cmul(mr, mi, gr, gi), nr, ni)
    xr, xi = cmul(vr, vi, ar, ai)
    zr, zi = cmul(wr, wi, hr, hi)
    xr, xi = xr + zr, xi + zi
    yr, yi = cmul(vr, vi, qr, qi)
    grads = (yr - timestep * xr, yi - timestep * xi, mixr, -mixi)
    for i, grad in enumerate(grads):
        out_ref[channels * i : channels * (i + 1), :] = grad.T
    out_ref[4 * channels :, 0:channels] = jnp.broadcast_to(
        jnp.sum(-damping * xr - frequency * xi, axis=0, keepdims=True), (8, channels)
    )


def modes_back(place, c, damping, frequency, timestep, mix_real, mix_imaginary, ties):
    channels, count = damping.shape
    count = count // 2
    return call(
        modes_back_kernel,
        "modes_back",
        [((4 * channels + 8, count), F32)],
        (place, c, damping, frequency, timestep, mix_real, mix_imaginary),
        scratch=[((count, channels), F32)] * 6 + [((REACH * 8, channels), F32)] * 2,
        micros=MODES_BACK,
        ties=ties,
    )[0]


def unit_rows(x):
    x = x.astype(F32)
    shifted = x - jnp.mean(x, axis=-1, keepdims=True)
    inverse = lax.rsqrt(jnp.mean(shifted * shifted, axis=-1, keepdims=True) + EPSILON)
    return shifted * inverse, inverse


def norm_kernel(x_ref, gain_ref, bias_ref, out_ref, unit_ref):
    def step(i, carry):
        rows = at(128 * i, 128)
        unit, _ = unit_rows(x_ref[rows, :])
        out_ref[rows, :] = (unit * gain_ref[...][None, :] + bias_ref[...][None, :]).astype(BF16)
        unit_ref[rows, :] = unit.astype(BF16)
        return carry

    lax.fori_loop(0, x_ref.shape[0] // 128, step, 0)


def reduce_kernel(place, x_ref, b_ref, *rest, count):
    pieces = rest[:count]
    lo_ref, hi_ref, slope_ref, full_ref = rest[count:]
    depth = pieces[0].shape[0]
    for k in range(count):
        full_ref[at(depth * (place[0] ^ k if count > 1 else 0), depth), :] = pieces[k][...]
    half = lo_ref.shape[0]
    for part, out in enumerate((lo_ref, hi_ref)):
        rows = slice(half * part, half * part + half)
        act, slope = gelu_pair(dot(x_ref[rows, :], full_ref[...]) + b_ref[...][None, :])
        out[...] = act
        slope_ref[rows, :] = slope


def gate_kernel(x_ref, w_ref, b_ref, act_ref, slope_ref):
    def step(i, carry):
        rows = at(128 * i, 128)
        act, slope = gelu_pair(dot(x_ref[rows, :], w_ref[...]) + b_ref[...][None, :])
        act_ref[rows, :] = act.astype(BF16)
        slope_ref[rows, :] = slope.astype(BF16)
        return carry

    lax.fori_loop(0, x_ref.shape[0] // 128, step, 0)


def pack_kernel(place, gate_ref, expand_ref, output_ref, mine_ref, rest_ref):
    rows = gate_ref.shape[0]
    some = expand_ref.shape[0] // 2

    def store(first_ref, second_ref):
        first_ref[0:rows, :] = gate_ref[...]
        first_ref[rows:, :] = expand_ref[0:some, :]
        second_ref[0:rows, :] = output_ref[...].T
        second_ref[rows:, :] = expand_ref[some:, :]

    @pl.when(place[1] == 0)
    def _():
        store(mine_ref, rest_ref)

    @pl.when(place[1] != 0)
    def _():
        store(rest_ref, mine_ref)


def stack_kernel(*refs):
    for k, ref in enumerate(refs[:-1]):
        refs[-1][k] = ref[...]


def unpack_kernel(place, mine_ref, rest_ref, near_ref, far_ref, gate_ref, expand_ref, output_ref):
    mines = [mine_ref] + [near_ref.at[k] for k in range(3)]
    rests = [rest_ref] + [far_ref.at[k] for k in range(3)]
    rows = gate_ref.shape[0] // 4
    some = expand_ref.shape[0] // 8

    def store(firsts, seconds):
        for k in range(4):
            s = place[0] ^ k
            gate_ref[at(rows * s, rows), :] = firsts[k][0:rows, :]
            output_ref[at(rows * s, rows), :] = seconds[k][0:rows, :]
            expand_ref[at(2 * some * s, some), :] = firsts[k][rows:, :]
            expand_ref[at(2 * some * s + some, some), :] = seconds[k][rows:, :]

    @pl.when(place[1] == 0)
    def _():
        store(mines, rests)

    @pl.when(place[1] != 0)
    def _():
        store(rests, mines)


def expand_rows(place, k, refs, pieces, size):
    act_ref, slope_ref, we_ref, b_ref, wo_ref = refs
    height = pieces[0].shape[0] // size
    channels = pieces[0].shape[1]
    rows = at(height * toward(place, k, size), height)
    expanded = b_ref[...][None, :]
    for j in range(size):
        source = origin(place, j, size)
        expanded = expanded + dot(pieces[j][rows, :], we_ref[at(channels * source, channels), :])
    coef = (slope_ref[rows, :].astype(F32) * expanded).astype(BF16)
    gated = (expanded * act_ref[rows, :].astype(F32)).astype(BF16)
    half = wo_ref.shape[0] // 2
    return rows, gated, coef, [dot_t(gated, wo_ref[half * h : half * (h + 1), :]) for h in range(2)]


def expand_first_kernel(place, *rest, size):
    refs, pieces, (gated_ref, coef_ref, *sends) = rest[:5], rest[5 : 5 + size], rest[5 + size :]
    _, gated_ref[...], coef_ref[...], parts = expand_rows(place, size - 1, refs, pieces, size)
    for send, part in zip(sends, parts):
        send[...] = part.astype(BF16)


def expand_kernel(place, *rest, size):
    refs, pieces, rest = rest[:5], rest[5 : 5 + size], rest[5 + size :]
    last_gated_ref, last_coef_ref, gated_ref, coef_ref, *rest = rest
    owns, sends = rest[:2], rest[2:]
    for k in range(size - 1):
        rows, gated, coef, parts = expand_rows(place, k, refs, pieces, size)
        gated_ref[rows, :] = gated
        coef_ref[rows, :] = coef
        for h, part in enumerate(parts):
            if k == 0:
                owns[h][...] = part
            else:
                sends[(size - 2) * h + k - 1][...] = part.astype(BF16)
    height = last_gated_ref.shape[0]
    rows = at(height * toward(place, size - 1, size), height)
    gated_ref[rows, :] = last_gated_ref[...]
    coef_ref[rows, :] = last_coef_ref[...]


def halves(x):
    high = x.astype(BF16).astype(F32)
    return high, x - high


def loss_kernel(
    place, x_ref, t_ref, mask_ref, b_ref, act_ref, coef_ref, wo_ref, we_ref, *rest, size
):
    pieces, others, rest = rest[:size], rest[size : 2 * size], rest[2 * size :]
    out_ref, back_ref, keep_ref, low_ref, gate_ref, ob_ref, eb_ref, gb_ref, err_ref, own_ref, *rest = rest
    sends, mask_s = rest[:-1], rest[-1]
    height = pieces[0].shape[0]
    channels = own_ref.shape[1]
    mask_s[...] = jnp.broadcast_to(mask_ref[...].astype(F32), (mask_s.shape[1], mask_s.shape[0])).T
    outb = jnp.zeros_like(ob_ref)
    expb = jnp.zeros_like(eb_ref)
    gatb = jnp.zeros_like(gb_ref)
    errors = jnp.zeros((1, 1), F32)
    for j in range(size):
        rows = at(height * origin(place, j, size), height)
        branch = jnp.concatenate([pieces[j][...], others[j][...]], 1).astype(F32)
        result = x_ref[rows, :].astype(F32) + branch + b_ref[...][None, :]
        out_ref[rows, :] = result.astype(BF16)
        back = (result - t_ref[rows, :].astype(F32)) * mask_s[rows, 0:1]
        low = back.astype(BF16)
        back_ref[rows, :] = low
        if j == 0:
            keep_ref[...] = back
        outb = outb + jnp.sum(back, axis=0, keepdims=True)
        errors = errors + jnp.sum(jnp.sum(back * back, axis=0, keepdims=True), axis=1, keepdims=True)
        gated_back = dot(low, wo_ref[...])
        expanded_back = gated_back * act_ref[rows, :].astype(F32)
        expb = expb + jnp.sum(expanded_back, axis=0, keepdims=True)
        expand_low = expanded_back.astype(BF16)
        low_ref[rows, :] = expand_low
        gate_back = gated_back * coef_ref[rows, :].astype(F32)
        gatb = gatb + jnp.sum(gate_back, axis=0, keepdims=True)
        gate_ref[rows, :] = gate_back.astype(BF16)
        for k in range(size):
            target = toward(place, k, size)
            part = dot_t(expand_low, we_ref[at(channels * target, channels), :])
            if k == 0:
                own_ref[rows, :] = part
            else:
                sends[k - 1][rows, :] = part.astype(BF16)
    ob_ref[...] = outb
    eb_ref[...] = expb
    gb_ref[...] = gatb
    count = jnp.sum(mask_ref[...].astype(F32), axis=1, keepdims=True)
    half = err_ref.shape[1] // 4
    high, low = halves(
        jnp.concatenate([jnp.broadcast_to(errors, (1, half)), jnp.broadcast_to(count, (1, half))], 1)
    )
    err_ref[...] = jnp.concatenate([high, low], 1)


def gate_back_kernel(low_ref, w_ref, out_ref):
    height = 128
    for i in range(low_ref.shape[0] // height):
        rows = slice(height * i, height * (i + 1))
        out_ref[rows, :] = dot_t(low_ref[rows, :], w_ref[...])


def sum_kernel(own_ref, *rest):
    *pieces, lo_ref, hi_ref = rest
    total = own_ref[...]
    for piece in pieces:
        total = total + piece[...].astype(F32)
    half = lo_ref.shape[0]
    lo_ref[...] = total[:half]
    hi_ref[...] = total[half:]


def scale_of(total_ref, scale):
    row, tokens_all = scale
    return tokens_all / (total_ref[row : row + 1, 0:1] + total_ref[row + 2 : row + 3, 0:1])


EXTRA = 16


def rows_kernel(place, x_ref, gain_ref, keep_ref, total_ref, own_ref, *rest, scale, norm_at):
    *pieces, out_ref = rest
    height, features = own_ref.shape
    step = 32
    factor = scale_of(total_ref, scale)
    gain = gain_ref[...][None, :]

    def one(i, carry):
        rows = at(step * i, step)
        total = own_ref[rows, :]
        for piece in pieces:
            total = total + piece[rows, :].astype(F32)
        unit, inverse = unit_rows(x_ref[at(height * place[2] + step * i, step), :])
        scaled = total * gain
        back = inverse * (
            scaled
            - jnp.mean(scaled, axis=-1, keepdims=True)
            - unit * jnp.mean(scaled * unit, axis=-1, keepdims=True)
        )
        out_ref[rows, :] = (factor * (keep_ref[rows, :] + back)).astype(BF16)
        return carry

    lax.fori_loop(0, height // step, one, 0, unroll=2)
    width = total_ref.shape[1]
    count = features // width
    start = norm_at
    both = []
    for v in range(2):
        first = start + count * v
        both.append(
            jnp.concatenate(
                [total_ref[first + i : first + i + 1, :] for i in range(count)], axis=1
            )
        )
    both.append(jnp.zeros((EXTRA - 2, features), F32))
    out_ref[height:, :] = (factor * jnp.concatenate(both, 0)).astype(BF16)


def join_kernel(place, *rest):
    *pieces, out_ref, gain_ref, bias_ref, parts = rest
    size = len(pieces)
    height = pieces[0].shape[0] - EXTRA
    for k in range(size):
        source = origin(place, k, size)
        out_ref[at(height * source, height), :] = pieces[k][0:height, :]
        parts[source] = pieces[k][height:, :].astype(F32)
    total = parts[0]
    for k in range(1, size):
        total = total + parts[k]
    gain_ref[...] = total[0:1]
    bias_ref[...] = total[1:2]


def finish_kernel(place, sum_ref, mine_ref, other_ref, *outs, starts, scale):
    dd_ref, df_ref, dmr_ref, dmi_ref, dt_ref, loss_ref, *vectors = outs
    channels, count = dd_ref.shape
    count = count // 2
    row, tokens_all, features = scale
    errors = sum_ref[row - 1 : row, 0:1] + sum_ref[row + 1 : row + 2, 0:1]
    scale = scale_of(sum_ref, (row, tokens_all))
    loss_ref[...] = errors * scale * (1.0 / (tokens_all * features))
    for i, out in enumerate((dd_ref, df_ref, dmr_ref, dmi_ref)):
        rows = slice(channels * i, channels * (i + 1))
        out[:, at(count * place[1], count)] = mine_ref[rows, :] * scale
        out[:, at(count * (1 - place[1]), count)] = other_ref[rows, :] * scale
    row = slice(4 * channels, 4 * channels + 1)
    dt_ref[...] = (mine_ref[row, 0:channels] + other_ref[row, 0:channels]) * scale
    width = sum_ref.shape[1]
    for out, start in zip(vectors, starts):
        for i in range(out.shape[1] // width):
            out[:, width * i : width * (i + 1)] = sum_ref[start + i : start + i + 1, :] * scale


def early_kernel(place, gated_ref, back_ref, low_ref, *rest, size):
    pieces, (keep_ref, give_ref, mixed_s) = rest[:size], rest[size:]
    core = place[1]
    channels = pieces[0].shape[1]
    for j in range(size):
        source = origin(place, j, size)
        mixed_s[:, at(channels * source, channels)] = pieces[j][...]
    half = back_ref.shape[1] // 8
    some = mixed_s.shape[1] // 8
    for s in range(4):
        k = s
        keep_ref[k, 0:half, :] = t_dot(back_ref[:, at((2 * s + core) * half, half)], gated_ref[...])
        give_ref[k, 0:half, :] = t_dot(
            back_ref[:, at((2 * s + 1 - core) * half, half)], gated_ref[...]
        ).astype(BF16)
        both = t_dot(mixed_s[:, at(2 * some * s, 2 * some)], low_ref[...])
        keep_ref[k, half:, :] = jnp.where(core == 0, both[:some], both[some:])
        give_ref[k, half:, :] = jnp.where(core == 0, both[some:], both[:some]).astype(BF16)


PACK_ROWS = 80


def late_kernel(place, x_ref, gate_ref, reduce_ref, pack_ref, keep_ref, give_ref, pack_s):
    core = place[1]
    half = x_ref.shape[1] // 8
    units = gate_ref.shape[1]
    for s in range(4):
        lines = slice(half * s, half * (s + 1))
        mine = x_ref[:, at((2 * s + core) * half, half)]
        keep_ref[lines, 0:units] = t_dot(mine, gate_ref[...])
        keep_ref[lines, units:] = t_dot(mine, reduce_ref[...])
        other = x_ref[:, at((2 * s + 1 - core) * half, half)]
        give_ref[lines, 0:units] = t_dot(other, gate_ref[...]).astype(BF16)
        give_ref[lines, units:] = t_dot(other, reduce_ref[...]).astype(BF16)
    pack_s[...] = jnp.zeros_like(pack_s)
    sums = pack_ref.shape[0]
    high, low = halves(pack_ref[0:REACH, :])
    pack_s[0:REACH, :] = high
    pack_s[REACH:sums, :] = pack_ref[REACH:, :]
    pack_s[sums : sums + REACH, :] = low
    width = pack_s.shape[1]
    for b in range(pack_s.shape[0] // PACK_ROWS):
        part = pack_s[PACK_ROWS * b : PACK_ROWS * (b + 1), :].astype(BF16)
        lanes = slice(width * b, width * (b + 1))
        give_ref[4 * half :, lanes] = part
        keep_ref[4 * half :, lanes] = part.astype(F32)


def pack_of(sums, pack_ref):
    width = pack_ref.shape[1]
    for b in range(pack_ref.shape[0] // PACK_ROWS):
        pack_ref[PACK_ROWS * b : PACK_ROWS * (b + 1), :] = sums[:, width * b : width * (b + 1)]


def late_pair_kernel(place, keep_ref, got_ref, own_ref, mine_ref, *rest, error_at, sums):
    *sends, pack_s = rest
    s = place[0]
    half = own_ref.shape[0]
    lines = at(half * s, half)
    own_ref[...] = keep_ref[lines, :] + got_ref[lines, :].astype(F32)
    pack_of(keep_ref[4 * half :, :] + got_ref[4 * half :, :].astype(F32), pack_s)
    high, low = halves(pack_s[error_at : error_at + 2, :] + pack_s[error_at + 2 : error_at + 4, :])
    pack_s[error_at : error_at + 2, :] = high
    pack_s[error_at + 2 : error_at + 4, :] = low
    high, low = halves(pack_s[0:REACH, :] + pack_s[sums : sums + REACH, :])
    pack_s[0:REACH, :] = high
    pack_s[sums : sums + REACH, :] = low
    width = pack_s.shape[1]
    for b in range(pack_s.shape[0] // PACK_ROWS):
        part = pack_s[PACK_ROWS * b : PACK_ROWS * (b + 1), :].astype(BF16)
        mine_ref[:, width * b : width * (b + 1)] = part
    for k in (1, 2, 3):
        lines = at(half * (s ^ k), half)
        sends[k - 1][0:half, :] = (keep_ref[lines, :] + got_ref[lines, :].astype(F32)).astype(BF16)
        sends[k - 1][half:, :] = mine_ref[...]


def late_sum_kernel(own_ref, mine_ref, first_ref, second_ref, third_ref, out_ref, total_ref, *, sums):
    half = own_ref.shape[0]
    first, second, third = (ref[...].astype(F32) for ref in (first_ref, second_ref, third_ref))
    out_ref[...] = (own_ref[...] + first[:half]) + (second[:half] + third[:half])
    pack_of(
        (mine_ref[...].astype(F32) + first[half:]) + (second[half:] + third[half:]), total_ref
    )
    total_ref[0:REACH, :] += total_ref[sums : sums + REACH, :]


def pair_kernel(place, keep_ref, got_ref, own_ref, *sends):
    s = place[0]
    own_ref[...] = keep_ref[s] + got_ref[s].astype(F32)
    for k in (1, 2, 3):
        sends[k - 1][...] = (keep_ref[s ^ k] + got_ref[s ^ k].astype(F32)).astype(BF16)


def early_out_kernel(place, own_ref, other_ref, total_ref, output_ref, expand_ref, *, scale):
    scale = scale_of(total_ref, scale)
    mine, other = own_ref[...].astype(F32) * scale, other_ref[...].astype(F32) * scale
    first = jnp.where(place[1] == 0, mine, other)
    second = jnp.where(place[1] == 0, other, mine)
    half = output_ref.shape[1] // 2
    some = expand_ref.shape[0] // 2
    output_ref[...] = jnp.concatenate([first[:half], second[:half]], 0).T
    expand_ref[0:some, :] = first[half:]
    expand_ref[some:, :] = second[half:]


def late_out_kernel(place, own_ref, other_ref, total_ref, gate_ref, reduce_ref, *, scale):
    scale = scale_of(total_ref, scale)
    mine, other = own_ref[...].astype(F32) * scale, other_ref[...].astype(F32) * scale
    first = jnp.where(place[1] == 0, mine, other)
    second = jnp.where(place[1] == 0, other, mine)
    half = gate_ref.shape[0] // 2
    units = gate_ref.shape[1]
    gate_ref[0:half, :] = first[:, :units]
    gate_ref[half:, :] = second[:, :units]
    reduce_ref[0:half, :] = first[:, units:]
    reduce_ref[half:, :] = second[:, units:]


def send_late(place, keep, give, channels, error_at, sums, ties):
    half = (keep.shape[0] - PACK_ROWS) // 4
    shape = (half, keep.shape[1])
    sent = (half + PACK_ROWS, keep.shape[1])
    pack = (PACK_ROWS * (keep.shape[1] // channels), channels)
    own, mine, *sends = call(
        partial(late_pair_kernel, error_at=error_at, sums=sums),
        "pair_late",
        [(shape, F32), ((PACK_ROWS, keep.shape[1]), BF16)] + [(sent, BF16)] * 3,
        (place, keep, swap_context(give)),
        scratch=[(pack, F32)],
        micros=PAIR,
        ties=ties,
    )
    got = [lax.ppermute(sends[k - 1], "shard", xor_pairs(4, k)) for k in (1, 2, 3)]
    own, total = call(
        partial(late_sum_kernel, sums=sums), "late_sum", [(shape, F32), (pack, F32)], (own, mine, *got), scalars=0, micros=1
    )
    return own, swap_context(own), total


def plain_grad(grad, scale, axis):
    paired = lax.psum(grad.astype(BF16), "context").astype(F32)
    return scale * lax.psum_scatter(paired, "shard", scatter_dimension=axis, tiled=True)


def per_device(
    inputs,
    teacher,
    segment_ids,
    valid_mask,
    norm_gain,
    norm_bias,
    gate_weight,
    gate_bias,
    reduce_weight,
    reduce_bias,
    damping,
    frequency,
    timestep,
    mix_real,
    mix_imaginary,
    expand_weight,
    expand_bias,
    output_weight,
    output_bias,
):
    tokens, width = inputs.shape
    channels = reduce_bias.shape[0]
    units = gate_bias.shape[0]
    size = lax.axis_size("tensor")
    shards = lax.axis_size("shard")
    contexts = lax.axis_size("context")
    core = lax.axis_index("context")
    shard = lax.axis_index("shard")
    tensor = lax.axis_index("tensor")
    fast = shards == 4 and contexts == 2 and size == 4
    height = tokens // size
    place = jnp.stack([shard, core, tensor]).astype(jnp.int32)

    ids = (segment_ids, swap_context(segment_ids))
    if fast:
        found = [lax.ppermute(reduce_weight, "shard", xor_pairs(4, k)) for k in (1, 2, 3)]
        reduce_pieces = [reduce_weight] + found
    else:
        reduce_pieces = [lax.all_gather(reduce_weight, "shard", axis=0, tiled=True)]
        gate_full = lax.all_gather(gate_weight, "shard", axis=0, tiled=True)
        expand_full = lax.all_gather(expand_weight, "shard", axis=0, tiled=True)
        output_full = lax.all_gather(output_weight.T, "shard", axis=0, tiled=True)

    normed, unit = call(
        norm_kernel,
        "norm",
        [(inputs.shape, BF16)] * 2,
        (inputs, norm_gain, norm_bias),
        scalars=0,
    )
    mode_args = (damping, frequency, timestep, mix_real, mix_imaginary)
    taps_mine = make_taps(place, *mode_args, REACH // 2)
    taps = (taps_mine, swap_context(taps_mine))
    half_rows = (tokens // 2, channels)
    u_low, u_high, reduce_slope, reduce_full = call(
        partial(reduce_kernel, count=len(reduce_pieces)),
        "reduce",
        [(half_rows, F32), (half_rows, F32), ((tokens, channels), F32), ((width, channels), BF16)],
        (place, normed, reduce_bias, *reduce_pieces),
    )
    if fast:
        some = expand_weight.shape[0] // 2
        shape = (gate_weight.shape[0] + some, units)
        mine, rest = call(
            pack_kernel, "pack", [(shape, BF16)] * 2, (place, gate_weight, expand_weight, output_weight),
            ties=(u_high,),
        )
        nears = [lax.ppermute(mine, "shard", xor_pairs(4, k)) for k in (1, 2, 3)]
    before = [(i, i + 1) for i in range(contexts - 1)]
    after = [(i + 1, i) for i in range(contexts - 1)]
    halo = lax.ppermute(u_high[tokens // 2 - REACH :], "context", before)
    mixed_own = forward_mix(place, ids, taps, halo, u_low, u_high)
    mixed = [mixed_own] + exchange_tensor([mixed_own] * (size - 1))
    if fast:
        shape = (3,) + mine.shape
        (near,) = call(stack_kernel, "stack", [(shape, BF16)], nears, scalars=0, ties=(mixed_own,))
        gate_full, expand_full, output_full = call(
            unpack_kernel,
            "unpack",
            [
                ((4 * gate_weight.shape[0], units), BF16),
                ((4 * expand_weight.shape[0], units), BF16),
                ((width, units), BF16),
            ],
            (place, mine, rest, near, swap_context(near)),
            micros=1,
        )
    gate_act, gate_slope = call(
        gate_kernel,
        "gate",
        [((tokens, units), BF16)] * 2,
        (normed, gate_full, gate_bias),
        scalars=0,
        micros=4,
    )
    piece = (height, width)
    half_piece = (height, width // 2)
    expand_args = (gate_act, gate_slope, expand_full, expand_bias, output_full, *mixed)
    last_gated, last_coef, *last_sends = call(
        partial(expand_first_kernel, size=size),
        "expand_first",
        [((height, units), BF16)] * 2 + [(half_piece, BF16)] * 2,
        (place, *expand_args),
        micros=1,
    )
    gated, coef, first_part, second_part, *branch_sends = call(
        partial(expand_kernel, size=size),
        "expand",
        [((tokens, units), BF16)] * 2 + [(half_piece, F32)] * 2 + [(half_piece, BF16)] * (2 * size - 4),
        (place, *expand_args, last_gated, last_coef),
        micros=3,
    )
    count = size - 2
    branch = sum_tensor(
        (first_part, second_part),
        (branch_sends[:count] + last_sends[:1], branch_sends[count:] + last_sends[1:]),
    )

    output, branch_back, keep_back, expand_low, gate_low, *rest = call(
        partial(loss_kernel, size=size),
        "loss",
        [
            (inputs.shape, BF16),
            (inputs.shape, BF16),
            (piece, F32),
            ((tokens, units), BF16),
            ((tokens, units), BF16),
            ((1, width), F32),
            ((1, units), F32),
            ((1, units), F32),
            ((1, 4 * channels), F32),
            ((tokens, channels), F32),
        ]
        + [((tokens, channels), BF16)] * (size - 1),
        (
            place,
            inputs,
            teacher,
            valid_mask,
            output_bias,
            gate_act,
            coef,
            output_full,
            expand_full,
            *branch[0],
            *branch[1],
        ),
        scratch=[((tokens, 128), F32)],
        micros=8,
    )
    output_sum, expand_sum, gate_sum, error_row, back_part, *back_sends = rest
    ties = ()
    if fast:
        shape = (4, (gate_weight.shape[0] + expand_weight.shape[0]) // 2, units)
        early = call(
            partial(early_kernel, size=size),
            "early",
            [(shape, F32), (shape, BF16)],
            (place, gated, branch_back, expand_low, *mixed),
            scratch=[((tokens, size * channels), BF16)],
            micros=EARLY,
        )
        early, *early_sends = call(
            pair_kernel,
            "pair_early",
            [(shape[1:], F32)] + [(shape[1:], BF16)] * 3,
            (place, early[0], swap_context(early[1])),
            micros=PAIR,
        )
        ties = (early,)
        early_got = [
            lax.ppermute(early_sends[k - 1], "shard", xor_pairs(4, k)).astype(F32) for k in (1, 2, 3)
        ]
        early = (early + early_got[0]) + (early_got[1] + early_got[2])
    back_got = exchange_tensor(back_sends)
    (gate_part,) = call(
        gate_back_kernel,
        "gate_back",
        [((tokens, width), F32)],
        (gate_low, gate_full),
        scalars=0,
        micros=1,
    )
    ties = ties + (gate_part,)
    g_low, g_high = call(
        sum_kernel,
        "sum",
        [(half_rows, F32)] * 2,
        (back_part, *back_got),
        scalars=0,
        ties=ties,
    )
    halo_back = lax.ppermute(g_low[:REACH], "context", after)
    reduce_low, reduce_sum, normed_part, *normed_sends = backward_mix(
        place, ids, taps, g_low, g_high, halo_back, reduce_slope, gate_part, reduce_full, size
    )
    normed_got, _ = deliver_tensor(normed_sends)

    vectors = (gate_sum, expand_sum, output_sum, reduce_sum, error_row)
    taps_part = taps_back(
        place, ids, halo, u_low, u_high, g_low, g_high, ()
    )
    pack = gain_sums(place, taps_part, unit, normed_part, normed_sends, vectors)
    norm_at = pack.shape[0] - 2 * width // channels
    error_at = norm_at - 4
    if fast:
        shape = (2 * gate_weight.shape[0] + PACK_ROWS, units + channels)
        late = call(
            late_kernel,
            "late",
            [(shape, F32), (shape, BF16)],
            (place, normed, gate_low, reduce_low, pack),
            ties=(early,),
            scratch=[((PACK_ROWS * (shape[1] // channels), channels), F32)],
            micros=LATE,
        )
        *late, total = send_late(place, *late, channels, error_at, pack.shape[0], ())
    else:
        total = sum_over(sum_over(pack, "context"), "shard")
    tokens_all = float(tokens * shards * contexts)

    scale = (error_at + 1, tokens_all)

    (rows_own,) = call(
        partial(rows_kernel, scale=scale, norm_at=norm_at),
        "rows",
        [((height + EXTRA, width), BF16)],
        (place, inputs, norm_gain, keep_back, total, normed_part, *normed_got),
        micros=3,
    )
    mode_mine = modes_back(place, total, *mode_args, ties=(rows_own,))
    inputs_grad, gain_grad, bias_grad = call(
        join_kernel,
        "join",
        [(inputs.shape, BF16), ((1, width), F32), ((1, width), F32)],
        (place, rows_own, *spread_tensor(rows_own, (mode_mine,))),
        scratch=[((size, EXTRA, width), F32)],
    )
    mode_other = swap_context(mode_mine)

    if fast:
        output_grad, expand_grad = call(
            partial(early_out_kernel, scale=scale),
            "early_out",
            [(output_weight.shape, F32), (expand_weight.shape, F32)],
            (place, early, swap_context(early), total),
        )
        gate_grad, reduce_grad = call(
            partial(late_out_kernel, scale=scale),
            "late_out",
            [(gate_weight.shape, F32), (reduce_weight.shape, F32)],
            (place, *late, total),
        )
    else:
        factor = tokens_all / total[error_at + 1, 0]
        mixed_full = lax.all_gather(mixed_own, "tensor", axis=1, tiled=True)
        output_grad = plain_grad(t_dot(gated, branch_back), factor, 1)
        expand_grad = plain_grad(t_dot(mixed_full, expand_low), factor, 0)
        gate_grad = plain_grad(t_dot(normed, gate_low), factor, 0)
        reduce_grad = plain_grad(t_dot(normed, reduce_low), factor, 0)

    counts = [v.shape[1] // channels for v in vectors]
    offsets = [REACH + sum(counts[:i]) for i in range(4)]
    whole = (damping.shape, F32)
    *mode_grads, timestep_grad, loss_value, gate_bias_grad, expand_bias_grad, output_bias_grad, reduce_bias_grad = call(
        partial(finish_kernel, starts=offsets, scale=scale + (float(width),)),
        "finish",
        [whole] * 4 + [((1, n), F32) for n in (channels, 1, units, units, width, channels)],
        (place, total, mode_mine, mode_other),
    )
    return (
        output,
        loss_value.reshape(()),
        inputs_grad,
        gain_grad[0],
        bias_grad[0],
        gate_grad,
        gate_bias_grad[0],
        reduce_grad,
        reduce_bias_grad[0],
        mode_grads[0],
        mode_grads[1],
        timestep_grad[0],
        mode_grads[2],
        mode_grads[3],
        expand_grad,
        expand_bias_grad[0],
        output_grad,
        output_bias_grad[0],
    )


def solution(mesh):
    tokens = P(("shard", "context"), None)
    ids = P("shard", "context")
    split = P("shard", "tensor")
    rows = P("tensor", None)
    units = P("tensor")
    return jax.shard_map(
        per_device,
        mesh=mesh,
        in_specs=(
            tokens, tokens, ids, ids, P(), P(), split, units, split, units,
            rows, rows, units, rows, rows, split, units, P("tensor", "shard"), P(),
        ),
        out_specs=(
            tokens, P(), tokens, P(), P(), split, units, split, units,
            rows, rows, units, rows, rows, split, units, P("tensor", "shard"), P(),
        ),
        check_vma=False,
    )
```

```python
import math
from functools import partial

import jax
import jax.numpy as jnp
from jax import lax
from jax.experimental import pallas as pl
from jax.experimental.pallas import tpu as pltpu
from jax.sharding import PartitionSpec as P

REACH = 256
EPSILON = 1e-05
EARLY, PAIR, LATE, TAPS_BACK, MODES_BACK, TAPS = 2,1,2,4,4,60
GELU_SCALE = 0.7978845608028654
F32 = jnp.float32
BF16 = jnp.bfloat16
SMEM_SPEC = pl.BlockSpec(memory_space=pltpu.SMEM)
VMEM_SPEC = pl.BlockSpec(memory_space=pltpu.VMEM)


def call(body, name, outs, args, scalars=1, scratch=(), micros=2, ties=()):
    held = [(a.shape, a.dtype) for a in args[scalars:]] + list(outs)
    held += [entry for entry in scratch if isinstance(entry, tuple)]
    room = 0
    for shape, kind in held:
        shape = (8,) * (2 - len(shape)) + tuple(shape)
        room += math.prod(shape[:-2] + (max(shape[-2], 8), max(shape[-1], 128))) * jnp.dtype(kind).itemsize
    count = len(args)

    def kernel(*refs):
        body(*refs[:count], *refs[count + len(ties) :])

    return pl.pallas_call(
        kernel,
        out_shape=[jax.ShapeDtypeStruct(shape, kind) for shape, kind in outs],
        in_specs=[SMEM_SPEC] * scalars
        + [VMEM_SPEC] * (len(args) - scalars)
        + [pl.BlockSpec(memory_space=pl.ANY)] * len(ties),
        out_specs=[VMEM_SPEC] * len(outs),
        scratch_shapes=[
            pltpu.VMEM(*entry) if isinstance(entry, tuple) else entry for entry in scratch
        ],
        compiler_params=pltpu.CompilerParams(vmem_limit_bytes=room + room // 16 + (3 << 20)),
        cost_estimate=pl.CostEstimate(
            flops=int(micros * 0.2e9), bytes_accessed=int(micros * 1e5), transcendentals=0
        ),
        name=name,
    )(*args, *ties)


def dot(a, b):
    return jnp.dot(a, b, preferred_element_type=F32)


def dot_t(a, b):
    return lax.dot_general(a, b, (((1,), (1,)), ((), ())), preferred_element_type=F32)


def t_dot(a, b):
    return lax.dot_general(a, b, (((0,), (0,)), ((), ())), preferred_element_type=F32)


def at(start, size, unit=None):
    return pl.ds(pl.multiple_of(start, unit or size), size)


def gelu_pair(a):
    square = a * a
    bent = jnp.tanh(GELU_SCALE * (a + 0.044715 * (a * square)))
    half = 0.5 * (1.0 + bent)
    slope = half + 0.5 * a * (1.0 - bent * bent) * (GELU_SCALE + 3 * 0.044715 * GELU_SCALE * square)
    return a * half, slope


def xor_pairs(size, mask):
    return [(i, i ^ mask) for i in range(size)]


def shift_pairs(size, step):
    return [(i, (i + step) % size) for i in range(size)]


def swap_context(x):
    return lax.ppermute(x, "context", [(0, 1), (1, 0)])


def sum_over(x, axis):
    size = lax.axis_size(axis)
    if size == 4:
        first = lax.ppermute(x, axis, xor_pairs(4, 1))
        second = lax.ppermute(x, axis, xor_pairs(4, 2))
        third = lax.ppermute(x, axis, xor_pairs(4, 3))
        return (x + first) + (second + third)
    step = 1
    while step < size:
        x = x + lax.ppermute(x, axis, xor_pairs(size, step))
        step *= 2
    return x


def copy_kernel(x_ref, out_ref):
    out_ref[...] = x_ref[...]


def add_kernel(x_ref, y_ref, z_ref, sum_ref, copy_ref):
    sum_ref[...] = (x_ref[...].astype(F32) + y_ref[...].astype(F32)).astype(BF16)
    copy_ref[...] = z_ref[...]


def toward(place, k, size):
    return place[2] ^ k if size == 4 else lax.rem(place[2] + k, size)


def origin(place, k, size):
    return place[2] ^ k if size == 4 else lax.rem(place[2] + size - k, size)


def tensor_pairs(size, k):
    return xor_pairs(size, k) if size == 4 else shift_pairs(size, k)


def exchange_tensor(pieces):
    size = lax.axis_size("tensor")
    return [lax.ppermute(x, "tensor", tensor_pairs(size, k + 1)) for k, x in enumerate(pieces)]


def stage_kernel(x_ref, y_ref, z_ref, w_ref, sum_ref, copy_ref, next_ref):
    sum_ref[...] = (x_ref[...].astype(F32) + y_ref[...].astype(F32)).astype(BF16)
    copy_ref[...] = z_ref[...]
    next_ref[...] = w_ref[...]


def sum_tensor(owns, sends):
    size = lax.axis_size("tensor")
    if size != 4:
        found = []
        for own, pieces in zip(owns, sends):
            for got in exchange_tensor(pieces):
                own = own + got.astype(F32)
            own = own.astype(BF16)
            found.append([own] + exchange_tensor([own] * (size - 1)))
        return found
    near_pairs, far_pairs = xor_pairs(4, 1), xor_pairs(4, 2)

    def stage(pieces, passed, after):
        return call(
            stage_kernel,
            "stage",
            [(passed.shape, BF16)] * 3,
            (pieces[1], passed, pieces[0], after),
            scalars=0,
            micros=0.5,
        )

    first, second = sends
    passed = lax.ppermute(first[2], "tensor", near_pairs)
    joined, near, after = stage(first, passed, second[2])
    first_far = lax.ppermute(joined, "tensor", far_pairs)
    passed = lax.ppermute(after, "tensor", near_pairs)
    first_near = lax.ppermute(near, "tensor", near_pairs)
    joined, near, _ = stage(second, passed, second[0])
    second_far = lax.ppermute(joined, "tensor", far_pairs)
    second_near = lax.ppermute(near, "tensor", near_pairs)
    found = []
    for own, far, near in ((owns[0], first_far, first_near), (owns[1], second_far, second_near)):
        total = (own + (far.astype(F32) + near.astype(F32))).astype(BF16)
        away = lax.ppermute(total, "tensor", far_pairs)
        beside = lax.ppermute(total, "tensor", near_pairs)
        found.append([total, beside, away, lax.ppermute(away, "tensor", near_pairs)])
    return found


def spread_tensor(x, ties=()):
    size = lax.axis_size("tensor")
    if size == 4:
        near = lax.ppermute(x, "tensor", xor_pairs(4, 1))
        far = lax.ppermute(x, "tensor", xor_pairs(4, 2))
        (again,) = call(
            copy_kernel,
            "again",
            [(x.shape, x.dtype)],
            (far,),
            scalars=0,
            micros=0.5,
            ties=(near,) + ties,
        )
        return [near, far, lax.ppermute(again, "tensor", xor_pairs(4, 1))]
    return [lax.ppermute(x, "tensor", shift_pairs(size, k)) for k in range(1, size)]


def deliver_tensor(pieces):
    size = lax.axis_size("tensor")
    if size == 4:
        passed = lax.ppermute(pieces[2], "tensor", xor_pairs(4, 1))
        joined, near = call(
            add_kernel,
            "joined",
            [(passed.shape, BF16)] * 2,
            (pieces[1], passed, pieces[0]),
            scalars=0,
            micros=0.5,
        )
        found = [
            lax.ppermute(near, "tensor", xor_pairs(4, 1)),
            lax.ppermute(joined, "tensor", xor_pairs(4, 2)),
        ]
        return found, joined
    found = [lax.ppermute(x, "tensor", shift_pairs(size, k + 1)) for k, x in enumerate(pieces)]
    return found, found[0]


def cmul(ar, ai, br, bi):
    return ar * br - ai * bi, ar * bi + ai * br


def modes(damping, frequency, timestep):
    magnitude = jnp.exp(-timestep * damping)
    angle = timestep * frequency
    return magnitude * jnp.cos(angle), magnitude * jnp.sin(angle)


def ratios(damping, frequency, ar, ai):
    minus = ar - 1.0
    inverse = 1.0 / (damping * damping + frequency * frequency)
    return (ai * frequency - minus * damping) * inverse, -(
        minus * frequency + ai * damping
    ) * inverse


def low_powers(ar, ai, count):
    found = [None, (ar, ai)]
    for j in range(2, count):
        found.append(cmul(*found[j // 2], *found[j - j // 2]))
    return found


def taps_kernel(place, d_ref, f_ref, t_ref, mr_ref, mi_ref, k_ref, ar_s, ai_s, wr_s, wi_s, acc, lags):
    damping, frequency, timestep = d_ref[...].T, f_ref[...].T, t_ref[...][None, :]
    ar, ai = modes(damping, frequency, timestep)
    qr, qi = ratios(damping, frequency, ar, ai)
    mr, mi = mr_ref[...].T, mi_ref[...].T
    wr, wi = mr * qr - mi * qi, mr * qi + mi * qr
    ar_s[...] = ar
    ai_s[...] = ai
    if lags < REACH:
        power = (ar, ai)
        for _ in range(lags.bit_length() - 1):
            power = cmul(*power, *power)
        later = place[1] > 0
        vr, vi = cmul(wr, wi, *power)
        wr, wi = jnp.where(later, vr, wr), jnp.where(later, vi, wi)
    wr_s[...] = wr
    wi_s[...] = wi
    acc[...] = jnp.zeros_like(acc)

    def pair(p, carry):
        rows = at(16 * p, 16)
        a = (ar_s[rows, :], ai_s[rows, :])
        base = low_powers(*a, 8)
        eight = cmul(*base[4], *base[4])

        def outer(o, w):
            wr, wi = w
            start = pl.multiple_of(64 * o, 64)
            for j in range(8):
                term = wr if j == 0 else wr * base[j][0] - wi * base[j][1]
                acc[pl.ds(start + 8 * j, 8), :] += term[:8] + term[8:]
            return cmul(wr, wi, *eight)

        lax.fori_loop(0, lags // 8, outer, (wr_s[rows, :], wi_s[rows, :]), unroll=4)
        return carry

    lax.fori_loop(0, ar_s.shape[0] // 16, pair, 0)
    k_ref[...] = jnp.sum(acc[...].reshape(lags, 8, acc.shape[1]), axis=1)


def make_taps(place, damping, frequency, timestep, mix_real, mix_imaginary, lags):
    channels, count = damping.shape
    return call(
        partial(taps_kernel, lags=lags),
        "taps",
        [((lags, channels), F32)],
        (place, damping, frequency, timestep, mix_real, mix_imaginary),
        scratch=[((count, channels), F32)] * 4 + [((lags * 8, channels), F32)],
        micros=TAPS,
    )[0]


def shifted_copies(pad, copies, lead):
    length = copies.shape[1]
    for r in range(8):
        start = 64 + lead - r
        copies[r, :, :] = pad[start : start + length, :]


def linked_blocks(edges, first, step, bound):
    blocks = edges.shape[0] // 2
    mine = edges[first] if step < 0 else edges[blocks + first]

    def more(count):
        there = jnp.clip(first + step * (count + 1), 0, blocks - 1)
        edge = edges[blocks + there] if step < 0 else edges[there]
        return jnp.logical_and(count < bound, edge == mine)

    return lax.while_loop(more, lambda c: c + 1, 0)


def tile(index):
    return at(8 * index, 8)


def fill_ids(place, own, other, own_row, other_row, edges, ids, early):
    length, channels = ids.shape
    tokens = own_row.shape[1]
    valid = place[1] > 0 if early else place[1] == 0
    near = slice(tokens - REACH, tokens) if early else slice(0, REACH)
    halo = jnp.where(valid, other_row[:, near].astype(F32), -1.0)
    mine = own_row[...].astype(F32)
    at_halo, at_own = (0, REACH) if early else (tokens, 0)
    ids[at_halo : at_halo + REACH, :] = jnp.broadcast_to(halo, (channels, REACH)).T
    ids[at_own : at_own + tokens, :] = jnp.broadcast_to(mine, (channels, tokens)).T
    blocks = length // 64
    for b in range(blocks):
        for edge, offset in ((0, 0), (blocks, 63)):
            position = 64 * b + offset
            if at_own <= position < at_own + tokens:
                edges[edge + b] = own[0, position - at_own]
            else:
                value = other[0, position - at_halo + near.start]
                edges[edge + b] = jnp.where(valid, value, -1)


def fill_taps(place, pad, mine_ref, other_ref, flip):
    mine, other = mine_ref[...], other_ref[...]
    first = jnp.where(place[1] == 0, mine, other)
    second = jnp.where(place[1] == 0, other, mine)
    half = mine.shape[0]
    pad[...] = jnp.zeros_like(pad)
    if not flip:
        pad[64 : 64 + half, :] = first
        pad[64 + half : 64 + 2 * half, :] = second
        return
    end = 64 + 2 * half
    for l in range(half):
        pad[end - 1 - l : end - l, :] = first[l : l + 1]
        pad[end - half - 1 - l : end - half - l, :] = second[l : l + 1]


def fill_rows(whole, pieces):
    start = 0
    for piece in pieces:
        whole[start : start + piece.shape[0], :] = piece[...]
        start += piece.shape[0]


def forward_kernel(
    place, own, other, own_row, other_row, k0_ref, k1_ref, halo_ref, lo_ref, hi_ref, y_ref,
    edges, pad, copies, kept, u_s, s_ref,
):
    channels = lo_ref.shape[1]
    blocks = u_s.shape[0] // 64
    ahead = REACH // 64
    fill_ids(place, own, other, own_row, other_row, edges, s_ref, True)
    fill_taps(place, pad, k0_ref, k1_ref, False)
    shifted_copies(pad, copies, 0)
    fill_rows(u_s, (halo_ref, lo_ref, hi_ref))
    for b in range(blocks):
        rows = slice(64 * b, 64 * b + 64)
        edge = edges[blocks + b].astype(F32)
        kept[rows, :] = jnp.where(s_ref[rows, :] == edge, u_s[rows, :], 0.0)

    def block(i, carry):
        mine = i + ahead
        zero = jnp.zeros((8, channels), F32)
        reach = linked_blocks(edges, mine, -1, ahead)

        def far(d, sums):
            sums = list(sums)
            start = pl.multiple_of(64 * (mine - 1 - d), 64)
            for r in range(8):
                taps = [copies[r, tile(8 * (d + 1) + m), :] for m in range(-7, 8)]
                for q in range(8):
                    u = kept[pl.ds(start + 8 * q + r, 1), :]
                    for t in range(8):
                        sums[t] += taps[t - q + 7] * u
            return tuple(sums)

        sums = lax.fori_loop(0, reach, far, (zero,) * 8)
        base = pl.multiple_of(64 * mine, 64)
        ids = [s_ref[pl.ds(base + 8 * t, 8), :] for t in range(8)]
        first = edges[mine].astype(F32)
        sums = [jnp.where(ids[t] == first, sums[t], 0.0) for t in range(8)]
        for r in range(8):
            taps = [copies[r, 8 * m : 8 * m + 8, :] for m in range(8)]
            for q in range(8):
                u = u_s[pl.ds(base + 8 * q + r, 1), :]
                own = s_ref[pl.ds(base + 8 * q + r, 1), :]
                for t in range(q, 8):
                    sums[t] += jnp.where(ids[t] == own, taps[t - q], 0.0) * u
        for t in range(0, 8, 2):
            both = jnp.concatenate([sums[t], sums[t + 1]], 0)
            y_ref[at(64 * i + 8 * t, 16), :] = both.astype(y_ref.dtype)
        return carry

    lax.fori_loop(0, blocks - ahead, block, 0)


def forward_mix(place, ids, taps, halo, low, high):
    channels = low.shape[1]
    length = halo.shape[0] + low.shape[0] + high.shape[0]
    return call(
        forward_kernel,
        "forward_mix",
        [((length - REACH, channels), BF16)],
        (place, *ids, *ids, *taps, halo, low, high),
        scalars=3,
        scratch=[
            pltpu.SMEM((2 * length // 64,), jnp.int32),
            ((64 + REACH + 128, channels), F32),
            ((8, 64 + REACH, channels), F32),
            ((length, channels), F32),
            ((length, channels), F32),
            ((length, channels), F32),
        ],
        micros=5,
    )[0]


def backward_kernel(
    place, own, other, own_row, other_row, k0_ref, k1_ref, lo_ref, hi_ref, halo_ref, slope_ref,
    part_ref, w_ref, low_ref, sum_ref, own_ref, *rest,
):
    *sends, edges, pad, copies, alive, g_s, s_ref = rest
    channels = lo_ref.shape[1]
    blocks = g_s.shape[0] // 64
    ahead = REACH // 64
    fill_ids(place, own, other, own_row, other_row, edges, s_ref, False)
    fill_taps(place, pad, k0_ref, k1_ref, True)
    shifted_copies(pad, copies, -57)
    fill_rows(g_s, (lo_ref, hi_ref, halo_ref))
    for b in range(blocks):
        rows = slice(64 * b, 64 * b + 64)
        edge = edges[b].astype(F32)
        alive[rows, :] = jnp.where(s_ref[rows, :] == edge, g_s[rows, :], 0.0)

    def block(j, total):
        zero = jnp.zeros((8, channels), F32)
        reach = linked_blocks(edges, j, 1, ahead)

        def far(d, sums):
            sums = list(sums)
            start = pl.multiple_of(64 * (j + 1 + d), 64)
            for r in range(8):
                taps = [copies[r, tile(39 - (8 * (d + 1) + m)), :] for m in range(-7, 8)]
                for q in range(8):
                    g = alive[pl.ds(start + 8 * q + r, 1), :]
                    for t in range(8):
                        sums[t] += taps[q - t + 7] * g
            return tuple(sums)

        sums = lax.fori_loop(0, reach, far, (zero,) * 8)
        base = pl.multiple_of(64 * j, 64)
        ids = [s_ref[pl.ds(base + 8 * t, 8), :] for t in range(8)]
        last = edges[blocks + j].astype(F32)
        sums = [jnp.where(ids[t] == last, sums[t], 0.0) for t in range(8)]
        for r in range(8):
            taps = [copies[r, 8 * (39 - m) : 8 * (39 - m) + 8, :] for m in range(8)]
            for q in range(8):
                g = g_s[pl.ds(base + 8 * q + r, 1), :]
                own = s_ref[pl.ds(base + 8 * q + r, 1), :]
                for t in range(q + 1):
                    sums[t] += jnp.where(ids[t] == own, taps[q - t], 0.0) * g
        for t in range(0, 8, 2):
            rows = at(64 * j + 8 * t, 16)
            both = jnp.concatenate([sums[t], sums[t + 1]], 0) * slope_ref[rows, :]
            low_ref[rows, :] = both.astype(low_ref.dtype)
            total = total + both
        return total

    total = lax.fori_loop(0, blocks - ahead, block, jnp.zeros((16, channels), F32))
    sum_ref[...] = jnp.sum(total, axis=0, keepdims=True)
    size = len(sends) + 1
    height = own_ref.shape[0]
    for k in range(size):
        rows = at(height * toward(place, k, size), height)
        piece = part_ref[rows, :] + dot_t(low_ref[rows, :], w_ref[...])
        if k == 0:
            own_ref[...] = piece
        else:
            sends[k - 1][...] = piece.astype(BF16)


def backward_mix(place, ids, taps, low, high, halo, slope, part, weight, size):
    channels = low.shape[1]
    length = halo.shape[0] + low.shape[0] + high.shape[0]
    piece = (part.shape[0] // size, part.shape[1])
    return call(
        backward_kernel,
        "backward_mix",
        [(slope.shape, BF16), ((1, channels), F32), (piece, F32)] + [(piece, BF16)] * (size - 1),
        (place, *ids, *ids, *taps, low, high, halo, slope, part, weight),
        scalars=3,
        scratch=[
            pltpu.SMEM((2 * length // 64,), jnp.int32),
            ((64 + REACH + 128, channels), F32),
            ((8, 64 + REACH, channels), F32),
            ((length, channels), F32),
            ((length, channels), F32),
            ((length, channels), F32),
        ],
        micros=6,
    )


def put_row(out_ref, start, row):
    width = out_ref.shape[1]
    for i in range(row.shape[1] // width):
        out_ref[start + i : start + i + 1, :] = row[:, width * i : width * (i + 1)]
    return start + row.shape[1] // width


def taps_back_kernel(
    place, own_id, other_id, own_row, other_row, halo_ref, ulo_ref, uhi_ref, lo_ref, hi_ref,
    out_ref, edges, kept, u_s, g_s, s_ref, sums,
):
    channels = ulo_ref.shape[1]
    blocks = u_s.shape[0] // 64
    ahead = REACH // 64
    fill_ids(place, own_id, other_id, own_row, other_row, edges, s_ref, True)
    fill_rows(u_s, (halo_ref, ulo_ref, uhi_ref))
    fill_rows(g_s, (lo_ref, hi_ref))
    sums[...] = jnp.zeros_like(sums)
    for b in range(blocks):
        rows = slice(64 * b, 64 * b + 64)
        edge = edges[blocks + b].astype(F32)
        kept[rows, :] = jnp.where(s_ref[rows, :] == edge, u_s[rows, :], 0.0)

    def block(i, carry):
        mine = i + ahead
        reach = linked_blocks(edges, mine, -1, ahead)
        base = pl.multiple_of(64 * mine, 64)
        back = pl.multiple_of(64 * i, 64)
        ids = [s_ref[pl.ds(base + 8 * t, 8), :] for t in range(8)]
        whole = [g_s[pl.ds(back + 8 * t, 8), :] for t in range(8)]
        first = edges[mine].astype(F32)
        alive = [jnp.where(ids[t] == first, whole[t], 0.0) for t in range(8)]

        def far(d, carried):
            start = pl.multiple_of(64 * (mine - 1 - d), 64)
            for r in range(8):
                found = [None] * 15
                for q in range(8):
                    u = kept[pl.ds(start + 8 * q + r, 1), :]
                    for t in range(8):
                        term = carried[t] * u
                        m = t - q + 7
                        found[m] = term if found[m] is None else found[m] + term
                for m in range(-7, 8):
                    sums[r, tile(8 * (d + 1) + m), :] += found[m + 7]
            return carried

        lax.fori_loop(0, reach, far, tuple(alive))
        for r in range(8):
            found = [None] * 8
            for q in range(8):
                u = u_s[pl.ds(base + 8 * q + r, 1), :]
                own = s_ref[pl.ds(base + 8 * q + r, 1), :]
                for t in range(q, 8):
                    term = jnp.where(ids[t] == own, whole[t], 0.0) * u
                    m = t - q
                    found[m] = term if found[m] is None else found[m] + term
            for m in range(8):
                sums[r, 8 * m : 8 * m + 8, :] += found[m]
        return carry

    lax.fori_loop(0, blocks - ahead, block, 0)
    total = sums[0, 0:REACH, :]
    for r in range(1, 8):
        total = total + sums[r, r : r + REACH, :]
    out_ref[...] = total


def gain_kernel(place, taps_ref, x_ref, own_ref, *rest, vectors):
    out_ref = rest[-1]
    sends = rest[: -1 - vectors]
    start = taps_ref.shape[0]
    out_ref[0:start, :] = taps_ref[...]
    for ref in rest[-1 - vectors : -1]:
        start = put_row(out_ref, start, ref[...])
    size = len(sends) + 1
    height = own_ref.shape[0]
    gain = jnp.zeros((8, x_ref.shape[1]), F32)
    bias = gain
    step = min(64, height)
    for k in range(size):
        source = own_ref if k == 0 else sends[k - 1]

        def rows_step(i, state, source=source, k=k):
            gain, bias = state
            unit = x_ref[at(height * toward(place, k, size) + step * i, step), :].astype(F32)
            part = source[at(step * i, step), :].astype(F32)
            scaled = part * unit
            for j in range(0, step, 8):
                gain = gain + scaled[j : j + 8]
                bias = bias + part[j : j + 8]
            return gain, bias

        gain, bias = lax.fori_loop(0, height // step, rows_step, (gain, bias))
    start = put_row(out_ref, start, jnp.sum(gain, axis=0, keepdims=True))
    put_row(out_ref, start, jnp.sum(bias, axis=0, keepdims=True))


def gain_sums(place, taps, rows, own, sends, vectors):
    count, channels = taps.shape
    count += (sum(v.shape[1] for v in vectors) + 2 * rows.shape[1]) // channels
    return call(
        partial(gain_kernel, vectors=len(vectors)),
        "gain",
        [((count, channels), F32)],
        (place, taps, rows, own, *sends, *vectors),
        micros=2,
    )[0]


def taps_back(place, ids, halo, u_low, u_high, low, high, ties):
    channels = low.shape[1]
    length = halo.shape[0] + low.shape[0] + high.shape[0]
    return call(
        taps_back_kernel,
        "taps_back",
        [((REACH, channels), F32)],
        (place, *ids, *ids, halo, u_low, u_high, low, high),
        scalars=3,
        ties=ties,
        scratch=[
            pltpu.SMEM((2 * length // 64,), jnp.int32),
            ((length, channels), F32),
            ((length, channels), F32),
            ((length - REACH, channels), F32),
            ((length, channels), F32),
            ((8, 64 + REACH, channels), F32),
        ],
        micros=TAPS_BACK,
    )[0]


def modes_back_kernel(
    place, c_ref, d_ref, f_ref, t_ref, mr_ref, mi_ref, out_ref,
    ar_s, ai_s, gr_s, gi_s, hr_s, hi_s, wide, wide_l,
):
    channels = c_ref.shape[1]
    count = ar_s.shape[0]
    half = at(count * place[1], count)
    damping, frequency, timestep = d_ref[:, half].T, f_ref[:, half].T, t_ref[...][None, :]
    ar, ai = modes(damping, frequency, timestep)
    ar_s[...] = ar
    ai_s[...] = ai
    for l in range(REACH):
        row = jnp.broadcast_to(c_ref[l : l + 1, :], (8, channels))
        wide[8 * l : 8 * l + 8, :] = row
        wide_l[8 * l : 8 * l + 8, :] = row * float(l)

    def one(p, carry):
        rows = at(8 * p, 8)
        a = (ar_s[rows, :], ai_s[rows, :])
        base = low_powers(*a, 16)
        jump = cmul(*base[8], *base[8])
        zero = jnp.zeros((8, channels), F32)

        def outer(o, state):
            pr, pi, gr, gi, hr, hi = state
            start = pl.multiple_of(128 * o, 128)
            sr = wide[pl.ds(start, 8), :]
            tr = wide_l[pl.ds(start, 8), :]
            si = zero
            ti = zero
            for j in range(1, 16):
                c = wide[pl.ds(start + 8 * j, 8), :]
                e = wide_l[pl.ds(start + 8 * j, 8), :]
                br, bi = base[j]
                sr += c * br
                si += c * bi
                tr += e * br
                ti += e * bi
            gr += pr * sr - pi * si
            gi += pr * si + pi * sr
            hr += pr * tr - pi * ti
            hi += pr * ti + pi * tr
            pr, pi = cmul(pr, pi, *jump)
            return pr, pi, gr, gi, hr, hi

        one_ = jnp.ones((8, channels), F32)
        _, _, gr, gi, hr, hi = lax.fori_loop(
            0, REACH // 16, outer, (one_, zero, zero, zero, zero, zero), unroll=4
        )
        gr_s[rows, :] = gr
        gi_s[rows, :] = gi
        hr_s[rows, :] = hr
        hi_s[rows, :] = hi
        return carry

    lax.fori_loop(0, ar_s.shape[0] // 8, one, 0)
    gr, gi, hr, hi = gr_s[...], gi_s[...], hr_s[...], hi_s[...]
    mr, mi = mr_ref[:, half].T, mi_ref[:, half].T
    qr, qi = ratios(damping, frequency, ar, ai)
    wr, wi = cmul(mr, mi, qr, qi)
    mixr, mixi = cmul(qr, qi, gr, gi)
    inverse = 1.0 / (damping * damping + frequency * frequency)
    nr, ni = -damping * inverse, -frequency * inverse
    vr, vi = cmul(*cmul(mr, mi, gr, gi), nr, ni)
    xr, xi = cmul(vr, vi, ar, ai)
    zr, zi = cmul(wr, wi, hr, hi)
    xr, xi = xr + zr, xi + zi
    yr, yi = cmul(vr, vi, qr, qi)
    grads = (yr - timestep * xr, yi - timestep * xi, mixr, -mixi)
    for i, grad in enumerate(grads):
        out_ref[channels * i : channels * (i + 1), :] = grad.T
    out_ref[4 * channels :, 0:channels] = jnp.broadcast_to(
        jnp.sum(-damping * xr - frequency * xi, axis=0, keepdims=True), (8, channels)
    )


def modes_back(place, c, damping, frequency, timestep, mix_real, mix_imaginary, ties):
    channels, count = damping.shape
    count = count // 2
    return call(
        modes_back_kernel,
        "modes_back",
        [((4 * channels + 8, count), F32)],
        (place, c, damping, frequency, timestep, mix_real, mix_imaginary),
        scratch=[((count, channels), F32)] * 6 + [((REACH * 8, channels), F32)] * 2,
        micros=MODES_BACK,
        ties=ties,
    )[0]


def unit_rows(x):
    x = x.astype(F32)
    shifted = x - jnp.mean(x, axis=-1, keepdims=True)
    inverse = lax.rsqrt(jnp.mean(shifted * shifted, axis=-1, keepdims=True) + EPSILON)
    return shifted * inverse, inverse


def norm_kernel(x_ref, gain_ref, bias_ref, out_ref, unit_ref):
    def step(i, carry):
        rows = at(128 * i, 128)
        unit, _ = unit_rows(x_ref[rows, :])
        out_ref[rows, :] = (unit * gain_ref[...][None, :] + bias_ref[...][None, :]).astype(BF16)
        unit_ref[rows, :] = unit.astype(BF16)
        return carry

    lax.fori_loop(0, x_ref.shape[0] // 128, step, 0)


def reduce_kernel(place, x_ref, b_ref, *rest, count):
    pieces = rest[:count]
    lo_ref, hi_ref, slope_ref, full_ref = rest[count:]
    depth = pieces[0].shape[0]
    for k in range(count):
        full_ref[at(depth * (place[0] ^ k if count > 1 else 0), depth), :] = pieces[k][...]
    half = lo_ref.shape[0]
    for part, out in enumerate((lo_ref, hi_ref)):
        rows = slice(half * part, half * part + half)
        act, slope = gelu_pair(dot(x_ref[rows, :], full_ref[...]) + b_ref[...][None, :])
        out[...] = act
        slope_ref[rows, :] = slope


def gate_kernel(x_ref, w_ref, b_ref, act_ref, slope_ref):
    def step(i, carry):
        rows = at(128 * i, 128)
        act, slope = gelu_pair(dot(x_ref[rows, :], w_ref[...]) + b_ref[...][None, :])
        act_ref[rows, :] = act.astype(BF16)
        slope_ref[rows, :] = slope.astype(BF16)
        return carry

    lax.fori_loop(0, x_ref.shape[0] // 128, step, 0)


def pack_kernel(place, gate_ref, expand_ref, output_ref, mine_ref, rest_ref):
    rows = gate_ref.shape[0]
    some = expand_ref.shape[0] // 2

    def store(first_ref, second_ref):
        first_ref[0:rows, :] = gate_ref[...]
        first_ref[rows:, :] = expand_ref[0:some, :]
        second_ref[0:rows, :] = output_ref[...].T
        second_ref[rows:, :] = expand_ref[some:, :]

    @pl.when(place[1] == 0)
    def _():
        store(mine_ref, rest_ref)

    @pl.when(place[1] != 0)
    def _():
        store(rest_ref, mine_ref)


def stack_kernel(*refs):
    for k, ref in enumerate(refs[:-1]):
        refs[-1][k] = ref[...]


def unpack_kernel(place, mine_ref, rest_ref, near_ref, far_ref, gate_ref, expand_ref, output_ref):
    mines = [mine_ref] + [near_ref.at[k] for k in range(3)]
    rests = [rest_ref] + [far_ref.at[k] for k in range(3)]
    rows = gate_ref.shape[0] // 4
    some = expand_ref.shape[0] // 8

    def store(firsts, seconds):
        for k in range(4):
            s = place[0] ^ k
            gate_ref[at(rows * s, rows), :] = firsts[k][0:rows, :]
            output_ref[at(rows * s, rows), :] = seconds[k][0:rows, :]
            expand_ref[at(2 * some * s, some), :] = firsts[k][rows:, :]
            expand_ref[at(2 * some * s + some, some), :] = seconds[k][rows:, :]

    @pl.when(place[1] == 0)
    def _():
        store(mines, rests)

    @pl.when(place[1] != 0)
    def _():
        store(rests, mines)


def expand_rows(place, k, refs, pieces, size):
    act_ref, slope_ref, we_ref, b_ref, wo_ref = refs
    height = pieces[0].shape[0] // size
    channels = pieces[0].shape[1]
    rows = at(height * toward(place, k, size), height)
    expanded = b_ref[...][None, :]
    for j in range(size):
        source = origin(place, j, size)
        expanded = expanded + dot(pieces[j][rows, :], we_ref[at(channels * source, channels), :])
    coef = (slope_ref[rows, :].astype(F32) * expanded).astype(BF16)
    gated = (expanded * act_ref[rows, :].astype(F32)).astype(BF16)
    half = wo_ref.shape[0] // 2
    return rows, gated, coef, [dot_t(gated, wo_ref[half * h : half * (h + 1), :]) for h in range(2)]


def expand_first_kernel(place, *rest, size):
    refs, pieces, (gated_ref, coef_ref, *sends) = rest[:5], rest[5 : 5 + size], rest[5 + size :]
    _, gated_ref[...], coef_ref[...], parts = expand_rows(place, size - 1, refs, pieces, size)
    for send, part in zip(sends, parts):
        send[...] = part.astype(BF16)


def expand_kernel(place, *rest, size):
    refs, pieces, rest = rest[:5], rest[5 : 5 + size], rest[5 + size :]
    last_gated_ref, last_coef_ref, gated_ref, coef_ref, *rest = rest
    owns, sends = rest[:2], rest[2:]
    for k in range(size - 1):
        rows, gated, coef, parts = expand_rows(place, k, refs, pieces, size)
        gated_ref[rows, :] = gated
        coef_ref[rows, :] = coef
        for h, part in enumerate(parts):
            if k == 0:
                owns[h][...] = part
            else:
                sends[(size - 2) * h + k - 1][...] = part.astype(BF16)
    height = last_gated_ref.shape[0]
    rows = at(height * toward(place, size - 1, size), height)
    gated_ref[rows, :] = last_gated_ref[...]
    coef_ref[rows, :] = last_coef_ref[...]


def halves(x):
    high = x.astype(BF16).astype(F32)
    return high, x - high


def loss_kernel(
    place, x_ref, t_ref, mask_ref, b_ref, act_ref, coef_ref, wo_ref, we_ref, *rest, size
):
    pieces, others, rest = rest[:size], rest[size : 2 * size], rest[2 * size :]
    out_ref, back_ref, keep_ref, low_ref, gate_ref, ob_ref, eb_ref, gb_ref, err_ref, own_ref, *rest = rest
    sends, mask_s = rest[:-1], rest[-1]
    height = pieces[0].shape[0]
    channels = own_ref.shape[1]
    mask_s[...] = jnp.broadcast_to(mask_ref[...].astype(F32), (mask_s.shape[1], mask_s.shape[0])).T
    outb = jnp.zeros_like(ob_ref)
    expb = jnp.zeros_like(eb_ref)
    gatb = jnp.zeros_like(gb_ref)
    errors = jnp.zeros((1, 1), F32)
    for j in range(size):
        rows = at(height * origin(place, j, size), height)
        branch = jnp.concatenate([pieces[j][...], others[j][...]], 1).astype(F32)
        result = x_ref[rows, :].astype(F32) + branch + b_ref[...][None, :]
        out_ref[rows, :] = result.astype(BF16)
        back = (result - t_ref[rows, :].astype(F32)) * mask_s[rows, 0:1]
        low = back.astype(BF16)
        back_ref[rows, :] = low
        if j == 0:
            keep_ref[...] = back
        outb = outb + jnp.sum(back, axis=0, keepdims=True)
        errors = errors + jnp.sum(jnp.sum(back * back, axis=0, keepdims=True), axis=1, keepdims=True)
        gated_back = dot(low, wo_ref[...])
        expanded_back = gated_back * act_ref[rows, :].astype(F32)
        expb = expb + jnp.sum(expanded_back, axis=0, keepdims=True)
        expand_low = expanded_back.astype(BF16)
        low_ref[rows, :] = expand_low
        gate_back = gated_back * coef_ref[rows, :].astype(F32)
        gatb = gatb + jnp.sum(gate_back, axis=0, keepdims=True)
        gate_ref[rows, :] = gate_back.astype(BF16)
        for k in range(size):
            target = toward(place, k, size)
            part = dot_t(expand_low, we_ref[at(channels * target, channels), :])
            if k == 0:
                own_ref[rows, :] = part
            else:
                sends[k - 1][rows, :] = part.astype(BF16)
    ob_ref[...] = outb
    eb_ref[...] = expb
    gb_ref[...] = gatb
    count = jnp.sum(mask_ref[...].astype(F32), axis=1, keepdims=True)
    half = err_ref.shape[1] // 4
    high, low = halves(
        jnp.concatenate([jnp.broadcast_to(errors, (1, half)), jnp.broadcast_to(count, (1, half))], 1)
    )
    err_ref[...] = jnp.concatenate([high, low], 1)


def gate_back_kernel(low_ref, w_ref, out_ref):
    height = 128
    for i in range(low_ref.shape[0] // height):
        rows = slice(height * i, height * (i + 1))
        out_ref[rows, :] = dot_t(low_ref[rows, :], w_ref[...])


def sum_kernel(own_ref, *rest):
    *pieces, lo_ref, hi_ref = rest
    total = own_ref[...]
    for piece in pieces:
        total = total + piece[...].astype(F32)
    half = lo_ref.shape[0]
    lo_ref[...] = total[:half]
    hi_ref[...] = total[half:]


def scale_of(total_ref, scale):
    row, tokens_all = scale
    return tokens_all / (total_ref[row : row + 1, 0:1] + total_ref[row + 2 : row + 3, 0:1])


EXTRA = 16


def rows_kernel(place, x_ref, gain_ref, keep_ref, total_ref, own_ref, *rest, scale, norm_at):
    *pieces, out_ref = rest
    height, features = own_ref.shape
    step = 32
    factor = scale_of(total_ref, scale)
    gain = gain_ref[...][None, :]

    def one(i, carry):
        rows = at(step * i, step)
        total = own_ref[rows, :]
        for piece in pieces:
            total = total + piece[rows, :].astype(F32)
        unit, inverse = unit_rows(x_ref[at(height * place[2] + step * i, step), :])
        scaled = total * gain
        back = inverse * (
            scaled
            - jnp.mean(scaled, axis=-1, keepdims=True)
            - unit * jnp.mean(scaled * unit, axis=-1, keepdims=True)
        )
        out_ref[rows, :] = (factor * (keep_ref[rows, :] + back)).astype(BF16)
        return carry

    lax.fori_loop(0, height // step, one, 0, unroll=2)
    width = total_ref.shape[1]
    count = features // width
    start = norm_at
    both = []
    for v in range(2):
        first = start + count * v
        both.append(
            jnp.concatenate(
                [total_ref[first + i : first + i + 1, :] for i in range(count)], axis=1
            )
        )
    both.append(jnp.zeros((EXTRA - 2, features), F32))
    out_ref[height:, :] = (factor * jnp.concatenate(both, 0)).astype(BF16)


def join_kernel(place, *rest):
    *pieces, out_ref, gain_ref, bias_ref, parts = rest
    size = len(pieces)
    height = pieces[0].shape[0] - EXTRA
    for k in range(size):
        source = origin(place, k, size)
        out_ref[at(height * source, height), :] = pieces[k][0:height, :]
        parts[source] = pieces[k][height:, :].astype(F32)
    total = parts[0]
    for k in range(1, size):
        total = total + parts[k]
    gain_ref[...] = total[0:1]
    bias_ref[...] = total[1:2]


def finish_kernel(place, sum_ref, mine_ref, other_ref, *outs, starts, scale):
    dd_ref, df_ref, dmr_ref, dmi_ref, dt_ref, loss_ref, *vectors = outs
    channels, count = dd_ref.shape
    count = count // 2
    row, tokens_all, features = scale
    errors = sum_ref[row - 1 : row, 0:1] + sum_ref[row + 1 : row + 2, 0:1]
    scale = scale_of(sum_ref, (row, tokens_all))
    loss_ref[...] = errors * scale * (1.0 / (tokens_all * features))
    for i, out in enumerate((dd_ref, df_ref, dmr_ref, dmi_ref)):
        rows = slice(channels * i, channels * (i + 1))
        out[:, at(count * place[1], count)] = mine_ref[rows, :] * scale
        out[:, at(count * (1 - place[1]), count)] = other_ref[rows, :] * scale
    row = slice(4 * channels, 4 * channels + 1)
    dt_ref[...] = (mine_ref[row, 0:channels] + other_ref[row, 0:channels]) * scale
    width = sum_ref.shape[1]
    for out, start in zip(vectors, starts):
        for i in range(out.shape[1] // width):
            out[:, width * i : width * (i + 1)] = sum_ref[start + i : start + i + 1, :] * scale


def early_kernel(place, gated_ref, back_ref, low_ref, *rest, size):
    pieces, (keep_ref, give_ref, mixed_s) = rest[:size], rest[size:]
    core = place[1]
    channels = pieces[0].shape[1]
    for j in range(size):
        source = origin(place, j, size)
        mixed_s[:, at(channels * source, channels)] = pieces[j][...]
    half = back_ref.shape[1] // 8
    some = mixed_s.shape[1] // 8
    for s in range(4):
        k = s
        keep_ref[k, 0:half, :] = t_dot(back_ref[:, at((2 * s + core) * half, half)], gated_ref[...])
        give_ref[k, 0:half, :] = t_dot(
            back_ref[:, at((2 * s + 1 - core) * half, half)], gated_ref[...]
        ).astype(BF16)
        both = t_dot(mixed_s[:, at(2 * some * s, 2 * some)], low_ref[...])
        keep_ref[k, half:, :] = jnp.where(core == 0, both[:some], both[some:])
        give_ref[k, half:, :] = jnp.where(core == 0, both[some:], both[:some]).astype(BF16)


PACK_ROWS = 80


def late_kernel(place, x_ref, gate_ref, reduce_ref, pack_ref, keep_ref, give_ref, pack_s):
    core = place[1]
    half = x_ref.shape[1] // 8
    units = gate_ref.shape[1]
    for s in range(4):
        lines = slice(half * s, half * (s + 1))
        mine = x_ref[:, at((2 * s + core) * half, half)]
        keep_ref[lines, 0:units] = t_dot(mine, gate_ref[...])
        keep_ref[lines, units:] = t_dot(mine, reduce_ref[...])
        other = x_ref[:, at((2 * s + 1 - core) * half, half)]
        give_ref[lines, 0:units] = t_dot(other, gate_ref[...]).astype(BF16)
        give_ref[lines, units:] = t_dot(other, reduce_ref[...]).astype(BF16)
    pack_s[...] = jnp.zeros_like(pack_s)
    sums = pack_ref.shape[0]
    high, low = halves(pack_ref[0:REACH, :])
    pack_s[0:REACH, :] = high
    pack_s[REACH:sums, :] = pack_ref[REACH:, :]
    pack_s[sums : sums + REACH, :] = low
    width = pack_s.shape[1]
    for b in range(pack_s.shape[0] // PACK_ROWS):
        part = pack_s[PACK_ROWS * b : PACK_ROWS * (b + 1), :].astype(BF16)
        lanes = slice(width * b, width * (b + 1))
        give_ref[4 * half :, lanes] = part
        keep_ref[4 * half :, lanes] = part.astype(F32)


def pack_of(sums, pack_ref):
    width = pack_ref.shape[1]
    for b in range(pack_ref.shape[0] // PACK_ROWS):
        pack_ref[PACK_ROWS * b : PACK_ROWS * (b + 1), :] = sums[:, width * b : width * (b + 1)]


def late_pair_kernel(place, keep_ref, got_ref, own_ref, mine_ref, *rest, error_at, sums):
    *sends, pack_s = rest
    s = place[0]
    half = own_ref.shape[0]
    lines = at(half * s, half)
    own_ref[...] = keep_ref[lines, :] + got_ref[lines, :].astype(F32)
    pack_of(keep_ref[4 * half :, :] + got_ref[4 * half :, :].astype(F32), pack_s)
    high, low = halves(pack_s[error_at : error_at + 2, :] + pack_s[error_at + 2 : error_at + 4, :])
    pack_s[error_at : error_at + 2, :] = high
    pack_s[error_at + 2 : error_at + 4, :] = low
    high, low = halves(pack_s[0:REACH, :] + pack_s[sums : sums + REACH, :])
    pack_s[0:REACH, :] = high
    pack_s[sums : sums + REACH, :] = low
    width = pack_s.shape[1]
    for b in range(pack_s.shape[0] // PACK_ROWS):
        part = pack_s[PACK_ROWS * b : PACK_ROWS * (b + 1), :].astype(BF16)
        mine_ref[:, width * b : width * (b + 1)] = part
    for k in (1, 2, 3):
        lines = at(half * (s ^ k), half)
        sends[k - 1][0:half, :] = (keep_ref[lines, :] + got_ref[lines, :].astype(F32)).astype(BF16)
        sends[k - 1][half:, :] = mine_ref[...]


def late_sum_kernel(own_ref, mine_ref, first_ref, second_ref, third_ref, out_ref, total_ref, *, sums):
    half = own_ref.shape[0]
    first, second, third = (ref[...].astype(F32) for ref in (first_ref, second_ref, third_ref))
    out_ref[...] = (own_ref[...] + first[:half]) + (second[:half] + third[:half])
    pack_of(
        (mine_ref[...].astype(F32) + first[half:]) + (second[half:] + third[half:]), total_ref
    )
    total_ref[0:REACH, :] += total_ref[sums : sums + REACH, :]


def pair_kernel(place, keep_ref, got_ref, own_ref, *sends):
    s = place[0]
    own_ref[...] = keep_ref[s] + got_ref[s].astype(F32)
    for k in (1, 2, 3):
        sends[k - 1][...] = (keep_ref[s ^ k] + got_ref[s ^ k].astype(F32)).astype(BF16)


def early_out_kernel(place, own_ref, other_ref, total_ref, output_ref, expand_ref, *, scale):
    scale = scale_of(total_ref, scale)
    mine, other = own_ref[...].astype(F32) * scale, other_ref[...].astype(F32) * scale
    first = jnp.where(place[1] == 0, mine, other)
    second = jnp.where(place[1] == 0, other, mine)
    half = output_ref.shape[1] // 2
    some = expand_ref.shape[0] // 2
    output_ref[...] = jnp.concatenate([first[:half], second[:half]], 0).T
    expand_ref[0:some, :] = first[half:]
    expand_ref[some:, :] = second[half:]


def late_out_kernel(place, own_ref, other_ref, total_ref, gate_ref, reduce_ref, *, scale):
    scale = scale_of(total_ref, scale)
    mine, other = own_ref[...].astype(F32) * scale, other_ref[...].astype(F32) * scale
    first = jnp.where(place[1] == 0, mine, other)
    second = jnp.where(place[1] == 0, other, mine)
    half = gate_ref.shape[0] // 2
    units = gate_ref.shape[1]
    gate_ref[0:half, :] = first[:, :units]
    gate_ref[half:, :] = second[:, :units]
    reduce_ref[0:half, :] = first[:, units:]
    reduce_ref[half:, :] = second[:, units:]


def send_late(place, keep, give, channels, error_at, sums, ties):
    half = (keep.shape[0] - PACK_ROWS) // 4
    shape = (half, keep.shape[1])
    sent = (half + PACK_ROWS, keep.shape[1])
    pack = (PACK_ROWS * (keep.shape[1] // channels), channels)
    own, mine, *sends = call(
        partial(late_pair_kernel, error_at=error_at, sums=sums),
        "pair_late",
        [(shape, F32), ((PACK_ROWS, keep.shape[1]), BF16)] + [(sent, BF16)] * 3,
        (place, keep, swap_context(give)),
        scratch=[(pack, F32)],
        micros=PAIR,
        ties=ties,
    )
    got = [lax.ppermute(sends[k - 1], "shard", xor_pairs(4, k)) for k in (1, 2, 3)]
    own, total = call(
        partial(late_sum_kernel, sums=sums), "late_sum", [(shape, F32), (pack, F32)], (own, mine, *got), scalars=0, micros=1
    )
    return own, swap_context(own), total


def plain_grad(grad, scale, axis):
    paired = lax.psum(grad.astype(BF16), "context").astype(F32)
    return scale * lax.psum_scatter(paired, "shard", scatter_dimension=axis, tiled=True)


def per_device(
    inputs,
    teacher,
    segment_ids,
    valid_mask,
    norm_gain,
    norm_bias,
    gate_weight,
    gate_bias,
    reduce_weight,
    reduce_bias,
    damping,
    frequency,
    timestep,
    mix_real,
    mix_imaginary,
    expand_weight,
    expand_bias,
    output_weight,
    output_bias,
):
    tokens, width = inputs.shape
    channels = reduce_bias.shape[0]
    units = gate_bias.shape[0]
    size = lax.axis_size("tensor")
    shards = lax.axis_size("shard")
    contexts = lax.axis_size("context")
    core = lax.axis_index("context")
    shard = lax.axis_index("shard")
    tensor = lax.axis_index("tensor")
    fast = shards == 4 and contexts == 2 and size == 4
    height = tokens // size
    place = jnp.stack([shard, core, tensor]).astype(jnp.int32)

    ids = (segment_ids, swap_context(segment_ids))
    if fast:
        found = [lax.ppermute(reduce_weight, "shard", xor_pairs(4, k)) for k in (1, 2, 3)]
        reduce_pieces = [reduce_weight] + found
    else:
        reduce_pieces = [lax.all_gather(reduce_weight, "shard", axis=0, tiled=True)]
        gate_full = lax.all_gather(gate_weight, "shard", axis=0, tiled=True)
        expand_full = lax.all_gather(expand_weight, "shard", axis=0, tiled=True)
        output_full = lax.all_gather(output_weight.T, "shard", axis=0, tiled=True)

    mode_args = (damping, frequency, timestep, mix_real, mix_imaginary)
    taps_mine = make_taps(place, *mode_args, REACH // 2)
    taps = (taps_mine, swap_context(taps_mine))
    normed, unit = call(
        norm_kernel,
        "norm",
        [(inputs.shape, BF16)] * 2,
        (inputs, norm_gain, norm_bias),
        scalars=0,
        ties=(taps_mine,),
    )
    half_rows = (tokens // 2, channels)
    u_low, u_high, reduce_slope, reduce_full = call(
        partial(reduce_kernel, count=len(reduce_pieces)),
        "reduce",
        [(half_rows, F32), (half_rows, F32), ((tokens, channels), F32), ((width, channels), BF16)],
        (place, normed, reduce_bias, *reduce_pieces),
    )
    if fast:
        some = expand_weight.shape[0] // 2
        shape = (gate_weight.shape[0] + some, units)
        mine, rest = call(
            pack_kernel, "pack", [(shape, BF16)] * 2, (place, gate_weight, expand_weight, output_weight),
        )
        nears = [lax.ppermute(mine, "shard", xor_pairs(4, k)) for k in (1, 2, 3)]
    before = [(i, i + 1) for i in range(contexts - 1)]
    after = [(i + 1, i) for i in range(contexts - 1)]
    halo = lax.ppermute(u_high[tokens // 2 - REACH :], "context", before)
    mixed_own = forward_mix(place, ids, taps, halo, u_low, u_high)
    mixed = [mixed_own] + exchange_tensor([mixed_own] * (size - 1))
    if fast:
        shape = (3,) + mine.shape
        (near,) = call(stack_kernel, "stack", [(shape, BF16)], nears, scalars=0, ties=(mixed_own,))
        gate_full, expand_full, output_full = call(
            unpack_kernel,
            "unpack",
            [
                ((4 * gate_weight.shape[0], units), BF16),
                ((4 * expand_weight.shape[0], units), BF16),
                ((width, units), BF16),
            ],
            (place, mine, rest, near, swap_context(near)),
            micros=1,
        )
    gate_act, gate_slope = call(
        gate_kernel,
        "gate",
        [((tokens, units), BF16)] * 2,
        (normed, gate_full, gate_bias),
        scalars=0,
        micros=4,
    )
    piece = (height, width)
    half_piece = (height, width // 2)
    expand_args = (gate_act, gate_slope, expand_full, expand_bias, output_full, *mixed)
    last_gated, last_coef, *last_sends = call(
        partial(expand_first_kernel, size=size),
        "expand_first",
        [((height, units), BF16)] * 2 + [(half_piece, BF16)] * 2,
        (place, *expand_args),
        micros=1,
    )
    gated, coef, first_part, second_part, *branch_sends = call(
        partial(expand_kernel, size=size),
        "expand",
        [((tokens, units), BF16)] * 2 + [(half_piece, F32)] * 2 + [(half_piece, BF16)] * (2 * size - 4),
        (place, *expand_args, last_gated, last_coef),
        micros=3,
    )
    count = size - 2
    branch = sum_tensor(
        (first_part, second_part),
        (branch_sends[:count] + last_sends[:1], branch_sends[count:] + last_sends[1:]),
    )

    output, branch_back, keep_back, expand_low, gate_low, *rest = call(
        partial(loss_kernel, size=size),
        "loss",
        [
            (inputs.shape, BF16),
            (inputs.shape, BF16),
            (piece, F32),
            ((tokens, units), BF16),
            ((tokens, units), BF16),
            ((1, width), F32),
            ((1, units), F32),
            ((1, units), F32),
            ((1, 4 * channels), F32),
            ((tokens, channels), F32),
        ]
        + [((tokens, channels), BF16)] * (size - 1),
        (
            place,
            inputs,
            teacher,
            valid_mask,
            output_bias,
            gate_act,
            coef,
            output_full,
            expand_full,
            *branch[0],
            *branch[1],
        ),
        scratch=[((tokens, 128), F32)],
        micros=8,
    )
    output_sum, expand_sum, gate_sum, error_row, back_part, *back_sends = rest
    ties = ()
    if fast:
        shape = (4, (gate_weight.shape[0] + expand_weight.shape[0]) // 2, units)
        early = call(
            partial(early_kernel, size=size),
            "early",
            [(shape, F32), (shape, BF16)],
            (place, gated, branch_back, expand_low, *mixed),
            scratch=[((tokens, size * channels), BF16)],
            micros=EARLY,
        )
        early, *early_sends = call(
            pair_kernel,
            "pair_early",
            [(shape[1:], F32)] + [(shape[1:], BF16)] * 3,
            (place, early[0], swap_context(early[1])),
            micros=PAIR,
        )
        ties = (early,)
        early_got = [
            lax.ppermute(early_sends[k - 1], "shard", xor_pairs(4, k)).astype(F32) for k in (1, 2, 3)
        ]
        early = (early + early_got[0]) + (early_got[1] + early_got[2])
    back_got = exchange_tensor(back_sends)
    (gate_part,) = call(
        gate_back_kernel,
        "gate_back",
        [((tokens, width), F32)],
        (gate_low, gate_full),
        scalars=0,
        micros=1,
    )
    ties = ties + (gate_part,)
    g_low, g_high = call(
        sum_kernel,
        "sum",
        [(half_rows, F32)] * 2,
        (back_part, *back_got),
        scalars=0,
        ties=ties,
    )
    halo_back = lax.ppermute(g_low[:REACH], "context", after)
    reduce_low, reduce_sum, normed_part, *normed_sends = backward_mix(
        place, ids, taps, g_low, g_high, halo_back, reduce_slope, gate_part, reduce_full, size
    )
    normed_got, _ = deliver_tensor(normed_sends)

    vectors = (gate_sum, expand_sum, output_sum, reduce_sum, error_row)
    taps_part = taps_back(
        place, ids, halo, u_low, u_high, g_low, g_high, ()
    )
    pack = gain_sums(place, taps_part, unit, normed_part, normed_sends, vectors)
    norm_at = pack.shape[0] - 2 * width // channels
    error_at = norm_at - 4
    if fast:
        shape = (2 * gate_weight.shape[0] + PACK_ROWS, units + channels)
        late = call(
            late_kernel,
            "late",
            [(shape, F32), (shape, BF16)],
            (place, normed, gate_low, reduce_low, pack),
            ties=(early,),
            scratch=[((PACK_ROWS * (shape[1] // channels), channels), F32)],
            micros=LATE,
        )
        *late, total = send_late(place, *late, channels, error_at, pack.shape[0], ())
    else:
        total = sum_over(sum_over(pack, "context"), "shard")
    tokens_all = float(tokens * shards * contexts)

    scale = (error_at + 1, tokens_all)

    (rows_own,) = call(
        partial(rows_kernel, scale=scale, norm_at=norm_at),
        "rows",
        [((height + EXTRA, width), BF16)],
        (place, inputs, norm_gain, keep_back, total, normed_part, *normed_got),
        micros=3,
    )
    mode_mine = modes_back(place, total, *mode_args, ties=(rows_own,))
    inputs_grad, gain_grad, bias_grad = call(
        join_kernel,
        "join",
        [(inputs.shape, BF16), ((1, width), F32), ((1, width), F32)],
        (place, rows_own, *spread_tensor(rows_own, (mode_mine,))),
        scratch=[((size, EXTRA, width), F32)],
    )
    mode_other = swap_context(mode_mine)

    if fast:
        output_grad, expand_grad = call(
            partial(early_out_kernel, scale=scale),
            "early_out",
            [(output_weight.shape, F32), (expand_weight.shape, F32)],
            (place, early, swap_context(early), total),
        )
        gate_grad, reduce_grad = call(
            partial(late_out_kernel, scale=scale),
            "late_out",
            [(gate_weight.shape, F32), (reduce_weight.shape, F32)],
            (place, *late, total),
        )
    else:
        factor = tokens_all / total[error_at + 1, 0]
        mixed_full = lax.all_gather(mixed_own, "tensor", axis=1, tiled=True)
        output_grad = plain_grad(t_dot(gated, branch_back), factor, 1)
        expand_grad = plain_grad(t_dot(mixed_full, expand_low), factor, 0)
        gate_grad = plain_grad(t_dot(normed, gate_low), factor, 0)
        reduce_grad = plain_grad(t_dot(normed, reduce_low), factor, 0)

    counts = [v.shape[1] // channels for v in vectors]
    offsets = [REACH + sum(counts[:i]) for i in range(4)]
    whole = (damping.shape, F32)
    *mode_grads, timestep_grad, loss_value, gate_bias_grad, expand_bias_grad, output_bias_grad, reduce_bias_grad = call(
        partial(finish_kernel, starts=offsets, scale=scale + (float(width),)),
        "finish",
        [whole] * 4 + [((1, n), F32) for n in (channels, 1, units, units, width, channels)],
        (place, total, mode_mine, mode_other),
    )
    return (
        output,
        loss_value.reshape(()),
        inputs_grad,
        gain_grad[0],
        bias_grad[0],
        gate_grad,
        gate_bias_grad[0],
        reduce_grad,
        reduce_bias_grad[0],
        mode_grads[0],
        mode_grads[1],
        timestep_grad[0],
        mode_grads[2],
        mode_grads[3],
        expand_grad,
        expand_bias_grad[0],
        output_grad,
        output_bias_grad[0],
    )


def solution(mesh):
    tokens = P(("shard", "context"), None)
    ids = P("shard", "context")
    split = P("shard", "tensor")
    rows = P("tensor", None)
    units = P("tensor")
    return jax.shard_map(
        per_device,
        mesh=mesh,
        in_specs=(
            tokens, tokens, ids, ids, P(), P(), split, units, split, units,
            rows, rows, units, rows, rows, split, units, P("tensor", "shard"), P(),
        ),
        out_specs=(
            tokens, P(), tokens, P(), P(), split, units, split, units,
            rows, rows, units, rows, rows, split, units, P("tensor", "shard"), P(),
        ),
        check_vma=False,
    )
```

```python
import math
from functools import partial

import jax
import jax.numpy as jnp
from jax import lax
from jax.experimental import pallas as pl
from jax.experimental.pallas import tpu as pltpu
from jax.sharding import PartitionSpec as P

REACH = 256
EPSILON = 1e-05
EARLY, PAIR, LATE, TAPS_BACK, MODES_BACK, TAPS = 2,1,2,4,4,60
GELU_SCALE = 0.7978845608028654
F32 = jnp.float32
BF16 = jnp.bfloat16
SMEM_SPEC = pl.BlockSpec(memory_space=pltpu.SMEM)
VMEM_SPEC = pl.BlockSpec(memory_space=pltpu.VMEM)


def call(body, name, outs, args, scalars=1, scratch=(), micros=2, ties=()):
    held = [(a.shape, a.dtype) for a in args[scalars:]] + list(outs)
    held += [entry for entry in scratch if isinstance(entry, tuple)]
    room = 0
    for shape, kind in held:
        shape = (8,) * (2 - len(shape)) + tuple(shape)
        room += math.prod(shape[:-2] + (max(shape[-2], 8), max(shape[-1], 128))) * jnp.dtype(kind).itemsize
    count = len(args)

    def kernel(*refs):
        body(*refs[:count], *refs[count + len(ties) :])

    return pl.pallas_call(
        kernel,
        out_shape=[jax.ShapeDtypeStruct(shape, kind) for shape, kind in outs],
        in_specs=[SMEM_SPEC] * scalars
        + [VMEM_SPEC] * (len(args) - scalars)
        + [pl.BlockSpec(memory_space=pl.ANY)] * len(ties),
        out_specs=[VMEM_SPEC] * len(outs),
        scratch_shapes=[
            pltpu.VMEM(*entry) if isinstance(entry, tuple) else entry for entry in scratch
        ],
        compiler_params=pltpu.CompilerParams(vmem_limit_bytes=room + room // 16 + (3 << 20)),
        cost_estimate=pl.CostEstimate(
            flops=int(micros * 0.2e9), bytes_accessed=int(micros * 1e5), transcendentals=0
        ),
        name=name,
    )(*args, *ties)


def dot(a, b):
    return jnp.dot(a, b, preferred_element_type=F32)


def dot_t(a, b):
    return lax.dot_general(a, b, (((1,), (1,)), ((), ())), preferred_element_type=F32)


def t_dot(a, b):
    return lax.dot_general(a, b, (((0,), (0,)), ((), ())), preferred_element_type=F32)


def at(start, size, unit=None):
    return pl.ds(pl.multiple_of(start, unit or size), size)


def gelu_pair(a):
    square = a * a
    bent = jnp.tanh(GELU_SCALE * (a + 0.044715 * (a * square)))
    half = 0.5 * (1.0 + bent)
    slope = half + 0.5 * a * (1.0 - bent * bent) * (GELU_SCALE + 3 * 0.044715 * GELU_SCALE * square)
    return a * half, slope


def xor_pairs(size, mask):
    return [(i, i ^ mask) for i in range(size)]


def shift_pairs(size, step):
    return [(i, (i + step) % size) for i in range(size)]


def swap_context(x):
    return lax.ppermute(x, "context", [(0, 1), (1, 0)])


def sum_over(x, axis):
    size = lax.axis_size(axis)
    if size == 4:
        first = lax.ppermute(x, axis, xor_pairs(4, 1))
        second = lax.ppermute(x, axis, xor_pairs(4, 2))
        third = lax.ppermute(x, axis, xor_pairs(4, 3))
        return (x + first) + (second + third)
    step = 1
    while step < size:
        x = x + lax.ppermute(x, axis, xor_pairs(size, step))
        step *= 2
    return x


def copy_kernel(x_ref, out_ref):
    out_ref[...] = x_ref[...]


def add_kernel(x_ref, y_ref, z_ref, sum_ref, copy_ref):
    sum_ref[...] = (x_ref[...].astype(F32) + y_ref[...].astype(F32)).astype(BF16)
    copy_ref[...] = z_ref[...]


def toward(place, k, size):
    return place[2] ^ k if size == 4 else lax.rem(place[2] + k, size)


def origin(place, k, size):
    return place[2] ^ k if size == 4 else lax.rem(place[2] + size - k, size)


def tensor_pairs(size, k):
    return xor_pairs(size, k) if size == 4 else shift_pairs(size, k)


def exchange_tensor(pieces):
    size = lax.axis_size("tensor")
    return [lax.ppermute(x, "tensor", tensor_pairs(size, k + 1)) for k, x in enumerate(pieces)]


def stage_kernel(x_ref, y_ref, z_ref, w_ref, sum_ref, copy_ref, next_ref):
    sum_ref[...] = (x_ref[...].astype(F32) + y_ref[...].astype(F32)).astype(BF16)
    copy_ref[...] = z_ref[...]
    next_ref[...] = w_ref[...]


def sum_tensor(owns, sends):
    size = lax.axis_size("tensor")
    if size != 4:
        found = []
        for own, pieces in zip(owns, sends):
            for got in exchange_tensor(pieces):
                own = own + got.astype(F32)
            own = own.astype(BF16)
            found.append([own] + exchange_tensor([own] * (size - 1)))
        return found
    near_pairs, far_pairs = xor_pairs(4, 1), xor_pairs(4, 2)

    def stage(pieces, passed, after):
        return call(
            stage_kernel,
            "stage",
            [(passed.shape, BF16)] * 3,
            (pieces[1], passed, pieces[0], after),
            scalars=0,
            micros=0.5,
        )

    first, second = sends
    passed = lax.ppermute(first[2], "tensor", near_pairs)
    joined, near, after = stage(first, passed, second[2])
    first_far = lax.ppermute(joined, "tensor", far_pairs)
    passed = lax.ppermute(after, "tensor", near_pairs)
    first_near = lax.ppermute(near, "tensor", near_pairs)
    joined, near, _ = stage(second, passed, second[0])
    second_far = lax.ppermute(joined, "tensor", far_pairs)
    second_near = lax.ppermute(near, "tensor", near_pairs)
    found = []
    for own, far, near in ((owns[0], first_far, first_near), (owns[1], second_far, second_near)):
        total = (own + (far.astype(F32) + near.astype(F32))).astype(BF16)
        away = lax.ppermute(total, "tensor", far_pairs)
        beside = lax.ppermute(total, "tensor", near_pairs)
        found.append([total, beside, away, lax.ppermute(away, "tensor", near_pairs)])
    return found


def spread_tensor(x, ties=()):
    size = lax.axis_size("tensor")
    if size == 4:
        near = lax.ppermute(x, "tensor", xor_pairs(4, 1))
        far = lax.ppermute(x, "tensor", xor_pairs(4, 2))
        (again,) = call(
            copy_kernel,
            "again",
            [(x.shape, x.dtype)],
            (far,),
            scalars=0,
            micros=0.5,
            ties=(near,) + ties,
        )
        return [near, far, lax.ppermute(again, "tensor", xor_pairs(4, 1))]
    return [lax.ppermute(x, "tensor", shift_pairs(size, k)) for k in range(1, size)]


def deliver_tensor(pieces):
    size = lax.axis_size("tensor")
    if size == 4:
        passed = lax.ppermute(pieces[2], "tensor", xor_pairs(4, 1))
        joined, near = call(
            add_kernel,
            "joined",
            [(passed.shape, BF16)] * 2,
            (pieces[1], passed, pieces[0]),
            scalars=0,
            micros=0.5,
        )
        found = [
            lax.ppermute(near, "tensor", xor_pairs(4, 1)),
            lax.ppermute(joined, "tensor", xor_pairs(4, 2)),
        ]
        return found, joined
    found = [lax.ppermute(x, "tensor", shift_pairs(size, k + 1)) for k, x in enumerate(pieces)]
    return found, found[0]


def cmul(ar, ai, br, bi):
    return ar * br - ai * bi, ar * bi + ai * br


def modes(damping, frequency, timestep):
    magnitude = jnp.exp(-timestep * damping)
    angle = timestep * frequency
    return magnitude * jnp.cos(angle), magnitude * jnp.sin(angle)


def ratios(damping, frequency, ar, ai):
    minus = ar - 1.0
    inverse = 1.0 / (damping * damping + frequency * frequency)
    return (ai * frequency - minus * damping) * inverse, -(
        minus * frequency + ai * damping
    ) * inverse


def low_powers(ar, ai, count):
    found = [None, (ar, ai)]
    for j in range(2, count):
        found.append(cmul(*found[j // 2], *found[j - j // 2]))
    return found


def taps_kernel(place, d_ref, f_ref, t_ref, mr_ref, mi_ref, k_ref, ar_s, ai_s, wr_s, wi_s, acc, lags):
    damping, frequency, timestep = d_ref[...].T, f_ref[...].T, t_ref[...][None, :]
    ar, ai = modes(damping, frequency, timestep)
    qr, qi = ratios(damping, frequency, ar, ai)
    mr, mi = mr_ref[...].T, mi_ref[...].T
    wr, wi = mr * qr - mi * qi, mr * qi + mi * qr
    ar_s[...] = ar
    ai_s[...] = ai
    if lags < REACH:
        power = (ar, ai)
        for _ in range(lags.bit_length() - 1):
            power = cmul(*power, *power)
        later = place[1] > 0
        vr, vi = cmul(wr, wi, *power)
        wr, wi = jnp.where(later, vr, wr), jnp.where(later, vi, wi)
    wr_s[...] = wr
    wi_s[...] = wi
    acc[...] = jnp.zeros_like(acc)

    def pair(p, carry):
        rows = at(16 * p, 16)
        a = (ar_s[rows, :], ai_s[rows, :])
        base = low_powers(*a, 8)
        eight = cmul(*base[4], *base[4])

        def outer(o, w):
            wr, wi = w
            start = pl.multiple_of(64 * o, 64)
            for j in range(8):
                term = wr if j == 0 else wr * base[j][0] - wi * base[j][1]
                acc[pl.ds(start + 8 * j, 8), :] += term[:8] + term[8:]
            return cmul(wr, wi, *eight)

        lax.fori_loop(0, lags // 8, outer, (wr_s[rows, :], wi_s[rows, :]), unroll=4)
        return carry

    lax.fori_loop(0, ar_s.shape[0] // 16, pair, 0)
    k_ref[...] = jnp.sum(acc[...].reshape(lags, 8, acc.shape[1]), axis=1)


def make_taps(place, damping, frequency, timestep, mix_real, mix_imaginary, lags):
    channels, count = damping.shape
    return call(
        partial(taps_kernel, lags=lags),
        "taps",
        [((lags, channels), F32)],
        (place, damping, frequency, timestep, mix_real, mix_imaginary),
        scratch=[((count, channels), F32)] * 4 + [((lags * 8, channels), F32)],
        micros=TAPS,
    )[0]


def shifted_copies(pad, copies, lead):
    length = copies.shape[1]
    for r in range(8):
        start = 64 + lead - r
        copies[r, :, :] = pad[start : start + length, :]


def linked_blocks(edges, first, step, bound):
    blocks = edges.shape[0] // 2
    mine = edges[first] if step < 0 else edges[blocks + first]

    def more(count):
        there = jnp.clip(first + step * (count + 1), 0, blocks - 1)
        edge = edges[blocks + there] if step < 0 else edges[there]
        return jnp.logical_and(count < bound, edge == mine)

    return lax.while_loop(more, lambda c: c + 1, 0)


def tile(index):
    return at(8 * index, 8)


def fill_ids(place, own, other, own_row, other_row, edges, ids, early):
    length, channels = ids.shape
    tokens = own_row.shape[1]
    valid = place[1] > 0 if early else place[1] == 0
    near = slice(tokens - REACH, tokens) if early else slice(0, REACH)
    halo = jnp.where(valid, other_row[:, near].astype(F32), -1.0)
    mine = own_row[...].astype(F32)
    at_halo, at_own = (0, REACH) if early else (tokens, 0)
    ids[at_halo : at_halo + REACH, :] = jnp.broadcast_to(halo, (channels, REACH)).T
    ids[at_own : at_own + tokens, :] = jnp.broadcast_to(mine, (channels, tokens)).T
    blocks = length // 64
    for b in range(blocks):
        for edge, offset in ((0, 0), (blocks, 63)):
            position = 64 * b + offset
            if at_own <= position < at_own + tokens:
                edges[edge + b] = own[0, position - at_own]
            else:
                value = other[0, position - at_halo + near.start]
                edges[edge + b] = jnp.where(valid, value, -1)


def fill_taps(place, pad, mine_ref, other_ref, flip):
    mine, other = mine_ref[...], other_ref[...]
    first = jnp.where(place[1] == 0, mine, other)
    second = jnp.where(place[1] == 0, other, mine)
    half = mine.shape[0]
    pad[...] = jnp.zeros_like(pad)
    if not flip:
        pad[64 : 64 + half, :] = first
        pad[64 + half : 64 + 2 * half, :] = second
        return
    end = 64 + 2 * half
    for l in range(half):
        pad[end - 1 - l : end - l, :] = first[l : l + 1]
        pad[end - half - 1 - l : end - half - l, :] = second[l : l + 1]


def fill_rows(whole, pieces):
    start = 0
    for piece in pieces:
        whole[start : start + piece.shape[0], :] = piece[...]
        start += piece.shape[0]


def forward_kernel(
    place, own, other, own_row, other_row, k0_ref, k1_ref, halo_ref, lo_ref, hi_ref, y_ref,
    edges, pad, copies, kept, u_s, s_ref,
):
    channels = lo_ref.shape[1]
    blocks = u_s.shape[0] // 64
    ahead = REACH // 64
    fill_ids(place, own, other, own_row, other_row, edges, s_ref, True)
    fill_taps(place, pad, k0_ref, k1_ref, False)
    shifted_copies(pad, copies, 0)
    fill_rows(u_s, (halo_ref, lo_ref, hi_ref))
    for b in range(blocks):
        rows = slice(64 * b, 64 * b + 64)
        edge = edges[blocks + b].astype(F32)
        kept[rows, :] = jnp.where(s_ref[rows, :] == edge, u_s[rows, :], 0.0)

    def block(i, carry):
        mine = i + ahead
        zero = jnp.zeros((8, channels), F32)
        reach = linked_blocks(edges, mine, -1, ahead)

        def far(d, sums):
            sums = list(sums)
            start = pl.multiple_of(64 * (mine - 1 - d), 64)
            for r in range(8):
                taps = [copies[r, tile(8 * (d + 1) + m), :] for m in range(-7, 8)]
                for q in range(8):
                    u = kept[pl.ds(start + 8 * q + r, 1), :]
                    for t in range(8):
                        sums[t] += taps[t - q + 7] * u
            return tuple(sums)

        sums = lax.fori_loop(0, reach, far, (zero,) * 8)
        base = pl.multiple_of(64 * mine, 64)
        ids = [s_ref[pl.ds(base + 8 * t, 8), :] for t in range(8)]
        first = edges[mine].astype(F32)
        sums = [jnp.where(ids[t] == first, sums[t], 0.0) for t in range(8)]
        for r in range(8):
            taps = [copies[r, 8 * m : 8 * m + 8, :] for m in range(8)]
            for q in range(8):
                u = u_s[pl.ds(base + 8 * q + r, 1), :]
                own = s_ref[pl.ds(base + 8 * q + r, 1), :]
                for t in range(q, 8):
                    sums[t] += jnp.where(ids[t] == own, taps[t - q], 0.0) * u
        for t in range(0, 8, 2):
            both = jnp.concatenate([sums[t], sums[t + 1]], 0)
            y_ref[at(64 * i + 8 * t, 16), :] = both.astype(y_ref.dtype)
        return carry

    lax.fori_loop(0, blocks - ahead, block, 0)


def forward_mix(place, ids, taps, halo, low, high):
    channels = low.shape[1]
    length = halo.shape[0] + low.shape[0] + high.shape[0]
    return call(
        forward_kernel,
        "forward_mix",
        [((length - REACH, channels), BF16)],
        (place, *ids, *ids, *taps, halo, low, high),
        scalars=3,
        scratch=[
            pltpu.SMEM((2 * length // 64,), jnp.int32),
            ((64 + REACH + 128, channels), F32),
            ((8, 64 + REACH, channels), F32),
            ((length, channels), F32),
            ((length, channels), F32),
            ((length, channels), F32),
        ],
        micros=5,
    )[0]


def backward_kernel(
    place, own, other, own_row, other_row, k0_ref, k1_ref, lo_ref, hi_ref, halo_ref, slope_ref,
    part_ref, w_ref, low_ref, sum_ref, own_ref, *rest,
):
    *sends, edges, pad, copies, alive, g_s, s_ref = rest
    channels = lo_ref.shape[1]
    blocks = g_s.shape[0] // 64
    ahead = REACH // 64
    fill_ids(place, own, other, own_row, other_row, edges, s_ref, False)
    fill_taps(place, pad, k0_ref, k1_ref, True)
    shifted_copies(pad, copies, -57)
    fill_rows(g_s, (lo_ref, hi_ref, halo_ref))
    for b in range(blocks):
        rows = slice(64 * b, 64 * b + 64)
        edge = edges[b].astype(F32)
        alive[rows, :] = jnp.where(s_ref[rows, :] == edge, g_s[rows, :], 0.0)

    def block(j, total):
        zero = jnp.zeros((8, channels), F32)
        reach = linked_blocks(edges, j, 1, ahead)

        def far(d, sums):
            sums = list(sums)
            start = pl.multiple_of(64 * (j + 1 + d), 64)
            for r in range(8):
                taps = [copies[r, tile(39 - (8 * (d + 1) + m)), :] for m in range(-7, 8)]
                for q in range(8):
                    g = alive[pl.ds(start + 8 * q + r, 1), :]
                    for t in range(8):
                        sums[t] += taps[q - t + 7] * g
            return tuple(sums)

        sums = lax.fori_loop(0, reach, far, (zero,) * 8)
        base = pl.multiple_of(64 * j, 64)
        ids = [s_ref[pl.ds(base + 8 * t, 8), :] for t in range(8)]
        last = edges[blocks + j].astype(F32)
        sums = [jnp.where(ids[t] == last, sums[t], 0.0) for t in range(8)]
        for r in range(8):
            taps = [copies[r, 8 * (39 - m) : 8 * (39 - m) + 8, :] for m in range(8)]
            for q in range(8):
                g = g_s[pl.ds(base + 8 * q + r, 1), :]
                own = s_ref[pl.ds(base + 8 * q + r, 1), :]
                for t in range(q + 1):
                    sums[t] += jnp.where(ids[t] == own, taps[q - t], 0.0) * g
        for t in range(0, 8, 2):
            rows = at(64 * j + 8 * t, 16)
            both = jnp.concatenate([sums[t], sums[t + 1]], 0) * slope_ref[rows, :]
            low_ref[rows, :] = both.astype(low_ref.dtype)
            total = total + both
        return total

    total = lax.fori_loop(0, blocks - ahead, block, jnp.zeros((16, channels), F32))
    sum_ref[...] = jnp.sum(total, axis=0, keepdims=True)
    size = len(sends) + 1
    height = own_ref.shape[0]
    for k in range(size):
        rows = at(height * toward(place, k, size), height)
        piece = part_ref[rows, :] + dot_t(low_ref[rows, :], w_ref[...])
        if k == 0:
            own_ref[...] = piece
        else:
            sends[k - 1][...] = piece.astype(BF16)


def backward_mix(place, ids, taps, low, high, halo, slope, part, weight, size):
    channels = low.shape[1]
    length = halo.shape[0] + low.shape[0] + high.shape[0]
    piece = (part.shape[0] // size, part.shape[1])
    return call(
        backward_kernel,
        "backward_mix",
        [(slope.shape, BF16), ((1, channels), F32), (piece, F32)] + [(piece, BF16)] * (size - 1),
        (place, *ids, *ids, *taps, low, high, halo, slope, part, weight),
        scalars=3,
        scratch=[
            pltpu.SMEM((2 * length // 64,), jnp.int32),
            ((64 + REACH + 128, channels), F32),
            ((8, 64 + REACH, channels), F32),
            ((length, channels), F32),
            ((length, channels), F32),
            ((length, channels), F32),
        ],
        micros=6,
    )


def put_row(out_ref, start, row):
    width = out_ref.shape[1]
    for i in range(row.shape[1] // width):
        out_ref[start + i : start + i + 1, :] = row[:, width * i : width * (i + 1)]
    return start + row.shape[1] // width


def taps_back_kernel(
    place, own_id, other_id, own_row, other_row, halo_ref, ulo_ref, uhi_ref, lo_ref, hi_ref,
    out_ref, edges, kept, u_s, g_s, s_ref, sums,
):
    channels = ulo_ref.shape[1]
    blocks = u_s.shape[0] // 64
    ahead = REACH // 64
    fill_ids(place, own_id, other_id, own_row, other_row, edges, s_ref, True)
    fill_rows(u_s, (halo_ref, ulo_ref, uhi_ref))
    fill_rows(g_s, (lo_ref, hi_ref))
    sums[...] = jnp.zeros_like(sums)
    for b in range(blocks):
        rows = slice(64 * b, 64 * b + 64)
        edge = edges[blocks + b].astype(F32)
        kept[rows, :] = jnp.where(s_ref[rows, :] == edge, u_s[rows, :], 0.0)

    def block(i, carry):
        mine = i + ahead
        reach = linked_blocks(edges, mine, -1, ahead)
        base = pl.multiple_of(64 * mine, 64)
        back = pl.multiple_of(64 * i, 64)
        ids = [s_ref[pl.ds(base + 8 * t, 8), :] for t in range(8)]
        whole = [g_s[pl.ds(back + 8 * t, 8), :] for t in range(8)]
        first = edges[mine].astype(F32)
        alive = [jnp.where(ids[t] == first, whole[t], 0.0) for t in range(8)]

        def far(d, carried):
            start = pl.multiple_of(64 * (mine - 1 - d), 64)
            for r in range(8):
                found = [None] * 15
                for q in range(8):
                    u = kept[pl.ds(start + 8 * q + r, 1), :]
                    for t in range(8):
                        term = carried[t] * u
                        m = t - q + 7
                        found[m] = term if found[m] is None else found[m] + term
                for m in range(-7, 8):
                    sums[r, tile(8 * (d + 1) + m), :] += found[m + 7]
            return carried

        lax.fori_loop(0, reach, far, tuple(alive))
        for r in range(8):
            found = [None] * 8
            for q in range(8):
                u = u_s[pl.ds(base + 8 * q + r, 1), :]
                own = s_ref[pl.ds(base + 8 * q + r, 1), :]
                for t in range(q, 8):
                    term = jnp.where(ids[t] == own, whole[t], 0.0) * u
                    m = t - q
                    found[m] = term if found[m] is None else found[m] + term
            for m in range(8):
                sums[r, 8 * m : 8 * m + 8, :] += found[m]
        return carry

    lax.fori_loop(0, blocks - ahead, block, 0)
    total = sums[0, 0:REACH, :]
    for r in range(1, 8):
        total = total + sums[r, r : r + REACH, :]
    out_ref[...] = total


def gain_kernel(place, taps_ref, x_ref, own_ref, *rest, vectors):
    out_ref = rest[-1]
    sends = rest[: -1 - vectors]
    start = taps_ref.shape[0]
    out_ref[0:start, :] = taps_ref[...]
    for ref in rest[-1 - vectors : -1]:
        start = put_row(out_ref, start, ref[...])
    size = len(sends) + 1
    height = own_ref.shape[0]
    gain = jnp.zeros((8, x_ref.shape[1]), F32)
    bias = gain
    step = min(64, height)
    for k in range(size):
        source = own_ref if k == 0 else sends[k - 1]

        def rows_step(i, state, source=source, k=k):
            gain, bias = state
            unit = x_ref[at(height * toward(place, k, size) + step * i, step), :].astype(F32)
            part = source[at(step * i, step), :].astype(F32)
            scaled = part * unit
            for j in range(0, step, 8):
                gain = gain + scaled[j : j + 8]
                bias = bias + part[j : j + 8]
            return gain, bias

        gain, bias = lax.fori_loop(0, height // step, rows_step, (gain, bias))
    start = put_row(out_ref, start, jnp.sum(gain, axis=0, keepdims=True))
    put_row(out_ref, start, jnp.sum(bias, axis=0, keepdims=True))


def gain_sums(place, taps, rows, own, sends, vectors):
    count, channels = taps.shape
    count += (sum(v.shape[1] for v in vectors) + 2 * rows.shape[1]) // channels
    return call(
        partial(gain_kernel, vectors=len(vectors)),
        "gain",
        [((count, channels), F32)],
        (place, taps, rows, own, *sends, *vectors),
        micros=2,
    )[0]


def taps_back(place, ids, halo, u_low, u_high, low, high, ties):
    channels = low.shape[1]
    length = halo.shape[0] + low.shape[0] + high.shape[0]
    return call(
        taps_back_kernel,
        "taps_back",
        [((REACH, channels), F32)],
        (place, *ids, *ids, halo, u_low, u_high, low, high),
        scalars=3,
        ties=ties,
        scratch=[
            pltpu.SMEM((2 * length // 64,), jnp.int32),
            ((length, channels), F32),
            ((length, channels), F32),
            ((length - REACH, channels), F32),
            ((length, channels), F32),
            ((8, 64 + REACH, channels), F32),
        ],
        micros=TAPS_BACK,
    )[0]


def modes_back_kernel(
    place, c_ref, d_ref, f_ref, t_ref, mr_ref, mi_ref, out_ref,
    ar_s, ai_s, gr_s, gi_s, hr_s, hi_s, wide, wide_l,
):
    channels = c_ref.shape[1]
    count = ar_s.shape[0]
    half = at(count * place[1], count)
    damping, frequency, timestep = d_ref[:, half].T, f_ref[:, half].T, t_ref[...][None, :]
    ar, ai = modes(damping, frequency, timestep)
    ar_s[...] = ar
    ai_s[...] = ai
    for l in range(REACH):
        row = jnp.broadcast_to(c_ref[l : l + 1, :], (8, channels))
        wide[8 * l : 8 * l + 8, :] = row
        wide_l[8 * l : 8 * l + 8, :] = row * float(l)

    def one(p, carry):
        rows = at(8 * p, 8)
        a = (ar_s[rows, :], ai_s[rows, :])
        base = low_powers(*a, 16)
        jump = cmul(*base[8], *base[8])
        zero = jnp.zeros((8, channels), F32)

        def outer(o, state):
            pr, pi, gr, gi, hr, hi = state
            start = pl.multiple_of(128 * o, 128)
            sr = wide[pl.ds(start, 8), :]
            tr = wide_l[pl.ds(start, 8), :]
            si = zero
            ti = zero
            for j in range(1, 16):
                c = wide[pl.ds(start + 8 * j, 8), :]
                e = wide_l[pl.ds(start + 8 * j, 8), :]
                br, bi = base[j]
                sr += c * br
                si += c * bi
                tr += e * br
                ti += e * bi
            gr += pr * sr - pi * si
            gi += pr * si + pi * sr
            hr += pr * tr - pi * ti
            hi += pr * ti + pi * tr
            pr, pi = cmul(pr, pi, *jump)
            return pr, pi, gr, gi, hr, hi

        one_ = jnp.ones((8, channels), F32)
        _, _, gr, gi, hr, hi = lax.fori_loop(
            0, REACH // 16, outer, (one_, zero, zero, zero, zero, zero), unroll=4
        )
        gr_s[rows, :] = gr
        gi_s[rows, :] = gi
        hr_s[rows, :] = hr
        hi_s[rows, :] = hi
        return carry

    lax.fori_loop(0, ar_s.shape[0] // 8, one, 0)
    gr, gi, hr, hi = gr_s[...], gi_s[...], hr_s[...], hi_s[...]
    mr, mi = mr_ref[:, half].T, mi_ref[:, half].T
    qr, qi = ratios(damping, frequency, ar, ai)
    wr, wi = cmul(mr, mi, qr, qi)
    mixr, mixi = cmul(qr, qi, gr, gi)
    inverse = 1.0 / (damping * damping + frequency * frequency)
    nr, ni = -damping * inverse, -frequency * inverse
    vr, vi = cmul(*cmul(mr, mi, gr, gi), nr, ni)
    xr, xi = cmul(vr, vi, ar, ai)
    zr, zi = cmul(wr, wi, hr, hi)
    xr, xi = xr + zr, xi + zi
    yr, yi = cmul(vr, vi, qr, qi)
    grads = (yr - timestep * xr, yi - timestep * xi, mixr, -mixi)
    for i, grad in enumerate(grads):
        out_ref[channels * i : channels * (i + 1), :] = grad.T
    out_ref[4 * channels :, 0:channels] = jnp.broadcast_to(
        jnp.sum(-damping * xr - frequency * xi, axis=0, keepdims=True), (8, channels)
    )


def modes_back(place, c, damping, frequency, timestep, mix_real, mix_imaginary, ties):
    channels, count = damping.shape
    count = count // 2
    return call(
        modes_back_kernel,
        "modes_back",
        [((4 * channels + 8, count), F32)],
        (place, c, damping, frequency, timestep, mix_real, mix_imaginary),
        scratch=[((count, channels), F32)] * 6 + [((REACH * 8, channels), F32)] * 2,
        micros=MODES_BACK,
        ties=ties,
    )[0]


def unit_rows(x):
    x = x.astype(F32)
    shifted = x - jnp.mean(x, axis=-1, keepdims=True)
    inverse = lax.rsqrt(jnp.mean(shifted * shifted, axis=-1, keepdims=True) + EPSILON)
    return shifted * inverse, inverse


def norm_kernel(x_ref, gain_ref, bias_ref, out_ref, unit_ref):
    def step(i, carry):
        rows = at(128 * i, 128)
        unit, _ = unit_rows(x_ref[rows, :])
        out_ref[rows, :] = (unit * gain_ref[...][None, :] + bias_ref[...][None, :]).astype(BF16)
        unit_ref[rows, :] = unit.astype(BF16)
        return carry

    lax.fori_loop(0, x_ref.shape[0] // 128, step, 0)


def reduce_kernel(place, x_ref, b_ref, *rest, count):
    pieces = rest[:count]
    lo_ref, hi_ref, slope_ref, full_ref = rest[count:]
    depth = pieces[0].shape[0]
    for k in range(count):
        full_ref[at(depth * (place[0] ^ k if count > 1 else 0), depth), :] = pieces[k][...]
    half = lo_ref.shape[0]
    for part, out in enumerate((lo_ref, hi_ref)):
        rows = slice(half * part, half * part + half)
        act, slope = gelu_pair(dot(x_ref[rows, :], full_ref[...]) + b_ref[...][None, :])
        out[...] = act
        slope_ref[rows, :] = slope


def gate_kernel(x_ref, w_ref, b_ref, act_ref, slope_ref):
    def step(i, carry):
        rows = at(128 * i, 128)
        act, slope = gelu_pair(dot(x_ref[rows, :], w_ref[...]) + b_ref[...][None, :])
        act_ref[rows, :] = act.astype(BF16)
        slope_ref[rows, :] = slope.astype(BF16)
        return carry

    lax.fori_loop(0, x_ref.shape[0] // 128, step, 0)


def pack_kernel(place, gate_ref, expand_ref, output_ref, mine_ref, rest_ref):
    rows = gate_ref.shape[0]
    some = expand_ref.shape[0] // 2

    def store(first_ref, second_ref):
        first_ref[0:rows, :] = gate_ref[...]
        first_ref[rows:, :] = expand_ref[0:some, :]
        second_ref[0:rows, :] = output_ref[...].T
        second_ref[rows:, :] = expand_ref[some:, :]

    @pl.when(place[1] == 0)
    def _():
        store(mine_ref, rest_ref)

    @pl.when(place[1] != 0)
    def _():
        store(rest_ref, mine_ref)


def stack_kernel(*refs):
    for k, ref in enumerate(refs[:-1]):
        refs[-1][k] = ref[...]


def unpack_kernel(place, mine_ref, rest_ref, near_ref, far_ref, gate_ref, expand_ref, output_ref):
    mines = [mine_ref] + [near_ref.at[k] for k in range(3)]
    rests = [rest_ref] + [far_ref.at[k] for k in range(3)]
    rows = gate_ref.shape[0] // 4
    some = expand_ref.shape[0] // 8

    def store(firsts, seconds):
        for k in range(4):
            s = place[0] ^ k
            gate_ref[at(rows * s, rows), :] = firsts[k][0:rows, :]
            output_ref[at(rows * s, rows), :] = seconds[k][0:rows, :]
            start = 2 * some * (s ^ place[2])
            expand_ref[at(start, some), :] = firsts[k][rows:, :]
            expand_ref[at(start + some, some), :] = seconds[k][rows:, :]

    @pl.when(place[1] == 0)
    def _():
        store(mines, rests)

    @pl.when(place[1] != 0)
    def _():
        store(rests, mines)


def expand_rows(place, k, refs, pieces, size, ordered):
    act_ref, slope_ref, we_ref, b_ref, wo_ref = refs
    height = pieces[0].shape[0] // size
    channels = pieces[0].shape[1]
    rows = at(height * toward(place, k, size), height)
    expanded = b_ref[...][None, :]
    if ordered:
        mixed = jnp.concatenate([piece[rows, :] for piece in pieces], 1)
        expanded = expanded + dot(mixed, we_ref[...])
    else:
        for j in range(size):
            source = origin(place, j, size)
            expanded = expanded + dot(pieces[j][rows, :], we_ref[at(channels * source, channels), :])
    coef = (slope_ref[rows, :].astype(F32) * expanded).astype(BF16)
    gated = (expanded * act_ref[rows, :].astype(F32)).astype(BF16)
    half = wo_ref.shape[0] // 2
    return rows, gated, coef, [dot_t(gated, wo_ref[half * h : half * (h + 1), :]) for h in range(2)]


def expand_first_kernel(place, *rest, size, ordered):
    refs, pieces, (gated_ref, coef_ref, *sends) = rest[:5], rest[5 : 5 + size], rest[5 + size :]
    _, gated_ref[...], coef_ref[...], parts = expand_rows(
        place, size - 1, refs, pieces, size, ordered
    )
    for send, part in zip(sends, parts):
        send[...] = part.astype(BF16)


def expand_kernel(place, *rest, size, ordered):
    refs, pieces, rest = rest[:5], rest[5 : 5 + size], rest[5 + size :]
    last_gated_ref, last_coef_ref, gated_ref, coef_ref, *rest = rest
    owns, sends = rest[:2], rest[2:]
    for k in range(size - 1):
        rows, gated, coef, parts = expand_rows(place, k, refs, pieces, size, ordered)
        gated_ref[rows, :] = gated
        coef_ref[rows, :] = coef
        for h, part in enumerate(parts):
            if k == 0:
                owns[h][...] = part
            else:
                sends[(size - 2) * h + k - 1][...] = part.astype(BF16)
    height = last_gated_ref.shape[0]
    rows = at(height * toward(place, size - 1, size), height)
    gated_ref[rows, :] = last_gated_ref[...]
    coef_ref[rows, :] = last_coef_ref[...]


def halves(x):
    high = x.astype(BF16).astype(F32)
    return high, x - high


def loss_kernel(
    place, x_ref, t_ref, mask_ref, b_ref, act_ref, coef_ref, wo_ref, we_ref, *rest, size, ordered
):
    pieces, others, rest = rest[:size], rest[size : 2 * size], rest[2 * size :]
    out_ref, back_ref, keep_ref, low_ref, gate_ref, ob_ref, eb_ref, gb_ref, err_ref, own_ref, *rest = rest
    sends, mask_s = rest[:-1], rest[-1]
    height = pieces[0].shape[0]
    channels = own_ref.shape[1]
    mask_s[...] = jnp.broadcast_to(mask_ref[...].astype(F32), (mask_s.shape[1], mask_s.shape[0])).T
    outb = jnp.zeros_like(ob_ref)
    expb = jnp.zeros_like(eb_ref)
    gatb = jnp.zeros_like(gb_ref)
    errors = jnp.zeros((1, 1), F32)
    for j in range(size):
        rows = at(height * origin(place, j, size), height)
        branch = jnp.concatenate([pieces[j][...], others[j][...]], 1).astype(F32)
        result = x_ref[rows, :].astype(F32) + branch + b_ref[...][None, :]
        out_ref[rows, :] = result.astype(BF16)
        back = (result - t_ref[rows, :].astype(F32)) * mask_s[rows, 0:1]
        low = back.astype(BF16)
        back_ref[rows, :] = low
        if j == 0:
            keep_ref[...] = back
        outb = outb + jnp.sum(back, axis=0, keepdims=True)
        errors = errors + jnp.sum(jnp.sum(back * back, axis=0, keepdims=True), axis=1, keepdims=True)
        gated_back = dot(low, wo_ref[...])
        expanded_back = gated_back * act_ref[rows, :].astype(F32)
        expb = expb + jnp.sum(expanded_back, axis=0, keepdims=True)
        expand_low = expanded_back.astype(BF16)
        low_ref[rows, :] = expand_low
        gate_back = gated_back * coef_ref[rows, :].astype(F32)
        gatb = gatb + jnp.sum(gate_back, axis=0, keepdims=True)
        gate_ref[rows, :] = gate_back.astype(BF16)
        if ordered:
            whole = dot_t(expand_low, we_ref[...])
        for k in range(size):
            if ordered:
                part = whole[:, channels * k : channels * (k + 1)]
            else:
                target = toward(place, k, size)
                part = dot_t(expand_low, we_ref[at(channels * target, channels), :])
            if k == 0:
                own_ref[rows, :] = part
            else:
                sends[k - 1][rows, :] = part.astype(BF16)
    ob_ref[...] = outb
    eb_ref[...] = expb
    gb_ref[...] = gatb
    count = jnp.sum(mask_ref[...].astype(F32), axis=1, keepdims=True)
    half = err_ref.shape[1] // 4
    high, low = halves(
        jnp.concatenate([jnp.broadcast_to(errors, (1, half)), jnp.broadcast_to(count, (1, half))], 1)
    )
    err_ref[...] = jnp.concatenate([high, low], 1)


def gate_back_kernel(low_ref, w_ref, out_ref):
    height = 128
    for i in range(low_ref.shape[0] // height):
        rows = slice(height * i, height * (i + 1))
        out_ref[rows, :] = dot_t(low_ref[rows, :], w_ref[...])


def sum_kernel(own_ref, *rest):
    *pieces, lo_ref, hi_ref = rest
    total = own_ref[...]
    for piece in pieces:
        total = total + piece[...].astype(F32)
    half = lo_ref.shape[0]
    lo_ref[...] = total[:half]
    hi_ref[...] = total[half:]


def scale_of(total_ref, scale):
    row, tokens_all = scale
    return tokens_all / (total_ref[row : row + 1, 0:1] + total_ref[row + 2 : row + 3, 0:1])


EXTRA = 16


def rows_kernel(place, x_ref, gain_ref, keep_ref, total_ref, own_ref, *rest, scale, norm_at):
    *pieces, out_ref = rest
    height, features = own_ref.shape
    step = 32
    factor = scale_of(total_ref, scale)
    gain = gain_ref[...][None, :]

    def one(i, carry):
        rows = at(step * i, step)
        total = own_ref[rows, :]
        for piece in pieces:
            total = total + piece[rows, :].astype(F32)
        unit, inverse = unit_rows(x_ref[at(height * place[2] + step * i, step), :])
        scaled = total * gain
        back = inverse * (
            scaled
            - jnp.mean(scaled, axis=-1, keepdims=True)
            - unit * jnp.mean(scaled * unit, axis=-1, keepdims=True)
        )
        out_ref[rows, :] = (factor * (keep_ref[rows, :] + back)).astype(BF16)
        return carry

    lax.fori_loop(0, height // step, one, 0, unroll=2)
    width = total_ref.shape[1]
    count = features // width
    start = norm_at
    both = []
    for v in range(2):
        first = start + count * v
        both.append(
            jnp.concatenate(
                [total_ref[first + i : first + i + 1, :] for i in range(count)], axis=1
            )
        )
    both.append(jnp.zeros((EXTRA - 2, features), F32))
    out_ref[height:, :] = (factor * jnp.concatenate(both, 0)).astype(BF16)


def join_kernel(place, *rest):
    *pieces, out_ref, gain_ref, bias_ref, parts = rest
    size = len(pieces)
    height = pieces[0].shape[0] - EXTRA
    for k in range(size):
        source = origin(place, k, size)
        out_ref[at(height * source, height), :] = pieces[k][0:height, :]
        parts[source] = pieces[k][height:, :].astype(F32)
    total = parts[0]
    for k in range(1, size):
        total = total + parts[k]
    gain_ref[...] = total[0:1]
    bias_ref[...] = total[1:2]


def finish_kernel(place, sum_ref, mine_ref, other_ref, *outs, starts, scale):
    dd_ref, df_ref, dmr_ref, dmi_ref, dt_ref, loss_ref, *vectors = outs
    channels, count = dd_ref.shape
    count = count // 2
    row, tokens_all, features = scale
    errors = sum_ref[row - 1 : row, 0:1] + sum_ref[row + 1 : row + 2, 0:1]
    scale = scale_of(sum_ref, (row, tokens_all))
    loss_ref[...] = errors * scale * (1.0 / (tokens_all * features))
    for i, out in enumerate((dd_ref, df_ref, dmr_ref, dmi_ref)):
        rows = slice(channels * i, channels * (i + 1))
        out[:, at(count * place[1], count)] = mine_ref[rows, :] * scale
        out[:, at(count * (1 - place[1]), count)] = other_ref[rows, :] * scale
    row = slice(4 * channels, 4 * channels + 1)
    dt_ref[...] = (mine_ref[row, 0:channels] + other_ref[row, 0:channels]) * scale
    width = sum_ref.shape[1]
    for out, start in zip(vectors, starts):
        for i in range(out.shape[1] // width):
            out[:, width * i : width * (i + 1)] = sum_ref[start + i : start + i + 1, :] * scale


def early_kernel(place, gated_ref, back_ref, low_ref, *rest, size):
    pieces, (keep_ref, give_ref, mixed_s) = rest[:size], rest[size:]
    core = place[1]
    channels = pieces[0].shape[1]
    for j in range(size):
        source = origin(place, j, size)
        mixed_s[:, at(channels * source, channels)] = pieces[j][...]
    half = back_ref.shape[1] // 8
    some = mixed_s.shape[1] // 8
    for s in range(4):
        k = s
        both = t_dot(back_ref[:, 2 * half * s : 2 * half * (s + 1)], gated_ref[...])
        keep_ref[k, 0:half, :] = jnp.where(core == 0, both[:half], both[half:])
        give_ref[k, 0:half, :] = jnp.where(core == 0, both[half:], both[:half]).astype(BF16)
        both = t_dot(mixed_s[:, at(2 * some * s, 2 * some)], low_ref[...])
        keep_ref[k, half:, :] = jnp.where(core == 0, both[:some], both[some:])
        give_ref[k, half:, :] = jnp.where(core == 0, both[some:], both[:some]).astype(BF16)


PACK_ROWS = 80


def late_kernel(place, x_ref, gate_ref, reduce_ref, pack_ref, keep_ref, give_ref, pack_s):
    core = place[1]
    half = x_ref.shape[1] // 8
    units = gate_ref.shape[1]
    for s in range(4):
        lines = slice(half * s, half * (s + 1))
        rows = x_ref[:, 2 * half * s : 2 * half * (s + 1)]
        for right, lanes in ((gate_ref, slice(0, units)), (reduce_ref, slice(units, None))):
            both = t_dot(rows, right[...])
            keep_ref[lines, lanes] = jnp.where(core == 0, both[:half], both[half:])
            give_ref[lines, lanes] = jnp.where(core == 0, both[half:], both[:half]).astype(BF16)
    pack_s[...] = jnp.zeros_like(pack_s)
    sums = pack_ref.shape[0]
    high, low = halves(pack_ref[0:REACH, :])
    pack_s[0:REACH, :] = high
    pack_s[REACH:sums, :] = pack_ref[REACH:, :]
    pack_s[sums : sums + REACH, :] = low
    width = pack_s.shape[1]
    for b in range(pack_s.shape[0] // PACK_ROWS):
        part = pack_s[PACK_ROWS * b : PACK_ROWS * (b + 1), :].astype(BF16)
        lanes = slice(width * b, width * (b + 1))
        give_ref[4 * half :, lanes] = part
        keep_ref[4 * half :, lanes] = part.astype(F32)


def pack_of(sums, pack_ref):
    width = pack_ref.shape[1]
    for b in range(pack_ref.shape[0] // PACK_ROWS):
        pack_ref[PACK_ROWS * b : PACK_ROWS * (b + 1), :] = sums[:, width * b : width * (b + 1)]


def late_pair_kernel(place, keep_ref, got_ref, own_ref, mine_ref, *rest, error_at, sums):
    *sends, pack_s = rest
    s = place[0]
    half = own_ref.shape[0]
    lines = at(half * s, half)
    own_ref[...] = keep_ref[lines, :] + got_ref[lines, :].astype(F32)
    pack_of(keep_ref[4 * half :, :] + got_ref[4 * half :, :].astype(F32), pack_s)
    high, low = halves(pack_s[error_at : error_at + 2, :] + pack_s[error_at + 2 : error_at + 4, :])
    pack_s[error_at : error_at + 2, :] = high
    pack_s[error_at + 2 : error_at + 4, :] = low
    high, low = halves(pack_s[0:REACH, :] + pack_s[sums : sums + REACH, :])
    pack_s[0:REACH, :] = high
    pack_s[sums : sums + REACH, :] = low
    width = pack_s.shape[1]
    for b in range(pack_s.shape[0] // PACK_ROWS):
        part = pack_s[PACK_ROWS * b : PACK_ROWS * (b + 1), :].astype(BF16)
        mine_ref[:, width * b : width * (b + 1)] = part
    for k in (1, 2, 3):
        lines = at(half * (s ^ k), half)
        sends[k - 1][0:half, :] = (keep_ref[lines, :] + got_ref[lines, :].astype(F32)).astype(BF16)
        sends[k - 1][half:, :] = mine_ref[...]


def late_sum_kernel(own_ref, mine_ref, first_ref, second_ref, third_ref, out_ref, total_ref, *, sums):
    half = own_ref.shape[0]
    first, second, third = (ref[...].astype(F32) for ref in (first_ref, second_ref, third_ref))
    out_ref[...] = (own_ref[...] + first[:half]) + (second[:half] + third[:half])
    pack_of(
        (mine_ref[...].astype(F32) + first[half:]) + (second[half:] + third[half:]), total_ref
    )
    total_ref[0:REACH, :] += total_ref[sums : sums + REACH, :]


def pair_kernel(place, keep_ref, got_ref, own_ref, *sends):
    s = place[0]
    own_ref[...] = keep_ref[s] + got_ref[s].astype(F32)
    for k in (1, 2, 3):
        sends[k - 1][...] = (keep_ref[s ^ k] + got_ref[s ^ k].astype(F32)).astype(BF16)


def early_out_kernel(place, own_ref, other_ref, total_ref, output_ref, expand_ref, *, scale):
    scale = scale_of(total_ref, scale)
    mine, other = own_ref[...].astype(F32) * scale, other_ref[...].astype(F32) * scale
    first = jnp.where(place[1] == 0, mine, other)
    second = jnp.where(place[1] == 0, other, mine)
    half = output_ref.shape[1] // 2
    some = expand_ref.shape[0] // 2
    output_ref[...] = jnp.concatenate([first[:half], second[:half]], 0).T
    expand_ref[0:some, :] = first[half:]
    expand_ref[some:, :] = second[half:]


def late_out_kernel(place, own_ref, other_ref, total_ref, gate_ref, reduce_ref, *, scale):
    scale = scale_of(total_ref, scale)
    mine, other = own_ref[...].astype(F32) * scale, other_ref[...].astype(F32) * scale
    first = jnp.where(place[1] == 0, mine, other)
    second = jnp.where(place[1] == 0, other, mine)
    half = gate_ref.shape[0] // 2
    units = gate_ref.shape[1]
    gate_ref[0:half, :] = first[:, :units]
    gate_ref[half:, :] = second[:, :units]
    reduce_ref[0:half, :] = first[:, units:]
    reduce_ref[half:, :] = second[:, units:]


def send_late(place, keep, give, channels, error_at, sums, ties):
    half = (keep.shape[0] - PACK_ROWS) // 4
    shape = (half, keep.shape[1])
    sent = (half + PACK_ROWS, keep.shape[1])
    pack = (PACK_ROWS * (keep.shape[1] // channels), channels)
    own, mine, *sends = call(
        partial(late_pair_kernel, error_at=error_at, sums=sums),
        "pair_late",
        [(shape, F32), ((PACK_ROWS, keep.shape[1]), BF16)] + [(sent, BF16)] * 3,
        (place, keep, swap_context(give)),
        scratch=[(pack, F32)],
        micros=PAIR,
        ties=ties,
    )
    got = [lax.ppermute(sends[k - 1], "shard", xor_pairs(4, k)) for k in (1, 2, 3)]
    own, total = call(
        partial(late_sum_kernel, sums=sums), "late_sum", [(shape, F32), (pack, F32)], (own, mine, *got), scalars=0, micros=1
    )
    return own, swap_context(own), total


def plain_grad(grad, scale, axis):
    paired = lax.psum(grad.astype(BF16), "context").astype(F32)
    return scale * lax.psum_scatter(paired, "shard", scatter_dimension=axis, tiled=True)


def per_device(
    inputs,
    teacher,
    segment_ids,
    valid_mask,
    norm_gain,
    norm_bias,
    gate_weight,
    gate_bias,
    reduce_weight,
    reduce_bias,
    damping,
    frequency,
    timestep,
    mix_real,
    mix_imaginary,
    expand_weight,
    expand_bias,
    output_weight,
    output_bias,
):
    tokens, width = inputs.shape
    channels = reduce_bias.shape[0]
    units = gate_bias.shape[0]
    size = lax.axis_size("tensor")
    shards = lax.axis_size("shard")
    contexts = lax.axis_size("context")
    core = lax.axis_index("context")
    shard = lax.axis_index("shard")
    tensor = lax.axis_index("tensor")
    fast = shards == 4 and contexts == 2 and size == 4
    height = tokens // size
    place = jnp.stack([shard, core, tensor]).astype(jnp.int32)

    ids = (segment_ids, swap_context(segment_ids))
    if fast:
        found = [lax.ppermute(reduce_weight, "shard", xor_pairs(4, k)) for k in (1, 2, 3)]
        reduce_pieces = [reduce_weight] + found
    else:
        reduce_pieces = [lax.all_gather(reduce_weight, "shard", axis=0, tiled=True)]
        gate_full = lax.all_gather(gate_weight, "shard", axis=0, tiled=True)
        expand_full = lax.all_gather(expand_weight, "shard", axis=0, tiled=True)
        output_full = lax.all_gather(output_weight.T, "shard", axis=0, tiled=True)

    mode_args = (damping, frequency, timestep, mix_real, mix_imaginary)
    taps_mine = make_taps(place, *mode_args, REACH // 2)
    taps = (taps_mine, swap_context(taps_mine))
    normed, unit = call(
        norm_kernel,
        "norm",
        [(inputs.shape, BF16)] * 2,
        (inputs, norm_gain, norm_bias),
        scalars=0,
        ties=(taps_mine,),
    )
    half_rows = (tokens // 2, channels)
    u_low, u_high, reduce_slope, reduce_full = call(
        partial(reduce_kernel, count=len(reduce_pieces)),
        "reduce",
        [(half_rows, F32), (half_rows, F32), ((tokens, channels), F32), ((width, channels), BF16)],
        (place, normed, reduce_bias, *reduce_pieces),
    )
    if fast:
        some = expand_weight.shape[0] // 2
        shape = (gate_weight.shape[0] + some, units)
        mine, rest = call(
            pack_kernel, "pack", [(shape, BF16)] * 2, (place, gate_weight, expand_weight, output_weight),
        )
        nears = [lax.ppermute(mine, "shard", xor_pairs(4, k)) for k in (1, 2, 3)]
    before = [(i, i + 1) for i in range(contexts - 1)]
    after = [(i + 1, i) for i in range(contexts - 1)]
    halo = lax.ppermute(u_high[tokens // 2 - REACH :], "context", before)
    mixed_own = forward_mix(place, ids, taps, halo, u_low, u_high)
    mixed = [mixed_own] + exchange_tensor([mixed_own] * (size - 1))
    if fast:
        shape = (3,) + mine.shape
        (near,) = call(stack_kernel, "stack", [(shape, BF16)], nears, scalars=0, ties=(mixed_own,))
        gate_full, expand_full, output_full = call(
            unpack_kernel,
            "unpack",
            [
                ((4 * gate_weight.shape[0], units), BF16),
                ((4 * expand_weight.shape[0], units), BF16),
                ((width, units), BF16),
            ],
            (place, mine, rest, near, swap_context(near)),
            micros=1,
        )
    gate_act, gate_slope = call(
        gate_kernel,
        "gate",
        [((tokens, units), BF16)] * 2,
        (normed, gate_full, gate_bias),
        scalars=0,
        micros=4,
    )
    piece = (height, width)
    half_piece = (height, width // 2)
    expand_args = (gate_act, gate_slope, expand_full, expand_bias, output_full, *mixed)
    last_gated, last_coef, *last_sends = call(
        partial(expand_first_kernel, size=size, ordered=fast),
        "expand_first",
        [((height, units), BF16)] * 2 + [(half_piece, BF16)] * 2,
        (place, *expand_args),
        micros=1,
    )
    gated, coef, first_part, second_part, *branch_sends = call(
        partial(expand_kernel, size=size, ordered=fast),
        "expand",
        [((tokens, units), BF16)] * 2 + [(half_piece, F32)] * 2 + [(half_piece, BF16)] * (2 * size - 4),
        (place, *expand_args, last_gated, last_coef),
        micros=3,
    )
    count = size - 2
    branch = sum_tensor(
        (first_part, second_part),
        (branch_sends[:count] + last_sends[:1], branch_sends[count:] + last_sends[1:]),
    )

    output, branch_back, keep_back, expand_low, gate_low, *rest = call(
        partial(loss_kernel, size=size, ordered=fast),
        "loss",
        [
            (inputs.shape, BF16),
            (inputs.shape, BF16),
            (piece, F32),
            ((tokens, units), BF16),
            ((tokens, units), BF16),
            ((1, width), F32),
            ((1, units), F32),
            ((1, units), F32),
            ((1, 4 * channels), F32),
            ((tokens, channels), F32),
        ]
        + [((tokens, channels), BF16)] * (size - 1),
        (
            place,
            inputs,
            teacher,
            valid_mask,
            output_bias,
            gate_act,
            coef,
            output_full,
            expand_full,
            *branch[0],
            *branch[1],
        ),
        scratch=[((tokens, 128), F32)],
        micros=8,
    )
    output_sum, expand_sum, gate_sum, error_row, back_part, *back_sends = rest
    ties = ()
    if fast:
        shape = (4, (gate_weight.shape[0] + expand_weight.shape[0]) // 2, units)
        early = call(
            partial(early_kernel, size=size),
            "early",
            [(shape, F32), (shape, BF16)],
            (place, gated, branch_back, expand_low, *mixed),
            scratch=[((tokens, size * channels), BF16)],
            micros=EARLY,
        )
        early, *early_sends = call(
            pair_kernel,
            "pair_early",
            [(shape[1:], F32)] + [(shape[1:], BF16)] * 3,
            (place, early[0], swap_context(early[1])),
            micros=PAIR,
        )
        ties = (early,)
        early_got = [
            lax.ppermute(early_sends[k - 1], "shard", xor_pairs(4, k)).astype(F32) for k in (1, 2, 3)
        ]
        early = (early + early_got[0]) + (early_got[1] + early_got[2])
    back_got = exchange_tensor(back_sends)
    (gate_part,) = call(
        gate_back_kernel,
        "gate_back",
        [((tokens, width), F32)],
        (gate_low, gate_full),
        scalars=0,
        micros=1,
    )
    ties = ties + (gate_part,)
    g_low, g_high = call(
        sum_kernel,
        "sum",
        [(half_rows, F32)] * 2,
        (back_part, *back_got),
        scalars=0,
        ties=ties,
    )
    halo_back = lax.ppermute(g_low[:REACH], "context", after)
    reduce_low, reduce_sum, normed_part, *normed_sends = backward_mix(
        place, ids, taps, g_low, g_high, halo_back, reduce_slope, gate_part, reduce_full, size
    )
    normed_got, _ = deliver_tensor(normed_sends)

    vectors = (gate_sum, expand_sum, output_sum, reduce_sum, error_row)
    taps_part = taps_back(
        place, ids, halo, u_low, u_high, g_low, g_high, ()
    )
    pack = gain_sums(place, taps_part, unit, normed_part, normed_sends, vectors)
    norm_at = pack.shape[0] - 2 * width // channels
    error_at = norm_at - 4
    if fast:
        shape = (2 * gate_weight.shape[0] + PACK_ROWS, units + channels)
        late = call(
            late_kernel,
            "late",
            [(shape, F32), (shape, BF16)],
            (place, normed, gate_low, reduce_low, pack),
            ties=(early,),
            scratch=[((PACK_ROWS * (shape[1] // channels), channels), F32)],
            micros=LATE,
        )
        *late, total = send_late(place, *late, channels, error_at, pack.shape[0], ())
    else:
        total = sum_over(sum_over(pack, "context"), "shard")
    tokens_all = float(tokens * shards * contexts)

    scale = (error_at + 1, tokens_all)

    (rows_own,) = call(
        partial(rows_kernel, scale=scale, norm_at=norm_at),
        "rows",
        [((height + EXTRA, width), BF16)],
        (place, inputs, norm_gain, keep_back, total, normed_part, *normed_got),
        micros=3,
    )
    mode_mine = modes_back(place, total, *mode_args, ties=(rows_own,))
    inputs_grad, gain_grad, bias_grad = call(
        join_kernel,
        "join",
        [(inputs.shape, BF16), ((1, width), F32), ((1, width), F32)],
        (place, rows_own, *spread_tensor(rows_own, (mode_mine,))),
        scratch=[((size, EXTRA, width), F32)],
    )
    mode_other = swap_context(mode_mine)

    if fast:
        output_grad, expand_grad = call(
            partial(early_out_kernel, scale=scale),
            "early_out",
            [(output_weight.shape, F32), (expand_weight.shape, F32)],
            (place, early, swap_context(early), total),
        )
        gate_grad, reduce_grad = call(
            partial(late_out_kernel, scale=scale),
            "late_out",
            [(gate_weight.shape, F32), (reduce_weight.shape, F32)],
            (place, *late, total),
        )
    else:
        factor = tokens_all / total[error_at + 1, 0]
        mixed_full = lax.all_gather(mixed_own, "tensor", axis=1, tiled=True)
        output_grad = plain_grad(t_dot(gated, branch_back), factor, 1)
        expand_grad = plain_grad(t_dot(mixed_full, expand_low), factor, 0)
        gate_grad = plain_grad(t_dot(normed, gate_low), factor, 0)
        reduce_grad = plain_grad(t_dot(normed, reduce_low), factor, 0)

    counts = [v.shape[1] // channels for v in vectors]
    offsets = [REACH + sum(counts[:i]) for i in range(4)]
    whole = (damping.shape, F32)
    *mode_grads, timestep_grad, loss_value, gate_bias_grad, expand_bias_grad, output_bias_grad, reduce_bias_grad = call(
        partial(finish_kernel, starts=offsets, scale=scale + (float(width),)),
        "finish",
        [whole] * 4 + [((1, n), F32) for n in (channels, 1, units, units, width, channels)],
        (place, total, mode_mine, mode_other),
    )
    return (
        output,
        loss_value.reshape(()),
        inputs_grad,
        gain_grad[0],
        bias_grad[0],
        gate_grad,
        gate_bias_grad[0],
        reduce_grad,
        reduce_bias_grad[0],
        mode_grads[0],
        mode_grads[1],
        timestep_grad[0],
        mode_grads[2],
        mode_grads[3],
        expand_grad,
        expand_bias_grad[0],
        output_grad,
        output_bias_grad[0],
    )


def solution(mesh):
    tokens = P(("shard", "context"), None)
    ids = P("shard", "context")
    split = P("shard", "tensor")
    rows = P("tensor", None)
    units = P("tensor")
    return jax.shard_map(
        per_device,
        mesh=mesh,
        in_specs=(
            tokens, tokens, ids, ids, P(), P(), split, units, split, units,
            rows, rows, units, rows, rows, split, units, P("tensor", "shard"), P(),
        ),
        out_specs=(
            tokens, P(), tokens, P(), P(), split, units, split, units,
            rows, rows, units, rows, rows, split, units, P("tensor", "shard"), P(),
        ),
        check_vma=False,
    )
```
